32 devices in a mesh: dp: 4 (over y, x), expert: 8 (over z, core).
Axes of the slice: x: 2, y: 2, z: 4, core: 2. Of those that a mesh axis runs over, the one named last changes fastest.
Arguments:
- tokens: bfloat16 [384, 4096], P(('dp', 'expert')), may hold values from -6 to 6
- expert_ids: int32 [384, 8], P(('dp', 'expert')), may hold values from 0 to 15, all different within a row; in each aligned block of 12 rows (0 to 11, 12 to 23, ...) at most 12 rows name the same one
- gate_probs: float32 [384, 8], P(('dp', 'expert')), may hold values from 0.02 to 5
- in_weight: bfloat16 [16, 4096, 3072], P('expert', None, 'dp'), may hold values from -0.09375 to 0.09375
- out_weight: bfloat16 [16, 1536, 4096], P('expert', 'dp'), may hold values from -0.15625 to 0.15625
- swap_slot: int32 [8], replicated, may hold values from 0 to 1
Outputs:
- mixed_out: bfloat16 [384, 4096], P(('dp', 'expert'))
- owner_load: float32 [8], replicated
The draws below stay inside these ranges and needn't reach their ends.
Inputs may be any that keep to these rules, and one draw needn't show every extreme that they name: `expert_ids`: among the rows of one device no expert is named more than 12 times, and in every draw some device's rows name some expert exactly 12 times; a row names 8 different experts.
All inputs are finite; a program needn't handle non-finite values.
Results may differ from the reference program's by a relative error of at most 0.018.
Values may be sent and summed in bfloat16 or wider, within the bound.
No kernel may reach another device: no remote copies, remote signals or barrier semaphores. Data moves between devices by JAX's collectives and lax.ppermute only.
A program may use at most 128 MiB of HBM per device.

```python
import math
import jax
import jax.numpy as jnp
import numpy as np
from jax import lax

D = 4096
FF = 1536
TOP = 8
EXP_DEV = 2
TOK_DEV = 12
EXPERTS = 16
OWNERS = 8
CAP = 12
TOKENS = 384
N_DP = 4


def draw_gate_probs(key, part):
    key = jax.random.fold_in(key, 5)
    rows = jnp.arange(TOKENS, dtype=jnp.float32)[:, None] / TOKENS
    logs = jax.random.uniform(key, (TOKENS, TOP), jnp.float32, jnp.log(0.02), jnp.log(0.5))
    base = jnp.exp(logs)
    scale = 1.0 + 4.0 * rows
    return jnp.clip(base * scale, 0.02, 5.0).astype(jnp.float32)


def plant(entries, own_key, low, top_value):
    longest = entries.shape.index(max(entries.shape))
    spots = []
    for shift in (0, 1):
        where = [jax.random.randint(jax.random.fold_in(own_key, axis), (), 0, length) for axis, length in enumerate(entries.shape)]
        where[longest] = (where[longest] + shift) % entries.shape[longest]
        spots.append(tuple(where))
    return entries.at[spots[0]].set(low).at[spots[1]].set(top_value)


def block_scale(own_key, extent, pieces, smallest, high):
    gain, own = 1.0, jax.random.fold_in(own_key, 6)
    for axis_at, parts in pieces:
        draws = jnp.exp(jax.random.uniform(jax.random.fold_in(own, axis_at), (parts,), jnp.float32, smallest / len(pieces), high / len(pieces)))
        gain = gain * jnp.repeat(draws, extent[axis_at] // parts).reshape([-1 if axis == axis_at else 1 for axis in range(len(extent))])
    return gain


def shared_out(own_key, own, number, rows, amount, top, reach, slope):
    ranking = jax.random.permutation(own_key, amount)
    packed, common = shares(amount, rows * top, reach, slope, True), shares(amount, rows * top, reach, slope, False)
    places = jnp.arange(amount)

    def named(lengths, turn):
        used = int((lengths > 0).sum())
        fixed = max(1, used // 4)
        moved = fixed + (places - fixed + turn * (used - fixed)) % max(1, amount - fixed)
        return jnp.zeros((amount,), jnp.int32).at[ranking[jnp.where(places < fixed, places, moved)]].set(jnp.asarray(lengths, jnp.int32))

    lengths = jnp.where(number % 4 == 0, named(packed, number // 4), named(common, number - number // 4 - 1))
    mixed = jax.random.permutation(jax.random.fold_in(own, 3), amount)
    giver, sink = mixed[0:amount // 2 * 2:2], mixed[1:amount // 2 * 2:2]
    room = jnp.minimum(lengths[giver] - 1, reach - lengths[sink]) // 2
    room = jnp.where((giver == ranking[0]) | (sink == ranking[0]) | (lengths[sink] == 0), 0, jnp.maximum(room, 0))
    moved = jax.random.randint(jax.random.fold_in(own, 4), (amount // 2,), 0, 1 << 20) % (room + 1)
    lengths = lengths.at[giver].add(-moved).at[sink].add(moved)
    labels = jnp.searchsorted(jnp.cumsum(lengths), jnp.arange(rows * top), side="right").astype(jnp.int32)
    listing = labels.reshape(top, rows).T
    listing = listing[jax.random.permutation(jax.random.fold_in(own, 1), rows)]
    turn = jax.random.randint(jax.random.fold_in(own, 2), (rows, 1), 0, top)
    return jnp.take_along_axis(listing, (jnp.arange(top)[None, :] + turn) % top, axis=1)


def shares(number_of, total, bound, slope, full):
    portions = [(1 << 20) // math.isqrt(rank ** slope) + 1 for rank in range(1, number_of + 1)]
    largest = bound if full else min(bound, max(-(-total // number_of), total * portions[0] // sum(portions)))
    least = 1 if total - largest >= number_of - 1 else 0
    given, rest = [largest] + [least] * (number_of - 1), total - largest - least * (number_of - 1)
    while rest > 0:
        candidates = [i for i in range(1, number_of) if given[i] < largest] or [i for i in range(1, number_of) if given[i] < bound]
        whole, left = sum([portions[i] for i in candidates]), rest
        for i in candidates:
            more = min(bound - given[i], max(1, left * portions[i] // whole), rest)
            given[i] = given[i] + more
            rest = rest - more
    return np.array(given)


def gaussian(stream_key, shape, scale, reach, pieces=(), held_as=jnp.bfloat16):
    factor_of = block_scale(stream_key, shape, pieces, -0.22, 0.18) if pieces else 1.0
    result = jax.random.normal(stream_key, shape, jnp.float32) * scale * factor_of
    return jnp.minimum(jnp.maximum(result, -reach), reach).astype(held_as)


def setup_inputs(seed: int = 0) -> dict:
    key_of = jax.random.split(jax.random.key(seed), 7)
    tokens = gaussian(key_of[0], (TOKENS, D), 1.0, 6.0, ((0, 32),))
    expert_ids_keys = jax.random.split(jax.random.fold_in(key_of[1], 1), TOKENS // TOK_DEV)
    expert_ids_turns = jax.random.permutation(jax.random.fold_in(key_of[1], 3), TOKENS // TOK_DEV)
    expert_ids = jax.vmap(lambda own, number: shared_out(jax.random.fold_in(key_of[1], 2), own, number, TOK_DEV, EXPERTS, TOP, CAP, 2))(expert_ids_keys, expert_ids_turns).reshape((TOKENS, TOP))
    gate_probs = draw_gate_probs(jax.random.fold_in(key_of[6], 71), 0)
    in_weight = gaussian(key_of[3], (EXPERTS, D, 2 * FF), D ** -0.5, 0.09375, ((0, 8), (2, 4)))
    out_weight = gaussian(key_of[4], (EXPERTS, FF, D), FF ** -0.5, 0.15625, ((0, 8), (1, 4)))
    swap_slot = plant(jax.random.randint(key_of[5], (OWNERS,), 0, EXP_DEV), jax.random.fold_in(key_of[5], 1), 0, EXP_DEV - 1).astype(jnp.int32)
    return dict(tokens=tokens, expert_ids=expert_ids, gate_probs=gate_probs, in_weight=in_weight, out_weight=out_weight, swap_slot=swap_slot)


def reference(tokens, expert_ids, gate_probs, in_weight, out_weight, swap_slot):
    row_block = 64
    half_width = FF // N_DP
    flat_ids = expert_ids.reshape(-1).astype(jnp.int32)
    assignments = flat_ids.shape[0]
    experts_range = jnp.arange(EXPERTS, dtype=jnp.int32)
    matches = flat_ids[:, None] == experts_range[None, :]
    counts = jnp.sum(matches.astype(jnp.int32), 0).astype(jnp.int32)
    mass = jnp.sum(jnp.where(matches, gate_probs.reshape(-1)[:, None].astype(jnp.float32), jnp.float32(0.0)), 0)
    starts = (jnp.cumsum(counts) - counts).astype(jnp.int32)
    sort_order = jnp.argsort(flat_ids, stable=True).astype(jnp.int32)
    token_rows = jnp.concatenate([(sort_order // TOP).astype(jnp.int32), jnp.zeros((row_block,), jnp.int32)]).astype(jnp.int32)

    def per_expert(expert, sorted_out):
        down_rows = out_weight[expert].astype(jnp.float32).reshape(N_DP, half_width, D)
        up_cols = in_weight[expert]

        def one_block(index, current):
            begin = (starts[expert] + index * row_block).astype(jnp.int32)
            picked = lax.dynamic_slice_in_dim(token_rows, begin, row_block)
            inputs_block = jnp.take(tokens, picked, axis=0)
            both_halves = jnp.dot(inputs_block, up_cols, preferred_element_type=jnp.float32).reshape(row_block, N_DP, 2, half_width)
            hidden = (jax.nn.silu(both_halves[:, :, 0]) * both_halves[:, :, 1]).astype(jnp.bfloat16)
            hidden = lax.optimization_barrier(hidden)
            partials = jnp.einsum("rbf,bfd->rbd", hidden.astype(jnp.float32), down_rows).astype(jnp.bfloat16)
            partials = lax.optimization_barrier(partials)
            block_out = jnp.sum(partials.astype(jnp.float32), 1).astype(jnp.bfloat16)
            return lax.dynamic_update_slice_in_dim(current, block_out, begin, 0)

        block_count = ((counts[expert] + row_block - 1) // row_block).astype(jnp.int32)
        return lax.fori_loop(jnp.int32(0), block_count, one_block, sorted_out)

    sorted_out = lax.fori_loop(0, EXPERTS, per_expert, jnp.zeros((assignments + row_block, D), jnp.bfloat16))
    inverse = jnp.argsort(sort_order).astype(jnp.int32)
    expert_out = jnp.take(sorted_out, inverse, axis=0).reshape(TOKENS, TOP, D)
    mixed_out = jnp.sum(gate_probs[..., None] * expert_out.astype(jnp.float32), 1).astype(jnp.bfloat16)

    home = experts_range // EXP_DEV
    within = experts_range % EXP_DEV
    partner = (home + OWNERS // 2) % OWNERS
    moved = within == swap_slot[home]
    holder = jnp.where(moved, partner, home)
    holder_hot = (holder[:, None] == jnp.arange(OWNERS, dtype=jnp.int32)[None, :]).astype(jnp.float32)
    owner_load = jnp.dot(mass, holder_hot, precision=lax.Precision.HIGHEST) * (OWNERS / TOKENS)
    return mixed_out, owner_load
```

```python
import jax
import jax.numpy as jnp
from jax import lax
from jax.sharding import PartitionSpec as P


def lookup_small(values_table, index_array):
    columns = jnp.arange(values_table.shape[0], dtype=jnp.int32)
    return jnp.sum(jnp.where(index_array[..., None] == columns, values_table, 0), -1)


def planned_holder(expert_index, swap_slot, per_device, owners):
    home = expert_index // per_device
    within = expert_index % per_device
    partner = (home + owners // 2) % owners
    moved = within == lookup_small(swap_slot, home)
    return jnp.where(moved, partner, home)


def on_device(tokens, expert_ids, gate_probs, in_weight, out_weight, swap_slot):
    owners = lax.axis_size("expert")
    per_device = in_weight.shape[0]
    top_count = expert_ids.shape[1]
    experts_all = per_device * owners
    half_width = out_weight.shape[1]
    axes = ("dp", "expert")
    routing = lax.all_gather(
        jnp.concatenate([expert_ids.astype(jnp.float32), gate_probs], 1), axes, axis=0, tiled=True
    )
    all_tokens = lax.all_gather(tokens, axes, axis=0, tiled=True)
    all_ids = routing[:, :top_count].astype(jnp.int32)
    all_gates = routing[:, top_count:]
    all_experts = jnp.arange(experts_all, dtype=jnp.int32)
    dense_gates = jnp.sum(
        jnp.where(all_ids[..., None] == all_experts, all_gates[..., None], jnp.float32(0.0)), 1
    )
    totals = jnp.sum(dense_gates, 0)
    holder = planned_holder(all_experts, swap_slot, per_device, owners)
    owner_load = jnp.sum(
        jnp.where(
            holder == jnp.arange(owners, dtype=jnp.int32)[:, None], totals[None, :], jnp.float32(0.0)
        ),
        1,
    ) * (owners / all_ids.shape[0])
    own = lax.axis_index("expert") * per_device + jnp.arange(per_device, dtype=jnp.int32)
    own_gates = jnp.sum(
        jnp.where(all_ids[..., None] == own, all_gates[..., None], jnp.float32(0.0)), 1
    )
    both = jnp.einsum("td,sdf->tsf", all_tokens, in_weight, preferred_element_type=jnp.float32)
    hidden = jax.nn.silu(both[..., :half_width]) * both[..., half_width:]
    hidden = (hidden * own_gates[..., None]).astype(jnp.bfloat16)
    partial = jnp.einsum("tsf,sfd->td", hidden, out_weight, preferred_element_type=jnp.float32)
    partial = partial.astype(jnp.bfloat16).reshape(-1, *tokens.shape)
    mixed_out = lax.psum_scatter(partial, axes, scatter_dimension=0, tiled=False)
    return (mixed_out, owner_load)


def solution(mesh):
    return jax.shard_map(
        on_device,
        mesh=mesh,
        in_specs=(
            P(("dp", "expert"), None),
            P(("dp", "expert"), None),
            P(("dp", "expert"), None),
            P("expert", None, "dp"),
            P("expert", "dp", None),
            P(),
        ),
        out_specs=(P(("dp", "expert"), None), P()),
        check_vma=False,
    )
```

```python
import jax
import jax.numpy as jnp
from jax import lax
from jax.sharding import Mesh, PartitionSpec as P

LANES = 128


def lookup_small(values_table, index_array):
    columns = jnp.arange(values_table.shape[0], dtype=jnp.int32)
    return jnp.sum(jnp.where(index_array[..., None] == columns, values_table, 0), -1)


def planned_holder(expert_index, swap_slot, per_device, owners):
    home = expert_index // per_device
    within = expert_index % per_device
    partner = (home + owners // 2) % owners
    moved = within == lookup_small(swap_slot, home)
    return jnp.where(moved, partner, home)


def swap(value, axis, distance):
    size = lax.axis_size(axis)
    return lax.ppermute(value, axis, [(i, i ^ distance) for i in range(size)])


def split_gates(gates):
    high = lax.reduce_precision(gates, 8, 7)
    middle = lax.reduce_precision(gates - high, 8, 7)
    return [part.astype(jnp.bfloat16) for part in (high, middle, gates - high - middle)]


def gathered(value, axis):
    pieces = [value] + [swap(value, axis, k) for k in range(1, lax.axis_size(axis))]
    return jnp.concatenate(pieces, 0)


def scattered(value, axis):
    size = lax.axis_size(axis)
    blocks = value.reshape(size, -1, value.shape[1])
    total = blocks[0].astype(jnp.float32)
    for k in range(1, size):
        total = total + swap(blocks[k], axis, k).astype(jnp.float32)
    return total.astype(jnp.bfloat16)


def in_order(blocks):
    for dim, axis in enumerate(("dp", "chip")):
        size = lax.axis_size(axis)
        here = jnp.arange(size, dtype=jnp.int32)
        match = (here[:, None] ^ here[None, :]) == lax.axis_index(axis)
        moved = jnp.moveaxis(blocks, dim, 0)
        picked = jnp.sum(jnp.where(match[..., None, None], moved[None], jnp.float32(0.0)), 1)
        blocks = jnp.moveaxis(picked, 0, dim)
    return blocks


def on_device(tokens, expert_ids, gate_probs, in_weight, out_weight, swap_slot):
    groups, chips = lax.axis_size("dp"), lax.axis_size("chip")
    owners = 2 * chips
    per_device = in_weight.shape[0]
    rows, width = tokens.shape
    part = width // 2
    top_count = expert_ids.shape[1]
    experts_all = per_device * owners
    half_width = out_weight.shape[1]
    core = lax.axis_index("core")
    first = core == 0

    routing = jnp.concatenate([expert_ids.astype(jnp.bfloat16), *split_gates(gate_probs)], 1)
    routing = jnp.pad(routing, ((0, 0), (0, LANES - routing.shape[1])))
    left, right = tokens[:, :part], tokens[:, part:]
    keep = jnp.concatenate([jnp.where(first, left, right), routing], 1)
    give = jnp.concatenate([jnp.where(first, right, left), routing], 1)
    taken = swap(give, "core", 1)
    both_cores = jnp.concatenate(
        [jnp.where(first, keep, taken), jnp.where(first, taken, keep)], 0
    )
    mine = gathered(gathered(both_cores, "chip"), "dp")
    own_half = mine[:, :part]
    other_half = swap(own_half, "core", 1)
    all_tokens = jnp.concatenate(
        [jnp.where(first, own_half, other_half), jnp.where(first, other_half, own_half)], 1
    )

    meta = mine[:, part:].astype(jnp.float32)
    all_ids = meta[:, :top_count].astype(jnp.int32)
    all_gates = (
        meta[:, top_count : 2 * top_count]
        + meta[:, 2 * top_count : 3 * top_count]
        + meta[:, 3 * top_count : 4 * top_count]
    )
    all_experts = jnp.arange(experts_all, dtype=jnp.int32)
    dense_gates = jnp.sum(
        jnp.where(all_ids[..., None] == all_experts, all_gates[..., None], jnp.float32(0.0)), 1
    )
    chip_totals = jnp.sum(dense_gates.reshape(groups, chips, 2 * rows, experts_all), 2)
    totals = jnp.sum(in_order(chip_totals), (0, 1))
    holder = planned_holder(all_experts, swap_slot, per_device, owners)
    owner_load = jnp.sum(
        jnp.where(
            holder == jnp.arange(owners, dtype=jnp.int32)[:, None], totals[None, :], jnp.float32(0.0)
        ),
        1,
    ) * (owners / all_ids.shape[0])

    home = lax.axis_index("chip") * 2 + core
    own = home * per_device + jnp.arange(per_device, dtype=jnp.int32)
    own_gates = jnp.sum(
        jnp.where(all_ids[..., None] == own, all_gates[..., None], jnp.float32(0.0)), 1
    )
    both = jnp.einsum("td,sdf->tsf", all_tokens, in_weight, preferred_element_type=jnp.float32)
    hidden = jax.nn.silu(both[..., :half_width]) * both[..., half_width:]
    hidden = (hidden * own_gates[..., None]).astype(jnp.bfloat16)
    partial = jnp.einsum(
        "tsf,sfd->td", hidden, out_weight, preferred_element_type=jnp.float32
    ).astype(jnp.bfloat16)

    left, right = partial[:, :part], partial[:, part:]
    arrived = swap(jnp.where(first, right, left), "core", 1)
    own_half = jnp.where(first, left, right).astype(jnp.float32) + arrived.astype(jnp.float32)
    summed = scattered(scattered(own_half.astype(jnp.bfloat16), "dp"), "chip")
    upper, lower = summed[:rows], summed[rows:]
    arrived = swap(jnp.where(first, lower, upper), "core", 1)
    kept = jnp.where(first, upper, lower)
    mixed_out = jnp.concatenate(
        [jnp.where(first, kept, arrived), jnp.where(first, arrived, kept)], 1
    )
    return (mixed_out, owner_load)


def solution(mesh):
    groups, owners = mesh.devices.shape
    fine = Mesh(mesh.devices.reshape(groups, owners // 2, 2), ("dp", "chip", "core"))
    rows = P(("dp", "chip", "core"), None)
    return jax.shard_map(
        on_device,
        mesh=fine,
        in_specs=(
            rows,
            rows,
            rows,
            P(("chip", "core"), None, "dp"),
            P(("chip", "core"), "dp", None),
            P(),
        ),
        out_specs=(rows, P()),
        check_vma=False,
    )
```

```python
import jax
import jax.numpy as jnp
from jax import lax
from jax.experimental.layout import Layout, with_layout_constraint
from jax.sharding import Mesh, PartitionSpec as P

LANES = 128


def lookup_small(values_table, index_array):
    columns = jnp.arange(values_table.shape[0], dtype=jnp.int32)
    return jnp.sum(jnp.where(index_array[..., None] == columns, values_table, 0), -1)


def planned_holder(expert_index, swap_slot, per_device, owners):
    home = expert_index // per_device
    within = expert_index % per_device
    partner = (home + owners // 2) % owners
    moved = within == lookup_small(swap_slot, home)
    return jnp.where(moved, partner, home)


def row_major(value):
    return with_layout_constraint(value, Layout(major_to_minor=tuple(range(value.ndim))))


def swap(value, axis, distance):
    size = lax.axis_size(axis)
    pairs = [(i, i ^ distance) for i in range(size)]
    return row_major(lax.ppermute(row_major(value), axis, pairs))


def split_gates(gates):
    high = lax.reduce_precision(gates, 8, 7)
    middle = lax.reduce_precision(gates - high, 8, 7)
    return [part.astype(jnp.bfloat16) for part in (high, middle, gates - high - middle)]


def spread(block):
    size = lax.axis_size("dp")
    if size != 4:
        return [block] + [swap(block, "dp", k) for k in range(1, size)]
    cut = block.shape[1] // (2 * LANES) * LANES
    near = [swap(block, "dp", 1), swap(block, "dp", 2)]
    far = [swap(near[0][:, :cut], "dp", 2), swap(near[1][:, cut:], "dp", 1)]
    return [block, *near, jnp.concatenate(far, 1)]


def wide(value):
    return value.astype(jnp.float32)


def collected(blocks):
    size = lax.axis_size("dp")
    if size != 4:
        total = wide(blocks[0])
        for k in range(1, size):
            total = total + wide(swap(blocks[k], "dp", k))
        return total.astype(jnp.bfloat16)
    own, one, two, both = blocks
    cut = own.shape[1] // (2 * LANES) * LANES
    upper = swap(both[:, :cut], "dp", 2)
    lower = swap(both[:, cut:], "dp", 1)
    one = jnp.concatenate(
        [(wide(one[:, :cut]) + wide(upper)).astype(jnp.bfloat16), one[:, cut:]], 1
    )
    two = jnp.concatenate(
        [two[:, :cut], (wide(two[:, cut:]) + wide(lower)).astype(jnp.bfloat16)], 1
    )
    total = wide(own) + wide(swap(one, "dp", 1)) + wide(swap(two, "dp", 2))
    return total.astype(jnp.bfloat16)


def in_order(blocks):
    for dim, axis in enumerate(("dp", "chip")):
        size = lax.axis_size(axis)
        here = jnp.arange(size, dtype=jnp.int32)
        match = (here[:, None] ^ here[None, :]) == lax.axis_index(axis)
        moved = jnp.moveaxis(blocks, dim, 0)
        picked = jnp.sum(jnp.where(match[..., None, None], moved[None], jnp.float32(0.0)), 1)
        blocks = jnp.moveaxis(picked, 0, dim)
    return blocks


def on_device(tokens, expert_ids, gate_probs, in_weight, out_weight, swap_slot):
    groups, chips = lax.axis_size("dp"), lax.axis_size("chip")
    owners = 2 * chips
    per_device = in_weight.shape[0]
    rows, width = tokens.shape
    part = width // 2
    top_count = expert_ids.shape[1]
    experts_all = per_device * owners
    half_width = out_weight.shape[1]
    core = lax.axis_index("core")
    first = core == 0
    all_experts = jnp.arange(experts_all, dtype=jnp.int32)
    home = lax.axis_index("chip") * 2 + core

    routing = jnp.concatenate(
        [row_major(expert_ids).astype(jnp.bfloat16), *split_gates(row_major(gate_probs))], 1
    )
    routing = row_major(jnp.pad(routing, ((0, 0), (0, LANES - routing.shape[1]))))
    left, right = tokens[:, :part], tokens[:, part:]
    keep = jnp.concatenate([jnp.where(first, left, right), routing], 1)
    give = jnp.concatenate([jnp.where(first, right, left), routing], 1)
    taken = swap(give, "core", 1)
    chip_rows = row_major(
        jnp.concatenate([jnp.where(first, keep, taken), jnp.where(first, taken, keep)], 0)
    )

    def routes(meta):
        ids = meta[:, :top_count].astype(jnp.int32)
        gates = sum(
            wide(meta[:, (i + 1) * top_count : (i + 2) * top_count]) for i in range(3)
        )
        return jnp.sum(
            jnp.where(ids[..., None] == all_experts, gates[..., None], jnp.float32(0.0)), 1
        )

    def expert_sum(held, own_gates):
        hidden = []
        for s in range(per_device):
            both = jnp.dot(held, in_weight[s], preferred_element_type=jnp.float32)
            unit = jax.nn.silu(both[:, :half_width]) * both[:, half_width:]
            hidden.append((unit * own_gates[:, s : s + 1]).astype(jnp.bfloat16))
        return jnp.dot(
            jnp.concatenate(hidden, 1),
            out_weight.reshape(per_device * half_width, width),
            preferred_element_type=jnp.float32,
        ).astype(jnp.bfloat16)

    chip_totals, returned = [], []
    for j in range(chips):
        block = chip_rows if j == 0 else swap(chip_rows, "chip", j)
        held = row_major(jnp.concatenate(spread(block), 0))
        own_half = held[:, :part]
        other_half = swap(own_half, "core", 1)
        held_tokens = row_major(
            jnp.concatenate(
                [
                    jnp.where(first, own_half, other_half),
                    jnp.where(first, other_half, own_half),
                ],
                1,
            )
        )
        dense_gates = routes(held[:, part:])
        chip_totals.append(jnp.sum(dense_gates.reshape(groups, 2 * rows, experts_all), 1))
        own = home * per_device + jnp.arange(per_device, dtype=jnp.int32)
        own_gates = jnp.sum(
            jnp.where(all_experts[:, None] == own, dense_gates[..., None], jnp.float32(0.0)), 1
        )
        summed = row_major(expert_sum(held_tokens, own_gates))
        left, right = summed[:, :part], summed[:, part:]
        arrived = swap(jnp.where(first, right, left), "core", 1)
        chip_sum = (wide(jnp.where(first, left, right)) + wide(arrived)).astype(jnp.bfloat16)
        chip_sum = row_major(chip_sum).reshape(groups, 2 * rows, part)
        block = collected([chip_sum[k] for k in range(groups)])
        returned.append(block if j == 0 else swap(block, "chip", j))

    total = sum(wide(block) for block in returned).astype(jnp.bfloat16)
    upper, lower = total[:rows], total[rows:]
    arrived = swap(jnp.where(first, lower, upper), "core", 1)
    kept = jnp.where(first, upper, lower)
    mixed_out = row_major(
        jnp.concatenate([jnp.where(first, kept, arrived), jnp.where(first, arrived, kept)], 1)
    )

    totals = jnp.sum(in_order(jnp.stack(chip_totals, 1)), (0, 1))
    holder = planned_holder(all_experts, swap_slot, per_device, owners)
    owner_load = jnp.sum(
        jnp.where(
            holder == jnp.arange(owners, dtype=jnp.int32)[:, None], totals[None, :], jnp.float32(0.0)
        ),
        1,
    ) * (owners / (groups * owners * rows))
    return (mixed_out, owner_load)


def solution(mesh):
    groups, owners = mesh.devices.shape
    fine = Mesh(mesh.devices.reshape(groups, owners // 2, 2), ("dp", "chip", "core"))
    rows = P(("dp", "chip", "core"), None)
    return jax.shard_map(
        on_device,
        mesh=fine,
        in_specs=(
            rows,
            rows,
            rows,
            P(("chip", "core"), None, "dp"),
            P(("chip", "core"), "dp", None),
            P(),
        ),
        out_specs=(rows, P()),
        check_vma=False,
    )
```

```python
import jax
import jax.numpy as jnp
from jax import lax
from jax.experimental.layout import Layout, with_layout_constraint
from jax.sharding import Mesh, PartitionSpec as P

LANES = 128
GATE_MOST = 5


def lookup_small(values_table, index_array):
    columns = jnp.arange(values_table.shape[0], dtype=jnp.int32)
    return jnp.sum(jnp.where(index_array[..., None] == columns, values_table, 0), -1)


def planned_holder(expert_index, swap_slot, per_device, owners):
    home = expert_index // per_device
    within = expert_index % per_device
    partner = (home + owners // 2) % owners
    moved = within == lookup_small(swap_slot, home)
    return jnp.where(moved, partner, home)


def row_major(value):
    return with_layout_constraint(value, Layout(major_to_minor=tuple(range(value.ndim))))


def swap(value, axis, distance):
    size = lax.axis_size(axis)
    pairs = [(i, i ^ distance) for i in range(size)]
    return row_major(lax.ppermute(row_major(value), axis, pairs))


def split_gates(gates):
    high = lax.reduce_precision(gates, 8, 7)
    middle = lax.reduce_precision(gates - high, 8, 7)
    return [part.astype(jnp.bfloat16) for part in (high, middle, gates - high - middle)]


def cut_of(block):
    return block.shape[1] // (2 * LANES) * LANES


def spread_near(block):
    size = lax.axis_size("dp")
    return [swap(block, "dp", k) for k in range(1, 3 if size == 4 else size)]


def spread_rest(near):
    if lax.axis_size("dp") != 4:
        return []
    cut = cut_of(near[0])
    return [swap(near[0][:, :cut], "dp", 2), swap(near[1][:, cut:], "dp", 1)]


def joined(halves):
    return [jnp.concatenate(halves, 1)] if halves else []


def behind(values, others):
    return lax.optimization_barrier((values, others))[0]


def wide(value):
    return value.astype(jnp.float32)


def with_fourth(blocks):
    if len(blocks) != 4:
        return blocks
    own, one, two, both = blocks
    cut = cut_of(own)
    upper = swap(both[:, :cut], "dp", 2)
    lower = swap(both[:, cut:], "dp", 1)
    one = jnp.concatenate(
        [(wide(one[:, :cut]) + wide(upper)).astype(jnp.bfloat16), one[:, cut:]], 1
    )
    two = jnp.concatenate(
        [two[:, :cut], (wide(two[:, cut:]) + wide(lower)).astype(jnp.bfloat16)], 1
    )
    return [own, one, two]


def collected(blocks):
    total = wide(blocks[0])
    for k, block in enumerate(blocks[1:], 1):
        total = total + wide(swap(block, "dp", k))
    return total.astype(jnp.bfloat16)


def on_device(tokens, expert_ids, gate_probs, in_weight, out_weight, swap_slot):
    groups, chips = lax.axis_size("dp"), lax.axis_size("chip")
    owners = 2 * chips
    per_device = in_weight.shape[0]
    rows, width = tokens.shape
    part = width // 2
    top_count = expert_ids.shape[1]
    experts_all = per_device * owners
    half_width = out_weight.shape[1]
    core = lax.axis_index("core")
    first = core == 0
    all_experts = jnp.arange(experts_all, dtype=jnp.int32)
    home = lax.axis_index("chip") * 2 + core

    routing = jnp.concatenate(
        [row_major(expert_ids).astype(jnp.bfloat16), *split_gates(row_major(gate_probs))], 1
    )
    routing = row_major(jnp.pad(routing, ((0, 0), (0, LANES - routing.shape[1]))))
    left, right = tokens[:, :part], tokens[:, part:]
    keep = jnp.concatenate([jnp.where(first, left, right), routing], 1)
    give = jnp.concatenate([jnp.where(first, right, left), routing], 1)
    taken = swap(give, "core", 1)
    chip_rows = row_major(
        jnp.concatenate([jnp.where(first, keep, taken), jnp.where(first, taken, keep)], 0)
    )

    def routes(meta):
        ids = meta[:, :top_count].astype(jnp.int32)
        gates = sum(
            wide(meta[:, (i + 1) * top_count : (i + 2) * top_count]) for i in range(3)
        )
        return ids, gates

    def own_sums(blocks):
        held = row_major(jnp.concatenate(blocks, 0))
        own_half = held[:, :part]
        other_half = swap(own_half, "core", 1)
        held_tokens = row_major(
            jnp.concatenate(
                [
                    jnp.where(first, own_half, other_half),
                    jnp.where(first, other_half, own_half),
                ],
                1,
            )
        )
        ids, gates = routes(held[:, part:])
        hidden = []
        for s in range(per_device):
            own_gate = jnp.sum(
                jnp.where(ids == home * per_device + s, gates, jnp.float32(0.0)), 1, keepdims=True
            )
            both = jnp.dot(held_tokens, in_weight[s], preferred_element_type=jnp.float32)
            unit = jax.nn.silu(both[:, :half_width]) * both[:, half_width:]
            hidden.append((unit * own_gate).astype(jnp.bfloat16))
        summed = jnp.dot(
            jnp.concatenate(hidden, 1),
            out_weight.reshape(per_device * half_width, width),
            preferred_element_type=jnp.float32,
        )
        return row_major(summed.astype(jnp.bfloat16))

    def chip_sums(summed, blocks):
        left, right = summed[:, :part], summed[:, part:]
        arrived = swap(jnp.where(first, right, left), "core", 1)
        chip_sum = (wide(jnp.where(first, left, right)) + wide(arrived)).astype(jnp.bfloat16)
        chip_sum = row_major(chip_sum)
        edges = [0]
        for block in blocks:
            edges.append(edges[-1] + block.shape[0])
        return [chip_sum[low:high] for low, high in zip(edges, edges[1:])]

    others = [swap(chip_rows, "chip", j) for j in range(1, chips)]
    near = [chip_rows, *spread_near(chip_rows)]
    near += joined(spread_rest(near[1:]))
    far = [row_major(jnp.concatenate(others, 0))]
    far += spread_near(far[0])
    first_blocks = [*near, far[0]]
    first_part = own_sums(first_blocks)
    far[1:] = behind(far[1:], first_part)
    rest = spread_rest(far[1:])
    first_sums = chip_sums(first_part, first_blocks)
    near_sums, far_sums = first_sums[:groups], first_sums[groups:]
    near_sums = with_fourth(near_sums)
    part_two = own_sums(far[1:])
    if rest:
        rest = joined(behind(rest, (part_two, near_sums)))
        part_three = own_sums(rest)
        far_sums += chip_sums(part_two, far[1:]) + chip_sums(part_three, rest)
    else:
        far_sums += chip_sums(part_two, far[1:])
    far += rest
    near_total = collected(near_sums)
    far_sums = with_fourth(far_sums)
    far_total = collected(far_sums)

    total = wide(near_total)
    for j in range(1, chips):
        block = far_total[(j - 1) * 2 * rows : j * 2 * rows]
        total = total + wide(swap(block, "chip", j))
    total = total.astype(jnp.bfloat16)
    upper, lower = total[:rows], total[rows:]
    arrived = swap(jnp.where(first, lower, upper), "core", 1)
    kept = jnp.where(first, upper, lower)
    mixed_out = row_major(
        jnp.concatenate([jnp.where(first, kept, arrived), jnp.where(first, arrived, kept)], 1)
    )

    ids, gates = routes(jnp.concatenate([block[:, part:] for block in near + far], 0))
    step = 2.0 ** (31 - (ids.shape[0] * GATE_MOST).bit_length())
    amounts = jnp.round(gates * step).astype(jnp.int32)
    totals = jnp.sum(jnp.where(ids[..., None] == all_experts, amounts[..., None], 0), (0, 1))
    totals = totals.astype(jnp.float32) * (1.0 / step)
    holder = planned_holder(all_experts, swap_slot, per_device, owners)
    owner_load = jnp.sum(
        jnp.where(
            holder == jnp.arange(owners, dtype=jnp.int32)[:, None], totals[None, :], jnp.float32(0.0)
        ),
        1,
    ) * (owners / ids.shape[0])
    return (mixed_out, owner_load)


def solution(mesh):
    groups, owners = mesh.devices.shape
    fine = Mesh(mesh.devices.reshape(groups, owners // 2, 2), ("dp", "chip", "core"))
    rows = P(("dp", "chip", "core"), None)
    return jax.shard_map(
        on_device,
        mesh=fine,
        in_specs=(
            rows,
            rows,
            rows,
            P(("chip", "core"), None, "dp"),
            P(("chip", "core"), "dp", None),
            P(),
        ),
        out_specs=(rows, P()),
        check_vma=False,
    )
```

```python
import jax
import jax.numpy as jnp
from jax import lax
from jax.experimental import pallas as pl
from jax.experimental.pallas import tpu as pltpu
from jax.experimental.layout import Layout, with_layout_constraint
from jax.sharding import Mesh, PartitionSpec as P

LANES = 128
GATE_MOST = 5


def lookup_small(values_table, index_array):
    columns = jnp.arange(values_table.shape[0], dtype=jnp.int32)
    return jnp.sum(jnp.where(index_array[..., None] == columns, values_table, 0), -1)


def planned_holder(expert_index, swap_slot, per_device, owners):
    home = expert_index // per_device
    within = expert_index % per_device
    partner = (home + owners // 2) % owners
    moved = within == lookup_small(swap_slot, home)
    return jnp.where(moved, partner, home)


def row_major(value):
    return with_layout_constraint(value, Layout(major_to_minor=tuple(range(value.ndim))))


def swap(value, axis, distance):
    size = lax.axis_size(axis)
    pairs = [(i, i ^ distance) for i in range(size)]
    return row_major(lax.ppermute(row_major(value), axis, pairs))


def split_gates(gates):
    high = lax.reduce_precision(gates, 8, 7)
    middle = lax.reduce_precision(gates - high, 8, 7)
    return [part.astype(jnp.bfloat16) for part in (high, middle, gates - high - middle)]


def cut_of(block):
    return block.shape[1] // (2 * LANES) * LANES


def spread_near(block):
    size = lax.axis_size("dp")
    return [swap(block, "dp", k) for k in range(1, 3 if size == 4 else size)]


def spread_rest(near):
    if lax.axis_size("dp") != 4:
        return []
    cut = cut_of(near[0])
    return [swap(near[0][:, :cut], "dp", 2), swap(near[1][:, cut:], "dp", 1)]


def joined(halves):
    return [jnp.concatenate(halves, 1)] if halves else []


def behind(values, others):
    return lax.optimization_barrier((values, others))[0]


def wide(value):
    return value.astype(jnp.float32)


def with_fourth(blocks):
    if len(blocks) != 4:
        return blocks
    own, one, two, both = blocks
    cut = cut_of(own)
    upper = swap(both[:, :cut], "dp", 2)
    lower = swap(both[:, cut:], "dp", 1)
    one = jnp.concatenate(
        [(wide(one[:, :cut]) + wide(upper)).astype(jnp.bfloat16), one[:, cut:]], 1
    )
    two = jnp.concatenate(
        [two[:, :cut], (wide(two[:, cut:]) + wide(lower)).astype(jnp.bfloat16)], 1
    )
    return [own, one, two]


def collected(blocks):
    total = wide(blocks[0])
    for k, block in enumerate(blocks[1:], 1):
        total = total + wide(swap(block, "dp", k))
    return total.astype(jnp.bfloat16)


def load_kernel(up_ref, down_ref, up_out, down_out, sems):
    copies = [
        pltpu.make_async_copy(up_ref, up_out, sems.at[0]),
        pltpu.make_async_copy(down_ref, down_out, sems.at[1]),
    ]
    for copy in copies:
        copy.start()
    for copy in copies:
        copy.wait()


def loaded(up, down):
    nbytes = up.nbytes + down.nbytes
    return pl.pallas_call(
        load_kernel,
        in_specs=[pl.BlockSpec(memory_space=pl.ANY)] * 2,
        out_specs=[pl.BlockSpec(memory_space=pltpu.VMEM)] * 2,
        out_shape=[pltpu.VMEM(up.shape, up.dtype), pltpu.VMEM(down.shape, down.dtype)],
        scratch_shapes=[pltpu.SemaphoreType.DMA((2,))],
        compiler_params=pltpu.CompilerParams(vmem_limit_bytes=32 * 2**20),
        cost_estimate=pl.CostEstimate(flops=0, bytes_accessed=nbytes, transcendentals=0),
    )(up, down)


def on_device(tokens, expert_ids, gate_probs, in_weight, out_weight, swap_slot):
    groups, chips = lax.axis_size("dp"), lax.axis_size("chip")
    owners = 2 * chips
    per_device = in_weight.shape[0]
    rows, width = tokens.shape
    part = width // 2
    top_count = expert_ids.shape[1]
    experts_all = per_device * owners
    half_width = out_weight.shape[1]
    core = lax.axis_index("core")
    first = core == 0
    all_experts = jnp.arange(experts_all, dtype=jnp.int32)
    home = lax.axis_index("chip") * 2 + core

    routing = jnp.concatenate(
        [row_major(expert_ids).astype(jnp.bfloat16), *split_gates(row_major(gate_probs))], 1
    )
    routing = row_major(jnp.pad(routing, ((0, 0), (0, LANES - routing.shape[1]))))
    left, right = tokens[:, :part], tokens[:, part:]
    keep = jnp.concatenate([jnp.where(first, left, right), routing], 1)
    give = jnp.concatenate([jnp.where(first, right, left), routing], 1)
    taken = swap(give, "core", 1)
    chip_rows = row_major(
        jnp.concatenate([jnp.where(first, keep, taken), jnp.where(first, taken, keep)], 0)
    )

    def routes(meta):
        ids = meta[:, :top_count].astype(jnp.int32)
        gates = sum(
            wide(meta[:, (i + 1) * top_count : (i + 2) * top_count]) for i in range(3)
        )
        return ids, gates

    def own_sums(blocks):
        held = row_major(jnp.concatenate(blocks, 0))
        own_half = held[:, :part]
        other_half = swap(own_half, "core", 1)
        held_tokens = row_major(
            jnp.concatenate(
                [
                    jnp.where(first, own_half, other_half),
                    jnp.where(first, other_half, own_half),
                ],
                1,
            )
        )
        ids, gates = routes(held[:, part:])
        hidden = []
        for s in range(per_device):
            own_gate = jnp.sum(
                jnp.where(ids == home * per_device + s, gates, jnp.float32(0.0)), 1, keepdims=True
            )
            both = jnp.dot(held_tokens, in_weight[s], preferred_element_type=jnp.float32)
            unit = jax.nn.silu(both[:, :half_width]) * both[:, half_width:]
            hidden.append((unit * own_gate).astype(jnp.bfloat16))
        summed = jnp.dot(
            jnp.concatenate(hidden, 1),
            out_weight.reshape(per_device * half_width, width),
            preferred_element_type=jnp.float32,
        )
        return row_major(summed.astype(jnp.bfloat16))

    def chip_sums(summed, blocks):
        left, right = summed[:, :part], summed[:, part:]
        arrived = swap(jnp.where(first, right, left), "core", 1)
        chip_sum = (wide(jnp.where(first, left, right)) + wide(arrived)).astype(jnp.bfloat16)
        chip_sum = row_major(chip_sum)
        edges = [0]
        for block in blocks:
            edges.append(edges[-1] + block.shape[0])
        return [chip_sum[low:high] for low, high in zip(edges, edges[1:])]

    others = [swap(chip_rows, "chip", j) for j in range(1, chips)]
    near = [chip_rows, *spread_near(behind(chip_rows, others[0]))]
    near += joined(spread_rest(near[1:]))
    in_weight, out_weight = loaded(*behind((in_weight, out_weight), near[1:3]))
    far = [row_major(jnp.concatenate(others, 0))]
    far += spread_near(far[0])
    first_blocks = [*near, far[0]]
    first_part = own_sums(first_blocks)
    far[1:] = behind(far[1:], first_part)
    rest = spread_rest(far[1:])
    sums = chip_sums(first_part, first_blocks)
    part_two = own_sums(far[1:])
    if rest:
        rest = joined(behind(rest, part_two))
        part_three = own_sums(rest)
        sums += chip_sums(part_two, far[1:]) + chip_sums(part_three, rest)
    else:
        sums += chip_sums(part_two, far[1:])
    far += rest
    sums = [jnp.concatenate([sums[k], sums[groups + k]], 0) for k in range(groups)]
    total = collected(with_fourth(sums))
    blocks = [total[j * 2 * rows : (j + 1) * 2 * rows] for j in range(chips)]
    total = wide(blocks[0])
    for j in range(1, chips):
        total = total + wide(swap(blocks[j], "chip", j))
    total = total.astype(jnp.bfloat16)
    upper, lower = total[:rows], total[rows:]
    arrived = swap(jnp.where(first, lower, upper), "core", 1)
    kept = jnp.where(first, upper, lower)
    mixed_out = row_major(
        jnp.concatenate([jnp.where(first, kept, arrived), jnp.where(first, arrived, kept)], 1)
    )

    ids, gates = routes(jnp.concatenate([block[:, part:] for block in near + far], 0))
    step = 2.0 ** (31 - (ids.shape[0] * GATE_MOST).bit_length())
    amounts = jnp.round(gates * step).astype(jnp.int32)
    totals = jnp.sum(jnp.where(ids[..., None] == all_experts, amounts[..., None], 0), (0, 1))
    totals = totals.astype(jnp.float32) * (1.0 / step)
    holder = planned_holder(all_experts, swap_slot, per_device, owners)
    owner_load = jnp.sum(
        jnp.where(
            holder == jnp.arange(owners, dtype=jnp.int32)[:, None], totals[None, :], jnp.float32(0.0)
        ),
        1,
    ) * (owners / ids.shape[0])
    return (mixed_out, owner_load)


def solution(mesh):
    groups, owners = mesh.devices.shape
    fine = Mesh(mesh.devices.reshape(groups, owners // 2, 2), ("dp", "chip", "core"))
    rows = P(("dp", "chip", "core"), None)
    return jax.shard_map(
        on_device,
        mesh=fine,
        in_specs=(
            rows,
            rows,
            rows,
            P(("chip", "core"), None, "dp"),
            P(("chip", "core"), "dp", None),
            P(),
        ),
        out_specs=(rows, P()),
        check_vma=False,
    )
```

```python
import jax
import jax.numpy as jnp
from jax import lax
from jax.experimental import pallas as pl
from jax.experimental.pallas import tpu as pltpu
from jax.experimental.layout import Layout, with_layout_constraint
from jax.sharding import Mesh, PartitionSpec as P

LANES = 128
GATE_MOST = 5


def lookup_small(values_table, index_array):
    columns = jnp.arange(values_table.shape[0], dtype=jnp.int32)
    return jnp.sum(jnp.where(index_array[..., None] == columns, values_table, 0), -1)


def planned_holder(expert_index, swap_slot, per_device, owners):
    home = expert_index // per_device
    within = expert_index % per_device
    partner = (home + owners // 2) % owners
    moved = within == lookup_small(swap_slot, home)
    return jnp.where(moved, partner, home)


def row_major(value):
    return with_layout_constraint(value, Layout(major_to_minor=tuple(range(value.ndim))))


def swap(value, axis, distance):
    size = lax.axis_size(axis)
    pairs = [(i, i ^ distance) for i in range(size)]
    return row_major(lax.ppermute(row_major(value), axis, pairs))


def split_gates(gates):
    high = lax.reduce_precision(gates, 8, 7)
    middle = lax.reduce_precision(gates - high, 8, 7)
    return [part.astype(jnp.bfloat16) for part in (high, middle, gates - high - middle)]


def cut_of(block):
    return block.shape[1] // (2 * LANES) * LANES


def spread_near(block):
    size = lax.axis_size("dp")
    return [swap(block, "dp", k) for k in range(1, 3 if size == 4 else size)]


def spread_rest(near):
    if lax.axis_size("dp") != 4:
        return []
    cut = cut_of(near[0])
    return [swap(near[0][:, :cut], "dp", 2), swap(near[1][:, cut:], "dp", 1)]


def joined(halves):
    return [jnp.concatenate(halves, 1)] if halves else []


def behind(values, others):
    return lax.optimization_barrier((values, others))[0]


def wide(value):
    return value.astype(jnp.float32)


def with_fourth(blocks):
    if len(blocks) != 4:
        return blocks
    own, one, two, both = blocks
    cut = cut_of(own)
    upper = swap(both[:, :cut], "dp", 2)
    lower = swap(both[:, cut:], "dp", 1)
    one = jnp.concatenate(
        [(wide(one[:, :cut]) + wide(upper)).astype(jnp.bfloat16), one[:, cut:]], 1
    )
    two = jnp.concatenate(
        [two[:, :cut], (wide(two[:, cut:]) + wide(lower)).astype(jnp.bfloat16)], 1
    )
    return [own, one, two]


def collected(blocks):
    total = wide(blocks[0])
    for k, block in enumerate(blocks[1:], 1):
        total = total + wide(swap(block, "dp", k))
    return total.astype(jnp.bfloat16)


def load_kernel(hbm_ref, vmem_ref, sem):
    copy = pltpu.make_async_copy(hbm_ref, vmem_ref, sem)
    copy.start()
    copy.wait()


def loaded(weight):
    weight = pltpu.with_memory_space_constraint(weight, pltpu.HBM)
    return pl.pallas_call(
        load_kernel,
        in_specs=[pl.BlockSpec(memory_space=pl.ANY)],
        out_specs=pl.BlockSpec(memory_space=pltpu.VMEM),
        out_shape=pltpu.VMEM(weight.shape, weight.dtype),
        scratch_shapes=[pltpu.SemaphoreType.DMA],
        compiler_params=pltpu.CompilerParams(vmem_limit_bytes=2 * 2**20),
        cost_estimate=pl.CostEstimate(
            flops=0, bytes_accessed=2 * weight.nbytes, transcendentals=0
        ),
    )(weight)


def on_device(tokens, expert_ids, gate_probs, in_weight, out_weight, swap_slot):
    groups, chips = lax.axis_size("dp"), lax.axis_size("chip")
    owners = 2 * chips
    near_chips = chips // 2
    per_device = in_weight.shape[0]
    rows, width = tokens.shape
    part = width // 2
    top_count = expert_ids.shape[1]
    experts_all = per_device * owners
    half_width = out_weight.shape[1]
    core = lax.axis_index("core")
    first = core == 0
    all_experts = jnp.arange(experts_all, dtype=jnp.int32)
    home = lax.axis_index("chip") * 2 + core

    routing = jnp.concatenate(
        [row_major(expert_ids).astype(jnp.bfloat16), *split_gates(row_major(gate_probs))], 1
    )
    routing = row_major(jnp.pad(routing, ((0, 0), (0, LANES - routing.shape[1]))))
    left, right = tokens[:, :part], tokens[:, part:]
    keep = jnp.concatenate([jnp.where(first, left, right), routing], 1)
    give = jnp.concatenate([jnp.where(first, right, left), routing], 1)
    taken = swap(give, "core", 1)
    chip_rows = row_major(
        jnp.concatenate([jnp.where(first, keep, taken), jnp.where(first, taken, keep)], 0)
    )

    def routes(meta):
        ids = meta[:, :top_count].astype(jnp.int32)
        gates = sum(
            wide(meta[:, (i + 1) * top_count : (i + 2) * top_count]) for i in range(3)
        )
        return ids, gates

    def own_sums(blocks):
        held = row_major(jnp.concatenate(blocks, 0))
        own_half = held[:, :part]
        other_half = swap(own_half, "core", 1)
        held_tokens = row_major(
            jnp.concatenate(
                [
                    jnp.where(first, own_half, other_half),
                    jnp.where(first, other_half, own_half),
                ],
                1,
            )
        )
        ids, gates = routes(held[:, part:])
        hidden = []
        for s in range(per_device):
            own_gate = jnp.sum(
                jnp.where(ids == home * per_device + s, gates, jnp.float32(0.0)), 1, keepdims=True
            )
            both = jnp.dot(held_tokens, in_weight[s], preferred_element_type=jnp.float32)
            unit = jax.nn.silu(both[:, :half_width]) * both[:, half_width:]
            hidden.append((unit * own_gate).astype(jnp.bfloat16))
        summed = jnp.dot(
            jnp.concatenate(hidden, 1),
            out_weight.reshape(per_device * half_width, width),
            preferred_element_type=jnp.float32,
        )
        return row_major(summed.astype(jnp.bfloat16))

    def chip_sums(summed, blocks):
        left, right = summed[:, :part], summed[:, part:]
        arrived = swap(jnp.where(first, right, left), "core", 1)
        chip_sum = (wide(jnp.where(first, left, right)) + wide(arrived)).astype(jnp.bfloat16)
        chip_sum = row_major(chip_sum)
        edges = [0]
        for block in blocks:
            edges.append(edges[-1] + block.shape[0])
        return [chip_sum[low:high] for low, high in zip(edges, edges[1:])]

    others = [swap(chip_rows, "chip", j) for j in range(1, chips)]
    near = [chip_rows, *spread_near(behind(chip_rows, others[0]))]
    near += joined(spread_rest(near[1:]))
    far = [row_major(jnp.concatenate(others, 0))]
    far += spread_near(far[0])
    in_weight = loaded(behind(in_weight, far[0]))
    first_blocks = [*near, far[0]]
    first_part = own_sums(first_blocks)
    far[1:] = behind(far[1:], first_part)
    rest = spread_rest(far[1:])
    sums = chip_sums(first_part, first_blocks)
    part_two = own_sums(far[1:])
    if rest:
        rest = joined(behind(rest, part_two))
        part_three = own_sums(rest)
        sums += chip_sums(part_two, far[1:]) + chip_sums(part_three, rest)
    else:
        sums += chip_sums(part_two, far[1:])
    far += rest
    sums = [jnp.concatenate([sums[k], sums[groups + k]], 0) for k in range(groups)]
    sums = with_fourth(sums)
    border = 2 * near_chips * rows
    total = collected([block[border:] for block in sums])
    blocks = [total[low : low + 2 * rows] for low in range(0, total.shape[0], 2 * rows)]
    total = collected(behind([block[:border] for block in sums], total))
    blocks = [total[low : low + 2 * rows] for low in range(0, border, 2 * rows)] + blocks
    total = wide(blocks[0])
    for j in range(1, chips):
        total = total + wide(swap(blocks[j], "chip", j))
    total = total.astype(jnp.bfloat16)
    upper, lower = total[:rows], total[rows:]
    arrived = swap(jnp.where(first, lower, upper), "core", 1)
    kept = jnp.where(first, upper, lower)
    mixed_out = row_major(
        jnp.concatenate([jnp.where(first, kept, arrived), jnp.where(first, arrived, kept)], 1)
    )

    ids, gates = routes(jnp.concatenate([block[:, part:] for block in near + far], 0))
    step = 2.0 ** (31 - (ids.shape[0] * GATE_MOST).bit_length())
    amounts = jnp.round(gates * step).astype(jnp.int32)
    totals = jnp.sum(jnp.where(ids[..., None] == all_experts, amounts[..., None], 0), (0, 1))
    totals = totals.astype(jnp.float32) * (1.0 / step)
    holder = planned_holder(all_experts, swap_slot, per_device, owners)
    owner_load = jnp.sum(
        jnp.where(
            holder == jnp.arange(owners, dtype=jnp.int32)[:, None], totals[None, :], jnp.float32(0.0)
        ),
        1,
    ) * (owners / ids.shape[0])
    return (mixed_out, owner_load)


def solution(mesh):
    groups, owners = mesh.devices.shape
    fine = Mesh(mesh.devices.reshape(groups, owners // 2, 2), ("dp", "chip", "core"))
    rows = P(("dp", "chip", "core"), None)
    return jax.shard_map(
        on_device,
        mesh=fine,
        in_specs=(
            rows,
            rows,
            rows,
            P(("chip", "core"), None, "dp"),
            P(("chip", "core"), "dp", None),
            P(),
        ),
        out_specs=(rows, P()),
        check_vma=False,
    )
```

```python
import jax
import jax.numpy as jnp
from jax import lax
from jax.experimental import pallas as pl
from jax.experimental.pallas import tpu as pltpu
from jax.experimental.layout import Layout, with_layout_constraint
from jax.sharding import Mesh, PartitionSpec as P

LANES = 128
GATE_MOST = 5


def lookup_small(values_table, index_array):
    columns = jnp.arange(values_table.shape[0], dtype=jnp.int32)
    return jnp.sum(jnp.where(index_array[..., None] == columns, values_table, 0), -1)


def planned_holder(expert_index, swap_slot, per_device, owners):
    home = expert_index // per_device
    within = expert_index % per_device
    partner = (home + owners // 2) % owners
    moved = within == lookup_small(swap_slot, home)
    return jnp.where(moved, partner, home)


def row_major(value):
    return with_layout_constraint(value, Layout(major_to_minor=tuple(range(value.ndim))))


def swap(value, axis, distance):
    size = lax.axis_size(axis)
    pairs = [(i, i ^ distance) for i in range(size)]
    return row_major(lax.ppermute(row_major(value), axis, pairs))


def split_gates(gates):
    high = lax.reduce_precision(gates, 8, 7)
    middle = lax.reduce_precision(gates - high, 8, 7)
    return [part.astype(jnp.bfloat16) for part in (high, middle, gates - high - middle)]


def cut_of(block):
    return block.shape[1] // (2 * LANES) * LANES


def spread_near(block):
    size = lax.axis_size("dp")
    return [swap(block, "dp", k) for k in range(1, 3 if size == 4 else size)]


def spread_rest(near):
    if lax.axis_size("dp") != 4:
        return []
    cut = cut_of(near[0])
    return [swap(near[0][:, :cut], "dp", 2), swap(near[1][:, cut:], "dp", 1)]


def joined(halves):
    return [jnp.concatenate(halves, 1)] if halves else []


def behind(values, others):
    return lax.optimization_barrier((values, others))[0]


def wide(value):
    return value.astype(jnp.float32)


def with_fourth(blocks):
    if len(blocks) != 4:
        return blocks
    own, one, two, both = blocks
    cut = cut_of(own)
    upper = swap(both[:, :cut], "dp", 2)
    lower = swap(both[:, cut:], "dp", 1)
    one = jnp.concatenate(
        [(wide(one[:, :cut]) + wide(upper)).astype(jnp.bfloat16), one[:, cut:]], 1
    )
    two = jnp.concatenate(
        [two[:, :cut], (wide(two[:, cut:]) + wide(lower)).astype(jnp.bfloat16)], 1
    )
    return [own, one, two]


def collected(blocks):
    total = wide(blocks[0])
    for k, block in enumerate(blocks[1:], 1):
        total = total + wide(swap(block, "dp", k))
    return total.astype(jnp.bfloat16)


def load_kernel(up_ref, down_ref, up_out, down_out, sems):
    copies = [
        pltpu.make_async_copy(up_ref, up_out, sems.at[0]),
        pltpu.make_async_copy(down_ref, down_out, sems.at[1]),
    ]
    for copy in copies:
        copy.start()
    for copy in copies:
        copy.wait()


def loaded(up, down):
    nbytes = up.nbytes + down.nbytes
    return pl.pallas_call(
        load_kernel,
        in_specs=[pl.BlockSpec(memory_space=pl.ANY)] * 2,
        out_specs=[pl.BlockSpec(memory_space=pltpu.VMEM)] * 2,
        out_shape=[pltpu.VMEM(up.shape, up.dtype), pltpu.VMEM(down.shape, down.dtype)],
        scratch_shapes=[pltpu.SemaphoreType.DMA((2,))],
        compiler_params=pltpu.CompilerParams(vmem_limit_bytes=32 * 2**20),
        cost_estimate=pl.CostEstimate(flops=0, bytes_accessed=nbytes, transcendentals=0),
    )(
        pltpu.with_memory_space_constraint(up, pltpu.HBM),
        pltpu.with_memory_space_constraint(down, pltpu.HBM),
    )


def on_device(tokens, expert_ids, gate_probs, in_weight, out_weight, swap_slot):
    groups, chips = lax.axis_size("dp"), lax.axis_size("chip")
    owners = 2 * chips
    near_chips = chips // 2
    per_device = in_weight.shape[0]
    rows, width = tokens.shape
    part = width // 2
    top_count = expert_ids.shape[1]
    experts_all = per_device * owners
    half_width = out_weight.shape[1]
    core = lax.axis_index("core")
    first = core == 0
    all_experts = jnp.arange(experts_all, dtype=jnp.int32)
    home = lax.axis_index("chip") * 2 + core

    routing = jnp.concatenate(
        [row_major(expert_ids).astype(jnp.bfloat16), *split_gates(row_major(gate_probs))], 1
    )
    routing = row_major(jnp.pad(routing, ((0, 0), (0, LANES - routing.shape[1]))))
    left, right = tokens[:, :part], tokens[:, part:]
    keep = jnp.concatenate([jnp.where(first, left, right), routing], 1)
    give = jnp.concatenate([jnp.where(first, right, left), routing], 1)
    taken = swap(give, "core", 1)
    chip_rows = row_major(
        jnp.concatenate([jnp.where(first, keep, taken), jnp.where(first, taken, keep)], 0)
    )

    def routes(meta):
        ids = meta[:, :top_count].astype(jnp.int32)
        gates = sum(
            wide(meta[:, (i + 1) * top_count : (i + 2) * top_count]) for i in range(3)
        )
        return ids, gates

    def own_sums(blocks):
        held = row_major(jnp.concatenate(blocks, 0))
        own_half = held[:, :part]
        other_half = swap(own_half, "core", 1)
        held_tokens = row_major(
            jnp.concatenate(
                [
                    jnp.where(first, own_half, other_half),
                    jnp.where(first, other_half, own_half),
                ],
                1,
            )
        )
        ids, gates = routes(held[:, part:])
        hidden = []
        for s in range(per_device):
            own_gate = jnp.sum(
                jnp.where(ids == home * per_device + s, gates, jnp.float32(0.0)), 1, keepdims=True
            )
            both = jnp.dot(held_tokens, in_weight[s], preferred_element_type=jnp.float32)
            unit = jax.nn.silu(both[:, :half_width]) * both[:, half_width:]
            hidden.append((unit * own_gate).astype(jnp.bfloat16))
        summed = jnp.dot(
            jnp.concatenate(hidden, 1),
            out_weight.reshape(per_device * half_width, width),
            preferred_element_type=jnp.float32,
        )
        return row_major(summed.astype(jnp.bfloat16))

    def chip_sums(summed, blocks):
        left, right = summed[:, :part], summed[:, part:]
        arrived = swap(jnp.where(first, right, left), "core", 1)
        chip_sum = (wide(jnp.where(first, left, right)) + wide(arrived)).astype(jnp.bfloat16)
        chip_sum = row_major(chip_sum)
        edges = [0]
        for block in blocks:
            edges.append(edges[-1] + block.shape[0])
        return [chip_sum[low:high] for low, high in zip(edges, edges[1:])]

    chip_blocks = [chip_rows] + [swap(chip_rows, "chip", j) for j in range(1, chips)]
    in_weight, out_weight = loaded(*behind((in_weight, out_weight), chip_rows))
    chip_blocks[1:] = behind(chip_blocks[1:], in_weight)
    held = [row_major(jnp.concatenate(chip_blocks, 0))]
    held += spread_near(held[0])
    first_part = own_sums(held[:1])
    held[1:] = behind(held[1:], first_part)
    rest = spread_rest(held[1:])
    sums = chip_sums(first_part, held[:1])
    second_part = own_sums(held[1:])
    sums += chip_sums(second_part, held[1:])
    if rest:
        rest = joined(behind(rest, second_part))
        sums += chip_sums(own_sums(rest), rest)
    held += rest
    sums = with_fourth(sums)
    border = 2 * near_chips * rows
    total = collected([block[border:] for block in sums])
    blocks = [total[low : low + 2 * rows] for low in range(0, total.shape[0], 2 * rows)]
    total = collected(behind([block[:border] for block in sums], total))
    blocks = [total[low : low + 2 * rows] for low in range(0, border, 2 * rows)] + blocks
    total = wide(blocks[0])
    for j in range(1, chips):
        total = total + wide(swap(blocks[j], "chip", j))
    total = total.astype(jnp.bfloat16)
    upper, lower = total[:rows], total[rows:]
    arrived = swap(jnp.where(first, lower, upper), "core", 1)
    kept = jnp.where(first, upper, lower)
    mixed_out = row_major(
        jnp.concatenate([jnp.where(first, kept, arrived), jnp.where(first, arrived, kept)], 1)
    )

    ids, gates = routes(jnp.concatenate([block[:, part:] for block in held], 0))
    step = 2.0 ** (31 - (ids.shape[0] * GATE_MOST).bit_length())
    amounts = jnp.round(gates * step).astype(jnp.int32)
    totals = jnp.sum(jnp.where(ids[..., None] == all_experts, amounts[..., None], 0), (0, 1))
    totals = totals.astype(jnp.float32) * (1.0 / step)
    holder = planned_holder(all_experts, swap_slot, per_device, owners)
    owner_load = jnp.sum(
        jnp.where(
            holder == jnp.arange(owners, dtype=jnp.int32)[:, None], totals[None, :], jnp.float32(0.0)
        ),
        1,
    ) * (owners / ids.shape[0])
    return (mixed_out, owner_load)


def solution(mesh):
    groups, owners = mesh.devices.shape
    fine = Mesh(mesh.devices.reshape(groups, owners // 2, 2), ("dp", "chip", "core"))
    rows = P(("dp", "chip", "core"), None)
    return jax.shard_map(
        on_device,
        mesh=fine,
        in_specs=(
            rows,
            rows,
            rows,
            P(("chip", "core"), None, "dp"),
            P(("chip", "core"), "dp", None),
            P(),
        ),
        out_specs=(rows, P()),
        check_vma=False,
    )
```

```python
import jax
import jax.numpy as jnp
from jax import lax
from jax.experimental import pallas as pl
from jax.experimental.pallas import tpu as pltpu
from jax.experimental.layout import Layout, with_layout_constraint
from jax.sharding import Mesh, PartitionSpec as P

LANES = 128
GATE_MOST = 5


def lookup_small(values_table, index_array):
    columns = jnp.arange(values_table.shape[0], dtype=jnp.int32)
    return jnp.sum(jnp.where(index_array[..., None] == columns, values_table, 0), -1)


def planned_holder(expert_index, swap_slot, per_device, owners):
    home = expert_index // per_device
    within = expert_index % per_device
    partner = (home + owners // 2) % owners
    moved = within == lookup_small(swap_slot, home)
    return jnp.where(moved, partner, home)


def row_major(value):
    return with_layout_constraint(value, Layout(major_to_minor=tuple(range(value.ndim))))


def swap(value, axis, distance):
    size = lax.axis_size(axis)
    pairs = [(i, i ^ distance) for i in range(size)]
    return row_major(lax.ppermute(row_major(value), axis, pairs))


def split_gates(gates):
    high = lax.reduce_precision(gates, 8, 7)
    middle = lax.reduce_precision(gates - high, 8, 7)
    return [part.astype(jnp.bfloat16) for part in (high, middle, gates - high - middle)]


def cut_of(block):
    return block.shape[1] // (2 * LANES) * LANES


def spread_near(block):
    size = lax.axis_size("dp")
    return [swap(block, "dp", k) for k in range(1, 3 if size == 4 else size)]


def spread_rest(near):
    if lax.axis_size("dp") != 4:
        return []
    cut = cut_of(near[0])
    return [swap(near[0][:, :cut], "dp", 2), swap(near[1][:, cut:], "dp", 1)]


def joined(halves):
    return [jnp.concatenate(halves, 1)] if halves else []


def behind(values, others):
    return lax.optimization_barrier((values, others))[0]


def wide(value):
    return value.astype(jnp.float32)


def with_fourth(blocks):
    if len(blocks) != 4:
        return blocks
    own, one, two, both = blocks
    cut = cut_of(own)
    upper = swap(both[:, :cut], "dp", 2)
    lower = swap(both[:, cut:], "dp", 1)
    one = jnp.concatenate(
        [(wide(one[:, :cut]) + wide(upper)).astype(jnp.bfloat16), one[:, cut:]], 1
    )
    two = jnp.concatenate(
        [two[:, :cut], (wide(two[:, cut:]) + wide(lower)).astype(jnp.bfloat16)], 1
    )
    return [own, one, two]


def collected(blocks):
    total = wide(blocks[0])
    for k, block in enumerate(blocks[1:], 1):
        total = total + wide(swap(block, "dp", k))
    return total.astype(jnp.bfloat16)


def load_kernel(up_ref, down_ref, rows_ref, up_out, down_out, rows_out, sems):
    copies = [
        pltpu.make_async_copy(up_ref, up_out, sems.at[0]),
        pltpu.make_async_copy(down_ref, down_out, sems.at[1]),
    ]
    for copy in copies:
        copy.start()
    rows_out[...] = rows_ref[...]
    for copy in copies:
        copy.wait()


def loaded(up, down, rows):
    nbytes = up.nbytes + down.nbytes
    return pl.pallas_call(
        load_kernel,
        in_specs=[pl.BlockSpec(memory_space=pl.ANY)] * 2
        + [pl.BlockSpec(memory_space=pltpu.VMEM)],
        out_specs=[pl.BlockSpec(memory_space=pltpu.VMEM)] * 3,
        out_shape=[
            pltpu.VMEM(up.shape, up.dtype),
            pltpu.VMEM(down.shape, down.dtype),
            jax.ShapeDtypeStruct(rows.shape, rows.dtype),
        ],
        scratch_shapes=[pltpu.SemaphoreType.DMA((2,))],
        compiler_params=pltpu.CompilerParams(vmem_limit_bytes=32 * 2**20),
        cost_estimate=pl.CostEstimate(flops=0, bytes_accessed=nbytes, transcendentals=0),
    )(
        pltpu.with_memory_space_constraint(up, pltpu.HBM),
        pltpu.with_memory_space_constraint(down, pltpu.HBM),
        rows,
    )


def on_device(tokens, expert_ids, gate_probs, in_weight, out_weight, swap_slot):
    groups, chips = lax.axis_size("dp"), lax.axis_size("chip")
    owners = 2 * chips
    near_chips = chips // 2
    per_device = in_weight.shape[0]
    rows, width = tokens.shape
    part = width // 2
    top_count = expert_ids.shape[1]
    experts_all = per_device * owners
    half_width = out_weight.shape[1]
    core = lax.axis_index("core")
    first = core == 0
    all_experts = jnp.arange(experts_all, dtype=jnp.int32)
    home = lax.axis_index("chip") * 2 + core

    routing = jnp.concatenate(
        [row_major(expert_ids).astype(jnp.bfloat16), *split_gates(row_major(gate_probs))], 1
    )
    routing = row_major(jnp.pad(routing, ((0, 0), (0, LANES - routing.shape[1]))))
    left, right = tokens[:, :part], tokens[:, part:]
    keep = jnp.concatenate([jnp.where(first, left, right), routing], 1)
    give = jnp.concatenate([jnp.where(first, right, left), routing], 1)
    taken = swap(give, "core", 1)
    chip_rows = row_major(
        jnp.concatenate([jnp.where(first, keep, taken), jnp.where(first, taken, keep)], 0)
    )

    def routes(meta):
        ids = meta[:, :top_count].astype(jnp.int32)
        gates = sum(
            wide(meta[:, (i + 1) * top_count : (i + 2) * top_count]) for i in range(3)
        )
        return ids, gates

    def own_sums(blocks):
        held = row_major(jnp.concatenate(blocks, 0))
        own_half = held[:, :part]
        other_half = swap(own_half, "core", 1)
        held_tokens = row_major(
            jnp.concatenate(
                [
                    jnp.where(first, own_half, other_half),
                    jnp.where(first, other_half, own_half),
                ],
                1,
            )
        )
        ids, gates = routes(held[:, part:])
        hidden = []
        for s in range(per_device):
            own_gate = jnp.sum(
                jnp.where(ids == home * per_device + s, gates, jnp.float32(0.0)), 1, keepdims=True
            )
            both = jnp.dot(held_tokens, in_weight[s], preferred_element_type=jnp.float32)
            unit = jax.nn.silu(both[:, :half_width]) * both[:, half_width:]
            hidden.append((unit * own_gate).astype(jnp.bfloat16))
        summed = jnp.dot(
            jnp.concatenate(hidden, 1),
            out_weight.reshape(per_device * half_width, width),
            preferred_element_type=jnp.float32,
        )
        return row_major(summed.astype(jnp.bfloat16))

    def chip_sums(summed, blocks):
        left, right = summed[:, :part], summed[:, part:]
        arrived = swap(jnp.where(first, right, left), "core", 1)
        chip_sum = (wide(jnp.where(first, left, right)) + wide(arrived)).astype(jnp.bfloat16)
        chip_sum = row_major(chip_sum)
        edges = [0]
        for block in blocks:
            edges.append(edges[-1] + block.shape[0])
        return [chip_sum[low:high] for low, high in zip(edges, edges[1:])]

    chip_blocks = [chip_rows] + [swap(chip_rows, "chip", j) for j in range(1, chips)]
    in_weight, out_weight, chip_blocks[0] = loaded(in_weight, out_weight, chip_rows)
    held = [row_major(jnp.concatenate(chip_blocks, 0))]
    held += spread_near(held[0])
    first_part = own_sums(held[:1])
    held[1:] = behind(held[1:], first_part)
    rest = spread_rest(held[1:])
    sums = chip_sums(first_part, held[:1])
    second_part = own_sums(held[1:])
    sums += chip_sums(second_part, held[1:])
    if rest:
        rest = joined(behind(rest, second_part))
        sums += chip_sums(own_sums(rest), rest)
    held += rest
    sums = with_fourth(sums)
    border = 2 * near_chips * rows
    total = collected([block[border:] for block in sums])
    blocks = [total[low : low + 2 * rows] for low in range(0, total.shape[0], 2 * rows)]
    total = collected(behind([block[:border] for block in sums], total))
    blocks = [total[low : low + 2 * rows] for low in range(0, border, 2 * rows)] + blocks
    total = wide(blocks[0])
    for j in range(1, chips):
        total = total + wide(swap(blocks[j], "chip", j))
    total = total.astype(jnp.bfloat16)
    upper, lower = total[:rows], total[rows:]
    arrived = swap(jnp.where(first, lower, upper), "core", 1)
    kept = jnp.where(first, upper, lower)
    mixed_out = row_major(
        jnp.concatenate([jnp.where(first, kept, arrived), jnp.where(first, arrived, kept)], 1)
    )

    ids, gates = routes(jnp.concatenate([block[:, part:] for block in held], 0))
    step = 2.0 ** (31 - (ids.shape[0] * GATE_MOST).bit_length())
    amounts = jnp.round(gates * step).astype(jnp.int32)
    totals = jnp.sum(jnp.where(ids[..., None] == all_experts, amounts[..., None], 0), (0, 1))
    totals = totals.astype(jnp.float32) * (1.0 / step)
    holder = planned_holder(all_experts, swap_slot, per_device, owners)
    owner_load = jnp.sum(
        jnp.where(
            holder == jnp.arange(owners, dtype=jnp.int32)[:, None], totals[None, :], jnp.float32(0.0)
        ),
        1,
    ) * (owners / ids.shape[0])
    return (mixed_out, owner_load)


def solution(mesh):
    groups, owners = mesh.devices.shape
    fine = Mesh(mesh.devices.reshape(groups, owners // 2, 2), ("dp", "chip", "core"))
    rows = P(("dp", "chip", "core"), None)
    return jax.shard_map(
        on_device,
        mesh=fine,
        in_specs=(
            rows,
            rows,
            rows,
            P(("chip", "core"), None, "dp"),
            P(("chip", "core"), "dp", None),
            P(),
        ),
        out_specs=(rows, P()),
        check_vma=False,
    )
```

```python
import jax
import jax.numpy as jnp
from jax import lax
from jax.experimental import pallas as pl
from jax.experimental.pallas import tpu as pltpu
from jax.experimental.layout import Layout, with_layout_constraint
from jax.sharding import Mesh, PartitionSpec as P

LANES = 128
TOP_LANES = 8
CHUNK = 1024
TILE = 512
VMEM_LIMIT = 12 * 2**20
GATE_MOST = 5


def lookup_small(values_table, index_array):
    columns = jnp.arange(values_table.shape[0], dtype=jnp.int32)
    return jnp.sum(jnp.where(index_array[..., None] == columns, values_table, 0), -1)


def planned_holder(expert_index, swap_slot, per_device, owners):
    home = expert_index // per_device
    within = expert_index % per_device
    partner = (home + owners // 2) % owners
    moved = within == lookup_small(swap_slot, home)
    return jnp.where(moved, partner, home)


def row_major(value):
    return with_layout_constraint(value, Layout(major_to_minor=tuple(range(value.ndim))))


def swap(value, axis, distance):
    size = lax.axis_size(axis)
    pairs = [(i, i ^ distance) for i in range(size)]
    return row_major(lax.ppermute(row_major(value), axis, pairs))


def split_gates(gates):
    high = lax.reduce_precision(gates, 8, 7)
    middle = lax.reduce_precision(gates - high, 8, 7)
    return [part.astype(jnp.bfloat16) for part in (high, middle, gates - high - middle)]


def cut_of(block):
    return block.shape[1] // (2 * LANES) * LANES


def spread_near(block):
    size = lax.axis_size("dp")
    return [swap(block, "dp", k) for k in range(1, 3 if size == 4 else size)]


def spread_rest(near):
    if lax.axis_size("dp") != 4:
        return []
    cut = cut_of(near[0])
    return [swap(near[0][:, :cut], "dp", 2), swap(near[1][:, cut:], "dp", 1)]


def behind(values, others):
    return lax.optimization_barrier((values, others))[0]


def wide(value):
    return value.astype(jnp.float32)


def with_fourth(blocks):
    if len(blocks) != 4:
        return blocks
    own, one, two, both = blocks
    cut = cut_of(own)
    upper = swap(both[:, :cut], "dp", 2)
    lower = swap(both[:, cut:], "dp", 1)
    one = jnp.concatenate(
        [(wide(one[:, :cut]) + wide(upper)).astype(jnp.bfloat16), one[:, cut:]], 1
    )
    two = jnp.concatenate(
        [two[:, :cut], (wide(two[:, cut:]) + wide(lower)).astype(jnp.bfloat16)], 1
    )
    return [own, one, two]


def collected(blocks):
    total = wide(blocks[0])
    for k, block in enumerate(blocks[1:], 1):
        total = total + wide(swap(block, "dp", k))
    return total.astype(jnp.bfloat16)


def sums_kernel(layout, filling, *refs):
    widths, block_count = layout
    refs = list(refs)
    place = refs.pop(0)
    sides = [[[refs.pop(0) for _ in range(block_count)] for _ in widths] for _ in range(2)]
    if filling:
        up_hbm, down_hbm, keep_ref, give_ref, up, down, acc, hidden, sems = refs
    else:
        up, down, keep_ref, give_ref, acc, hidden = refs
    core, first_expert = place[0], place[1]
    per_device, width, both_width = up.shape
    half_width = both_width // 2
    part = width // 2
    bases = [core * part, (1 - core) * part]
    arrivals = {}
    if filling:
        copies = []
        for side in range(2):
            for low in range(0, part, CHUNK):
                for s in range(per_device):
                    at = pl.ds(pl.multiple_of(bases[side] + low, CHUNK), CHUNK)
                    copies.append((up_hbm.at[s, at], up.at[s, at], (side, low)))
        deep = down.shape[0]
        for low in range(0, deep, half_width):
            at = pl.ds(low, half_width)
            copies.append((down_hbm.at[at], down.at[at], "down"))
        for number, (source, target, key) in enumerate(copies):
            copy = pltpu.make_async_copy(source, target, sems.at[number])
            copy.start()
            arrivals.setdefault(key, []).append(copy)

    def arrive(key):
        for copy in arrivals.get(key, ()):
            copy.wait()

    acc[...] = jnp.zeros_like(acc)
    for side in range(2):
        offset = 0
        for blocks, seg_width in zip(sides[side], widths):
            for low in range(0, seg_width, CHUNK):
                arrive((side, offset + low))

                @pl.loop(0, CHUNK // TILE)
                def _(step, blocks=blocks, low=low, at=bases[side] + offset + low):
                    columns = pl.ds(pl.multiple_of(low + step * TILE, TILE), TILE)
                    held = [block[:, columns] for block in blocks]
                    held = held[0] if len(held) == 1 else jnp.concatenate(held, 0)
                    rows = pl.ds(pl.multiple_of(at + step * TILE, TILE), TILE)
                    for s in range(per_device):
                        acc[s] += jnp.dot(held, up[s, rows], preferred_element_type=jnp.float32)

            offset += seg_width

    last = widths[-1]
    meta = [block[:, last:].astype(jnp.float32) for block in sides[0][-1]]
    meta = meta[0] if len(meta) == 1 else jnp.concatenate(meta, 0)
    gates = sum(pltpu.roll(meta, LANES - k * TOP_LANES, 1) for k in (1, 2, 3))
    lanes = lax.broadcasted_iota(jnp.int32, meta.shape, 1)
    for s in range(per_device):
        chosen = (meta.astype(jnp.int32) == first_expert + s) & (lanes < TOP_LANES)
        own_gate = jnp.sum(jnp.where(chosen, gates, 0.0), 1, keepdims=True)
        gate_half, up_half = acc[s, :, :half_width], acc[s, :, half_width:]
        unit = gate_half * (1.0 / (1.0 + jnp.exp(-gate_half))) * up_half
        hidden[:, s * half_width : (s + 1) * half_width] = (unit * own_gate).astype(jnp.bfloat16)

    arrive("down")
    for base, out in ((bases[1], give_ref), (bases[0], keep_ref)):

        @pl.loop(0, part // TILE)
        def _(step, base=base, out=out):
            columns = pl.ds(pl.multiple_of(base + step * TILE, TILE), TILE)
            target = pl.ds(pl.multiple_of(step * TILE, TILE), TILE)
            out[:, target] = jnp.dot(
                hidden[...], down[:, columns], preferred_element_type=jnp.float32
            ).astype(jnp.bfloat16)


def gated_sums(place, own, other, up, down, filling):
    widths = tuple(segment[0].shape[1] for segment in other)
    block_count = len(own[0])
    count = sum(block.shape[0] for block in own[0])
    per_device, width, both_width = up.shape
    operands = [block for segments in (own, other) for segment in segments for block in segment]
    in_vmem = pl.BlockSpec(memory_space=pltpu.VMEM)
    operands = [pltpu.with_memory_space_constraint(x, pltpu.VMEM) for x in operands]
    out_shape = [pltpu.VMEM((count, width // 2), jnp.bfloat16)] * 2
    scratch = [
        pltpu.VMEM((per_device, count, both_width), jnp.float32),
        pltpu.VMEM((count, down.shape[0]), jnp.bfloat16),
    ]
    if filling:
        weights = [pltpu.with_memory_space_constraint(w, pltpu.HBM) for w in (up, down)]
        weight_specs = [pl.BlockSpec(memory_space=pl.ANY)] * 2
        out_shape += [pltpu.VMEM(up.shape, up.dtype), pltpu.VMEM(down.shape, down.dtype)]
        scratch += [pltpu.SemaphoreType.DMA((per_device * (width // CHUNK + 1),))]
        moved = up.nbytes + down.nbytes
    else:
        weights = [pltpu.with_memory_space_constraint(w, pltpu.VMEM) for w in (up, down)]
        weight_specs = [in_vmem] * 2
        moved = 0
    return pl.pallas_call(
        lambda *refs: sums_kernel((widths, block_count), filling, *refs),
        in_specs=[pl.BlockSpec(memory_space=pltpu.SMEM)]
        + [in_vmem] * len(operands)
        + weight_specs,
        out_specs=[in_vmem] * len(out_shape),
        out_shape=out_shape,
        scratch_shapes=scratch,
        compiler_params=pltpu.CompilerParams(vmem_limit_bytes=VMEM_LIMIT),
        cost_estimate=pl.CostEstimate(
            flops=2 * count * (up.size + down.size),
            bytes_accessed=moved,
            transcendentals=count * down.shape[0],
        ),
    )(place, *operands, *weights)


def on_device(tokens, expert_ids, gate_probs, in_weight, out_weight, swap_slot):
    groups, chips = lax.axis_size("dp"), lax.axis_size("chip")
    owners = 2 * chips
    near_chips = chips // 2
    per_device = in_weight.shape[0]
    rows, width = tokens.shape
    part = width // 2
    top_count = expert_ids.shape[1]
    experts_all = per_device * owners
    half_width = out_weight.shape[1]
    core = lax.axis_index("core")
    first = core == 0
    all_experts = jnp.arange(experts_all, dtype=jnp.int32)
    first_expert = (lax.axis_index("chip") * 2 + core) * per_device
    place = jnp.stack([core, first_expert]).astype(jnp.int32)

    routing = jnp.concatenate(
        [row_major(expert_ids).astype(jnp.bfloat16), *split_gates(row_major(gate_probs))], 1
    )
    routing = row_major(jnp.pad(routing, ((0, 0), (0, LANES - routing.shape[1]))))
    left, right = tokens[:, :part], tokens[:, part:]
    keep = jnp.concatenate([jnp.where(first, left, right), routing], 1)
    give = jnp.concatenate([jnp.where(first, right, left), routing], 1)
    taken = swap(give, "core", 1)
    chip_rows = row_major(
        jnp.concatenate([jnp.where(first, keep, taken), jnp.where(first, taken, keep)], 0)
    )

    def routes(meta):
        ids = meta[:, :top_count].astype(jnp.int32)
        gates = sum(
            wide(meta[:, (i + 1) * top_count : (i + 2) * top_count]) for i in range(3)
        )
        return ids, gates

    def sums_of(own, weights, filling=False):
        last = len(own) - 1
        bare = [
            [block[:, : block.shape[1] - (LANES if i == last else 0)] for block in segment]
            for i, segment in enumerate(own)
        ]
        other = [[swap(block, "core", 1) for block in segment] for segment in bare]
        keep, give, *filled = gated_sums(place, own, other, *weights, filling)
        return keep, give, filled or weights

    def chip_sums(keep, give):
        return (wide(keep) + wide(swap(give, "core", 1))).astype(jnp.bfloat16)

    chip_blocks = [chip_rows] + [swap(chip_rows, "chip", j) for j in range(1, chips)]
    held = [row_major(jnp.concatenate(chip_blocks, 0))]
    near = spread_near(held[0])
    weights = (in_weight, out_weight.reshape(per_device * half_width, width))
    keep, give, weights = sums_of([held], weights, filling=True)
    near = behind(near, give)
    rest = spread_rest(near)
    sums = [chip_sums(keep, give)]
    if rest:
        keep, give, _ = sums_of([near], weights)
        pair = chip_sums(keep, give)
        sums += [pair[: pair.shape[0] // 2], pair[pair.shape[0] // 2 :]]
        rest = behind(rest, give)
        keep, give, _ = sums_of([[half] for half in rest], weights)
        sums += [chip_sums(keep, give)]
    else:
        for block in near:
            keep, give, _ = sums_of([[block]], weights)
            sums += [chip_sums(keep, give)]
    metas = [block[:, block.shape[1] - LANES :] for block in held + near + rest[1:]]
    sums = with_fourth(sums)
    border = 2 * near_chips * rows
    total = collected([block[border:] for block in sums])
    blocks = [total[low : low + 2 * rows] for low in range(0, total.shape[0], 2 * rows)]
    total = collected(behind([block[:border] for block in sums], total))
    blocks = [total[low : low + 2 * rows] for low in range(0, border, 2 * rows)] + blocks
    total = wide(blocks[0])
    for j in range(1, chips):
        total = total + wide(swap(blocks[j], "chip", j))
    total = total.astype(jnp.bfloat16)
    upper, lower = total[:rows], total[rows:]
    arrived = swap(jnp.where(first, lower, upper), "core", 1)
    kept = jnp.where(first, upper, lower)
    mixed_out = row_major(
        jnp.concatenate([jnp.where(first, kept, arrived), jnp.where(first, arrived, kept)], 1)
    )

    ids, gates = routes(jnp.concatenate(metas, 0))
    step = 2.0 ** (31 - (ids.shape[0] * GATE_MOST).bit_length())
    amounts = jnp.round(gates * step).astype(jnp.int32)
    totals = jnp.sum(jnp.where(ids[..., None] == all_experts, amounts[..., None], 0), (0, 1))
    totals = totals.astype(jnp.float32) * (1.0 / step)
    holder = planned_holder(all_experts, swap_slot, per_device, owners)
    owner_load = jnp.sum(
        jnp.where(
            holder == jnp.arange(owners, dtype=jnp.int32)[:, None], totals[None, :], jnp.float32(0.0)
        ),
        1,
    ) * (owners / ids.shape[0])
    return (mixed_out, owner_load)


def solution(mesh):
    groups, owners = mesh.devices.shape
    fine = Mesh(mesh.devices.reshape(groups, owners // 2, 2), ("dp", "chip", "core"))
    rows = P(("dp", "chip", "core"), None)
    return jax.shard_map(
        on_device,
        mesh=fine,
        in_specs=(
            rows,
            rows,
            rows,
            P(("chip", "core"), None, "dp"),
            P(("chip", "core"), "dp", None),
            P(),
        ),
        out_specs=(rows, P()),
        check_vma=False,
    )
```

```python
import jax
import jax.numpy as jnp
from jax import lax
from jax.experimental import pallas as pl
from jax.experimental.pallas import tpu as pltpu
from jax.experimental.layout import Layout, with_layout_constraint
from jax.sharding import Mesh, PartitionSpec as P

LANES = 128
CHUNK = 1024
VMEM_LIMIT = 12 * 2**20
GATE_MOST = 5


def lookup_small(values_table, index_array):
    columns = jnp.arange(values_table.shape[0], dtype=jnp.int32)
    return jnp.sum(jnp.where(index_array[..., None] == columns, values_table, 0), -1)


def planned_holder(expert_index, swap_slot, per_device, owners):
    home = expert_index // per_device
    within = expert_index % per_device
    partner = (home + owners // 2) % owners
    moved = within == lookup_small(swap_slot, home)
    return jnp.where(moved, partner, home)


def row_major(value):
    return with_layout_constraint(value, Layout(major_to_minor=tuple(range(value.ndim))))


def swap(value, axis, distance):
    size = lax.axis_size(axis)
    pairs = [(i, i ^ distance) for i in range(size)]
    return row_major(lax.ppermute(row_major(value), axis, pairs))


def cut_of(block):
    return block.shape[1] // (2 * LANES) * LANES


def spread_near(block):
    size = lax.axis_size("dp")
    return [swap(block, "dp", k) for k in range(1, 3 if size == 4 else size)]


def spread_rest(near):
    if lax.axis_size("dp") != 4:
        return []
    cut = cut_of(near[0])
    return [swap(near[0][:, :cut], "dp", 2), swap(near[1][:, cut:], "dp", 1)]


def behind(values, others):
    return lax.optimization_barrier((values, others))[0]


def wide(value):
    return value.astype(jnp.float32)


def with_fourth(blocks, halves):
    own, one, two = blocks
    cut = cut_of(own)
    upper, lower = swap(halves[0], "dp", 2), swap(halves[1], "dp", 1)
    one = jnp.concatenate(
        [(wide(one[:, :cut]) + wide(upper)).astype(jnp.bfloat16), one[:, cut:]], 1
    )
    two = jnp.concatenate(
        [two[:, :cut], (wide(two[:, cut:]) + wide(lower)).astype(jnp.bfloat16)], 1
    )
    return [own, one, two]


def collected(blocks):
    total = wide(blocks[0])
    for k, block in enumerate(blocks[1:], 1):
        total = total + wide(swap(block, "dp", k))
    return total.astype(jnp.bfloat16)


def sums_kernel(layout, filling, *refs):
    widths, block_count, top_count = layout
    refs = list(refs)
    place = refs.pop(0)
    sides = [[[refs.pop(0) for _ in range(block_count)] for _ in widths] for _ in range(2)]
    if filling:
        up_hbm, down_hbm, keep_ref, give_ref, up, down, acc, hidden, sems = refs
    else:
        up, down, keep_ref, give_ref, acc, hidden = refs
    core, first_expert = place[0], place[1]
    per_device, width, both_width = up.shape
    half_width = both_width // 2
    part = width // 2
    bases = [core * part, (1 - core) * part]
    arrivals = {}
    if filling:
        copies = []
        for side in range(2):
            for low in range(0, part, CHUNK):
                for s in range(per_device):
                    at = pl.ds(pl.multiple_of(bases[side] + low, CHUNK), CHUNK)
                    copies.append((up_hbm.at[s, at], up.at[s, at], (side, low)))
        deep = down.shape[0]
        for low in range(0, deep, half_width):
            at = pl.ds(low, half_width)
            copies.append((down_hbm.at[at], down.at[at], "down"))
        for number, (source, target, key) in enumerate(copies):
            copy = pltpu.make_async_copy(source, target, sems.at[number])
            copy.start()
            arrivals.setdefault(key, []).append(copy)

    def arrive(key):
        for copy in arrivals.get(key, ()):
            copy.wait()

    acc[...] = jnp.zeros_like(acc)
    for side in range(2):
        offset = 0
        for blocks, seg_width in zip(sides[side], widths):
            for low in range(0, seg_width, CHUNK):
                arrive((side, offset + low))
                held = [block[:, low : low + CHUNK] for block in blocks]
                held = held[0] if len(held) == 1 else jnp.concatenate(held, 0)
                rows = pl.ds(pl.multiple_of(bases[side] + offset + low, CHUNK), CHUNK)
                for s in range(per_device):
                    acc[s] += jnp.dot(held, up[s, rows], preferred_element_type=jnp.float32)
            offset += seg_width

    last = widths[-1]
    meta = [block[:, last:].astype(jnp.float32) for block in sides[0][-1]]
    meta = meta[0] if len(meta) == 1 else jnp.concatenate(meta, 0)
    gates = sum(pltpu.roll(meta, LANES - k * top_count, 1) for k in (1, 2, 3))
    lanes = lax.broadcasted_iota(jnp.int32, meta.shape, 1)
    for s in range(per_device):
        chosen = (meta.astype(jnp.int32) == first_expert + s) & (lanes < top_count)
        own_gate = jnp.sum(jnp.where(chosen, gates, 0.0), 1, keepdims=True)
        gate_half, up_half = acc[s, :, :half_width], acc[s, :, half_width:]
        unit = gate_half * (1.0 / (1.0 + jnp.exp(-gate_half))) * up_half
        hidden[:, s * half_width : (s + 1) * half_width] = (unit * own_gate).astype(jnp.bfloat16)

    arrive("down")
    for base, out in ((bases[1], give_ref), (bases[0], keep_ref)):
        for low in range(0, part, CHUNK):
            columns = pl.ds(pl.multiple_of(base + low, CHUNK), CHUNK)
            out[:, low : low + CHUNK] = jnp.dot(
                hidden[...], down[:, columns], preferred_element_type=jnp.float32
            ).astype(jnp.bfloat16)


def gated_sums(place, top_count, own, other, up, down, filling):
    widths = tuple(segment[0].shape[1] for segment in other)
    block_count = len(own[0])
    count = sum(block.shape[0] for block in own[0])
    per_device, width, both_width = up.shape
    operands = [block for segments in (own, other) for segment in segments for block in segment]
    in_vmem = pl.BlockSpec(memory_space=pltpu.VMEM)
    operands = [pltpu.with_memory_space_constraint(x, pltpu.VMEM) for x in operands]
    out_shape = [pltpu.VMEM((count, width // 2), jnp.bfloat16)] * 2
    scratch = [
        pltpu.VMEM((per_device, count, both_width), jnp.float32),
        pltpu.VMEM((count, down.shape[0]), jnp.bfloat16),
    ]
    if filling:
        weights = [pltpu.with_memory_space_constraint(w, pltpu.HBM) for w in (up, down)]
        weight_specs = [pl.BlockSpec(memory_space=pl.ANY)] * 2
        out_shape += [pltpu.VMEM(up.shape, up.dtype), pltpu.VMEM(down.shape, down.dtype)]
        scratch += [pltpu.SemaphoreType.DMA((per_device * (width // CHUNK + 1),))]
        moved = up.nbytes + down.nbytes
    else:
        weights = [pltpu.with_memory_space_constraint(w, pltpu.VMEM) for w in (up, down)]
        weight_specs = [in_vmem] * 2
        moved = 0
    return pl.pallas_call(
        lambda *refs: sums_kernel((widths, block_count, top_count), filling, *refs),
        in_specs=[pl.BlockSpec(memory_space=pltpu.SMEM)]
        + [in_vmem] * len(operands)
        + weight_specs,
        out_specs=[in_vmem] * len(out_shape),
        out_shape=out_shape,
        scratch_shapes=scratch,
        compiler_params=pltpu.CompilerParams(vmem_limit_bytes=VMEM_LIMIT),
        cost_estimate=pl.CostEstimate(
            flops=2 * count * (up.size + down.size),
            bytes_accessed=moved,
            transcendentals=count * down.shape[0],
        ),
    )(place, *operands, *weights)


def first_kernel(place, *refs):
    sources, (keep_ref, give_ref, tokens, ids, gates, turned, sems) = refs[:3], refs[3:]
    copies = [
        pltpu.make_async_copy(source, target, sems.at[number])
        for number, (source, target) in enumerate(zip(sources, (tokens, ids, gates)))
    ]
    for copy in copies:
        copy.start()
    for copy in copies:
        copy.wait()
    core = place[0]
    part = tokens.shape[1] // 2
    top_count, rows = ids.shape
    turned[...] = jnp.zeros_like(turned)
    left = gates[...]
    parts = [ids[...].astype(jnp.float32)]
    for _ in range(3):
        parts.append(left.astype(jnp.bfloat16).astype(jnp.float32))
        left = left - parts[-1]
    for number, values in enumerate(parts):
        turned[number * top_count : (number + 1) * top_count, :rows] = values
    routing = turned[...].T[:rows].astype(jnp.bfloat16)
    for half, out in ((core, keep_ref), (1 - core, give_ref)):
        out[:, :part] = tokens[:, pl.ds(pl.multiple_of(half * part, LANES), part)]
        out[:, part:] = routing


def first_halves(place, tokens, expert_ids, gate_probs):
    rows, width = tokens.shape
    sources = [tokens, expert_ids.T, gate_probs.T]
    return pl.pallas_call(
        first_kernel,
        in_specs=[pl.BlockSpec(memory_space=pltpu.SMEM)]
        + [pl.BlockSpec(memory_space=pl.ANY)] * 3,
        out_specs=[pl.BlockSpec(memory_space=pltpu.VMEM)] * 2,
        out_shape=[pltpu.VMEM((rows, width // 2 + LANES), jnp.bfloat16)] * 2,
        scratch_shapes=[pltpu.VMEM(x.shape, x.dtype) for x in sources]
        + [pltpu.VMEM((LANES, LANES), jnp.float32), pltpu.SemaphoreType.DMA((3,))],
        compiler_params=pltpu.CompilerParams(vmem_limit_bytes=VMEM_LIMIT),
    )(place, *(pltpu.with_memory_space_constraint(x, pltpu.HBM) for x in sources))


def added_kernel(kept_ref, taken_ref, left_ref, right_ref):
    total = kept_ref[...].astype(jnp.float32) + taken_ref[...].astype(jnp.float32)
    cut = left_ref.shape[1]
    left_ref[...] = total[:, :cut].astype(jnp.bfloat16)
    right_ref[...] = total[:, cut:].astype(jnp.bfloat16)


def added(kept, taken, cut):
    in_vmem = pl.BlockSpec(memory_space=pltpu.VMEM)
    count, width = kept.shape
    return pl.pallas_call(
        added_kernel,
        in_specs=[in_vmem] * 2,
        out_specs=[in_vmem] * 2,
        out_shape=[
            pltpu.VMEM((count, cut), jnp.bfloat16),
            pltpu.VMEM((count, width - cut), jnp.bfloat16),
        ],
        compiler_params=pltpu.CompilerParams(vmem_limit_bytes=VMEM_LIMIT),
    )(*(pltpu.with_memory_space_constraint(x, pltpu.VMEM) for x in (kept, taken)))


def on_device(tokens, expert_ids, gate_probs, in_weight, out_weight, swap_slot):
    groups, chips = lax.axis_size("dp"), lax.axis_size("chip")
    owners = 2 * chips
    near_chips = chips // 2
    per_device = in_weight.shape[0]
    rows, width = tokens.shape
    part = width // 2
    top_count = expert_ids.shape[1]
    experts_all = per_device * owners
    half_width = out_weight.shape[1]
    core = lax.axis_index("core")
    first = core == 0
    all_experts = jnp.arange(experts_all, dtype=jnp.int32)
    first_expert = (lax.axis_index("chip") * 2 + core) * per_device
    place = jnp.stack([core, first_expert]).astype(jnp.int32)

    keep, give = first_halves(place, tokens, expert_ids, gate_probs)
    taken = swap(give, "core", 1)
    chip_rows = row_major(
        jnp.concatenate([jnp.where(first, keep, taken), jnp.where(first, taken, keep)], 0)
    )

    def routes(meta):
        ids = meta[:, :top_count].astype(jnp.int32)
        gates = sum(
            wide(meta[:, (i + 1) * top_count : (i + 2) * top_count]) for i in range(3)
        )
        return ids, gates

    def sums_of(own, weights, filling=False):
        last = len(own) - 1
        bare = [
            [block[:, : block.shape[1] - (LANES if i == last else 0)] for block in segment]
            for i, segment in enumerate(own)
        ]
        other = [[swap(block, "core", 1) for block in segment] for segment in bare]
        keep, give, *filled = gated_sums(
            place, top_count, own, other, *weights, filling
        )
        return keep, give, filled or weights

    def chip_sums(keep, give):
        return (wide(keep) + wide(swap(give, "core", 1))).astype(jnp.bfloat16)

    chip_blocks = [chip_rows] + [swap(chip_rows, "chip", j) for j in range(1, chips)]
    direct = [swap(chip_rows, "dp", k) for k in range(1, groups)]
    far = row_major(jnp.concatenate(chip_blocks[1:], 0))
    held = row_major(jnp.concatenate([*chip_blocks, *direct], 0))
    near = spread_near(far)
    weights = (in_weight, out_weight.reshape(per_device * half_width, width))
    keep, give, weights = sums_of([[held]], weights, filling=True)
    near = behind(near, give)
    rest = spread_rest(near)
    first_sum = chip_sums(keep, give)
    own_sum = first_sum[: chips * 2 * rows]
    direct_sums = [
        first_sum[low : low + 2 * rows]
        for low in range(chips * 2 * rows, first_sum.shape[0], 2 * rows)
    ]
    if rest:
        near = row_major(jnp.concatenate(near, 0))
        keep, give, _ = sums_of([[near]], weights)
        pair = chip_sums(keep, give)
        sums = [pair[: far.shape[0]], pair[far.shape[0] :]]
        rest = behind(rest, give)
        keep, give, _ = sums_of([[half] for half in rest], weights)
        cut = rest[0].shape[1]
        diagonal = added(keep, swap(give, "core", 1), cut)
        diagonal = [
            jnp.concatenate([block, half], 0)
            for block, half in zip((direct_sums[2][:, :cut], direct_sums[2][:, cut:]), diagonal)
        ]
        sums = [jnp.concatenate([o, s], 0) for o, s in zip(direct_sums, sums)]
        sums = with_fourth([own_sum, *sums], diagonal)
        metas = [held, near, rest[1]]
    else:
        sums = [own_sum]
        for block, o in zip(near, direct_sums):
            keep, give, _ = sums_of([[block]], weights)
            sums += [jnp.concatenate([o, chip_sums(keep, give)], 0)]
        metas = [held, *near]
    metas = [block[:, block.shape[1] - LANES :] for block in metas]
    border = 2 * near_chips * rows
    total = collected([block[border:] for block in sums])
    blocks = [total[low : low + 2 * rows] for low in range(0, total.shape[0], 2 * rows)]
    total = collected(behind([block[:border] for block in sums], total))
    blocks = [total[low : low + 2 * rows] for low in range(0, border, 2 * rows)] + blocks
    total = wide(blocks[0])
    for j in range(1, chips):
        total = total + wide(swap(blocks[j], "chip", j))
    total = total.astype(jnp.bfloat16)
    upper, lower = total[:rows], total[rows:]
    arrived = swap(jnp.where(first, lower, upper), "core", 1)
    kept = jnp.where(first, upper, lower)
    mixed_out = row_major(
        jnp.concatenate([jnp.where(first, kept, arrived), jnp.where(first, arrived, kept)], 1)
    )

    ids, gates = routes(jnp.concatenate(metas, 0))
    step = 2.0 ** (31 - (ids.shape[0] * GATE_MOST).bit_length())
    amounts = jnp.round(gates * step).astype(jnp.int32)
    totals = jnp.sum(jnp.where(ids[..., None] == all_experts, amounts[..., None], 0), (0, 1))
    totals = totals.astype(jnp.float32) * (1.0 / step)
    holder = planned_holder(all_experts, swap_slot, per_device, owners)
    owner_load = jnp.sum(
        jnp.where(
            holder == jnp.arange(owners, dtype=jnp.int32)[:, None], totals[None, :], jnp.float32(0.0)
        ),
        1,
    ) * (owners / ids.shape[0])
    return (mixed_out, owner_load)


def solution(mesh):
    groups, owners = mesh.devices.shape
    fine = Mesh(mesh.devices.reshape(groups, owners // 2, 2), ("dp", "chip", "core"))
    rows = P(("dp", "chip", "core"), None)
    return jax.shard_map(
        on_device,
        mesh=fine,
        in_specs=(
            rows,
            rows,
            rows,
            P(("chip", "core"), None, "dp"),
            P(("chip", "core"), "dp", None),
            P(),
        ),
        out_specs=(rows, P()),
        check_vma=False,
    )
```

```python
import jax
import jax.numpy as jnp
from jax import lax
from jax.experimental import pallas as pl
from jax.experimental.pallas import tpu as pltpu
from jax.experimental.layout import Layout, with_layout_constraint
from jax.sharding import Mesh, PartitionSpec as P

LANES = 128
PART = 1024.0
CHUNK = 1024
VMEM_LIMIT = 12 * 2**20
GATE_MOST = 5


def row_major(value):
    return with_layout_constraint(value, Layout(major_to_minor=tuple(range(value.ndim))))


def swap(value, axis, distance):
    size = lax.axis_size(axis)
    pairs = [(i, i ^ distance) for i in range(size)]
    return row_major(lax.ppermute(row_major(value), axis, pairs))


def cut_of(block):
    return block.shape[1] // (2 * LANES) * LANES


def spread_near(block):
    size = lax.axis_size("dp")
    return [swap(block, "dp", k) for k in range(1, 3 if size == 4 else size)]


def spread_rest(near):
    if lax.axis_size("dp") != 4:
        return []
    cut = cut_of(near[0])
    return [swap(near[0][:, :cut], "dp", 2), swap(near[1][:, cut:], "dp", 1)]


def behind(values, others):
    return lax.optimization_barrier((values, others))[0]


def wide(value):
    return value.astype(jnp.float32)


def with_fourth(blocks, halves):
    own, one, two = blocks
    cut = cut_of(own)
    upper, lower = swap(halves[0], "dp", 2), swap(halves[1], "dp", 1)
    one = jnp.concatenate(
        [(wide(one[:, :cut]) + wide(upper)).astype(jnp.bfloat16), one[:, cut:]], 1
    )
    two = jnp.concatenate(
        [two[:, :cut], (wide(two[:, cut:]) + wide(lower)).astype(jnp.bfloat16)], 1
    )
    return [own, one, two]


def collected(blocks):
    total = wide(blocks[0])
    for k, block in enumerate(blocks[1:], 1):
        total = total + wide(swap(block, "dp", k))
    return total.astype(jnp.bfloat16)


def sums_kernel(layout, filling, *refs):
    widths, block_count, top_count = layout
    refs = list(refs)
    place = refs.pop(0)
    sides = [[[refs.pop(0) for _ in range(block_count)] for _ in widths] for _ in range(2)]
    if filling:
        up_hbm, down_hbm, keep_ref, give_ref, up, down, acc, hidden, sems = refs
    else:
        up, down, keep_ref, give_ref, acc, hidden = refs
    core, first_expert = place[0], place[1]
    per_device, width, both_width = up.shape
    half_width = both_width // 2
    part = width // 2
    bases = [core * part, (1 - core) * part]
    arrivals = {}
    if filling:
        copies = []
        for side in range(2):
            for low in range(0, part, CHUNK):
                for s in range(per_device):
                    at = pl.ds(pl.multiple_of(bases[side] + low, CHUNK), CHUNK)
                    copies.append((up_hbm.at[s, at], up.at[s, at], (side, low)))
        deep = down.shape[0]
        for low in range(0, deep, half_width):
            at = pl.ds(low, half_width)
            copies.append((down_hbm.at[at], down.at[at], "down"))
        for number, (source, target, key) in enumerate(copies):
            copy = pltpu.make_async_copy(source, target, sems.at[number])
            copy.start()
            arrivals.setdefault(key, []).append(copy)

    def arrive(key):
        for copy in arrivals.get(key, ()):
            copy.wait()

    acc[...] = jnp.zeros_like(acc)
    for side in range(2):
        offset = 0
        for blocks, seg_width in zip(sides[side], widths):
            for low in range(0, seg_width, CHUNK):
                arrive((side, offset + low))
                held = [block[:, low : low + CHUNK] for block in blocks]
                held = held[0] if len(held) == 1 else jnp.concatenate(held, 0)
                rows = pl.ds(pl.multiple_of(bases[side] + offset + low, CHUNK), CHUNK)
                for s in range(per_device):
                    acc[s] += jnp.dot(held, up[s, rows], preferred_element_type=jnp.float32)
            offset += seg_width

    last = widths[-1]
    meta = [block[:, last:].astype(jnp.float32) for block in sides[0][-1]]
    meta = meta[0] if len(meta) == 1 else jnp.concatenate(meta, 0)
    gates = sum(pltpu.roll(meta, LANES - k * top_count, 1) for k in (1, 2, 3))
    lanes = lax.broadcasted_iota(jnp.int32, meta.shape, 1)
    for s in range(per_device):
        chosen = (meta.astype(jnp.int32) == first_expert + s) & (lanes < top_count)
        own_gate = jnp.sum(jnp.where(chosen, gates, 0.0), 1, keepdims=True)
        gate_half, up_half = acc[s, :, :half_width], acc[s, :, half_width:]
        unit = gate_half * (1.0 / (1.0 + jnp.exp(-gate_half))) * up_half
        hidden[:, s * half_width : (s + 1) * half_width] = (unit * own_gate).astype(jnp.bfloat16)

    arrive("down")
    for base, out in ((bases[1], give_ref), (bases[0], keep_ref)):
        for low in range(0, part, CHUNK):
            columns = pl.ds(pl.multiple_of(base + low, CHUNK), CHUNK)
            out[:, low : low + CHUNK] = jnp.dot(
                hidden[...], down[:, columns], preferred_element_type=jnp.float32
            ).astype(jnp.bfloat16)


def gated_sums(place, top_count, own, other, up, down, filling):
    widths = tuple(segment[0].shape[1] for segment in other)
    block_count = len(own[0])
    count = sum(block.shape[0] for block in own[0])
    per_device, width, both_width = up.shape
    operands = [block for segments in (own, other) for segment in segments for block in segment]
    in_vmem = pl.BlockSpec(memory_space=pltpu.VMEM)
    operands = [pltpu.with_memory_space_constraint(x, pltpu.VMEM) for x in operands]
    out_shape = [pltpu.VMEM((count, width // 2), jnp.bfloat16)] * 2
    scratch = [
        pltpu.VMEM((per_device, count, both_width), jnp.float32),
        pltpu.VMEM((count, down.shape[0]), jnp.bfloat16),
    ]
    if filling:
        weights = [pltpu.with_memory_space_constraint(w, pltpu.HBM) for w in (up, down)]
        weight_specs = [pl.BlockSpec(memory_space=pl.ANY)] * 2
        out_shape += [pltpu.VMEM(up.shape, up.dtype), pltpu.VMEM(down.shape, down.dtype)]
        scratch += [pltpu.SemaphoreType.DMA((per_device * (width // CHUNK + 1),))]
        moved = up.nbytes + down.nbytes
    else:
        weights = [pltpu.with_memory_space_constraint(w, pltpu.VMEM) for w in (up, down)]
        weight_specs = [in_vmem] * 2
        moved = 0
    return pl.pallas_call(
        lambda *refs: sums_kernel((widths, block_count, top_count), filling, *refs),
        in_specs=[pl.BlockSpec(memory_space=pltpu.SMEM)]
        + [in_vmem] * len(operands)
        + weight_specs,
        out_specs=[in_vmem] * len(out_shape),
        out_shape=out_shape,
        scratch_shapes=scratch,
        compiler_params=pltpu.CompilerParams(vmem_limit_bytes=VMEM_LIMIT),
        cost_estimate=pl.CostEstimate(
            flops=2 * count * (up.size + down.size),
            bytes_accessed=moved,
            transcendentals=count * down.shape[0],
        ),
    )(place, *operands, *weights)


def first_kernel(place, *refs):
    sources, (keep_ref, give_ref, tokens, ids, gates, turned, sems) = refs[:3], refs[3:]
    copies = [
        pltpu.make_async_copy(source, target, sems.at[number])
        for number, (source, target) in enumerate(zip(sources, (tokens, ids, gates)))
    ]
    for copy in copies:
        copy.start()
    for copy in copies:
        copy.wait()
    core = place[0]
    part = tokens.shape[1] // 2
    top_count, rows = ids.shape
    turned[...] = jnp.zeros_like(turned)
    left = gates[...]
    parts = [ids[...].astype(jnp.float32)]
    for _ in range(3):
        parts.append(left.astype(jnp.bfloat16).astype(jnp.float32))
        left = left - parts[-1]
    for number, values in enumerate(parts):
        turned[number * top_count : (number + 1) * top_count, :rows] = values
    routing = turned[...].T[:rows].astype(jnp.bfloat16)
    for half, out in ((core, keep_ref), (1 - core, give_ref)):
        out[:, :part] = tokens[:, pl.ds(pl.multiple_of(half * part, LANES), part)]
        out[:, part:] = routing


def first_halves(place, tokens, expert_ids, gate_probs):
    rows, width = tokens.shape
    sources = [tokens, expert_ids.T, gate_probs.T]
    return pl.pallas_call(
        first_kernel,
        in_specs=[pl.BlockSpec(memory_space=pltpu.SMEM)]
        + [pl.BlockSpec(memory_space=pl.ANY)] * 3,
        out_specs=[pl.BlockSpec(memory_space=pltpu.VMEM)] * 2,
        out_shape=[pltpu.VMEM((rows, width // 2 + LANES), jnp.bfloat16)] * 2,
        scratch_shapes=[pltpu.VMEM(x.shape, x.dtype) for x in sources]
        + [pltpu.VMEM((LANES, LANES), jnp.float32), pltpu.SemaphoreType.DMA((3,))],
        compiler_params=pltpu.CompilerParams(vmem_limit_bytes=VMEM_LIMIT),
    )(place, *(pltpu.with_memory_space_constraint(x, pltpu.HBM) for x in sources))


def added_kernel(kept_ref, taken_ref, left_ref, right_ref):
    total = kept_ref[...].astype(jnp.float32) + taken_ref[...].astype(jnp.float32)
    cut = left_ref.shape[1]
    left_ref[...] = total[:, :cut].astype(jnp.bfloat16)
    right_ref[...] = total[:, cut:].astype(jnp.bfloat16)


def added(kept, taken, cut):
    in_vmem = pl.BlockSpec(memory_space=pltpu.VMEM)
    count, width = kept.shape
    return pl.pallas_call(
        added_kernel,
        in_specs=[in_vmem] * 2,
        out_specs=[in_vmem] * 2,
        out_shape=[
            pltpu.VMEM((count, cut), jnp.bfloat16),
            pltpu.VMEM((count, width - cut), jnp.bfloat16),
        ],
        compiler_params=pltpu.CompilerParams(vmem_limit_bytes=VMEM_LIMIT),
    )(*(pltpu.with_memory_space_constraint(x, pltpu.VMEM) for x in (kept, taken)))


def load_kernel(layout, swap_slot, *refs):
    owners, per_device, top_count, step, scale = layout
    *metas, load_ref = refs
    experts_all = owners * per_device
    high, low = [], []
    for meta in metas:
        values = meta[...].astype(jnp.float32)
        lanes = lax.broadcasted_iota(jnp.int32, values.shape, 1)
        gates = sum(pltpu.roll(values, LANES - k * top_count, 1) for k in (1, 2, 3))
        amounts = jnp.round(gates * step)
        upper = jnp.floor(amounts * (1.0 / PART))
        lower = amounts - upper * PART
        ids = jnp.where(lanes < top_count, values, -1.0)
        high.append([])
        low.append([])
        for e in range(experts_all):
            chosen = ids == e
            high[-1].append(jnp.sum(jnp.where(chosen, upper, 0.0), 0, keepdims=True))
            low[-1].append(jnp.sum(jnp.where(chosen, lower, 0.0), 0, keepdims=True))
    sums = []
    for part in (high, low):
        rows = [sum(block[e] for block in part) for e in range(experts_all)]
        sums.append(jnp.sum(jnp.concatenate(rows, 0), 1, keepdims=True))
    totals = (sums[0] * PART + sums[1]) * (1.0 / step)
    expert = lax.broadcasted_iota(jnp.int32, (experts_all, LANES), 0)
    owner = lax.broadcasted_iota(jnp.int32, (experts_all, LANES), 1)
    home = expert // per_device
    slot = jnp.zeros_like(home)
    for h in range(owners):
        slot = jnp.where(home == h, swap_slot[h], slot)
    partner = (home + owners // 2) % owners
    holder = jnp.where(expert % per_device == slot, partner, home)
    load_ref[...] = jnp.sum(jnp.where(holder == owner, totals, 0.0), 0, keepdims=True) * scale


def planned_load(metas, swap_slot, owners, per_device, top_count):
    count = sum(meta.shape[0] for meta in metas)
    step = 2.0 ** (31 - (count * GATE_MOST).bit_length())
    layout = (owners, per_device, top_count, step, owners / count)
    in_vmem = pl.BlockSpec(memory_space=pltpu.VMEM)
    load = pl.pallas_call(
        lambda *refs: load_kernel(layout, *refs),
        in_specs=[pl.BlockSpec(memory_space=pltpu.SMEM)] + [in_vmem] * len(metas),
        out_specs=in_vmem,
        out_shape=jax.ShapeDtypeStruct((1, LANES), jnp.float32),
        compiler_params=pltpu.CompilerParams(vmem_limit_bytes=VMEM_LIMIT),
    )(swap_slot, *metas)
    return load[0, :owners]


def on_device(tokens, expert_ids, gate_probs, in_weight, out_weight, swap_slot):
    groups, chips = lax.axis_size("dp"), lax.axis_size("chip")
    owners = 2 * chips
    near_chips = chips // 2
    per_device = in_weight.shape[0]
    rows, width = tokens.shape
    part = width // 2
    top_count = expert_ids.shape[1]
    half_width = out_weight.shape[1]
    core = lax.axis_index("core")
    first = core == 0
    first_expert = (lax.axis_index("chip") * 2 + core) * per_device
    place = jnp.stack([core, first_expert]).astype(jnp.int32)

    keep, give = first_halves(place, tokens, expert_ids, gate_probs)
    taken = swap(give, "core", 1)
    chip_rows = row_major(
        jnp.concatenate([jnp.where(first, keep, taken), jnp.where(first, taken, keep)], 0)
    )

    def sums_of(own, weights, filling=False):
        last = len(own) - 1
        bare = [
            [block[:, : block.shape[1] - (LANES if i == last else 0)] for block in segment]
            for i, segment in enumerate(own)
        ]
        other = [[swap(block, "core", 1) for block in segment] for segment in bare]
        keep, give, *filled = gated_sums(
            place, top_count, own, other, *weights, filling
        )
        return keep, give, filled or weights

    def chip_sums(keep, give):
        return (wide(keep) + wide(swap(give, "core", 1))).astype(jnp.bfloat16)

    chip_blocks = [chip_rows] + [swap(chip_rows, "chip", j) for j in range(1, chips)]
    direct = [swap(chip_rows, "dp", k) for k in range(1, groups)]
    far = row_major(jnp.concatenate(chip_blocks[1:], 0))
    held = row_major(jnp.concatenate([*chip_blocks, *direct], 0))
    near = spread_near(far)
    weights = (in_weight, out_weight.reshape(per_device * half_width, width))
    keep, give, weights = sums_of([[held]], weights, filling=True)
    near = behind(near, give)
    rest = spread_rest(near)
    first_sum = chip_sums(keep, give)
    own_sum = first_sum[: chips * 2 * rows]
    direct_sums = [
        first_sum[low : low + 2 * rows]
        for low in range(chips * 2 * rows, first_sum.shape[0], 2 * rows)
    ]
    if rest:
        near = row_major(jnp.concatenate(near, 0))
        keep, give, _ = sums_of([[near]], weights)
        pair = chip_sums(keep, give)
        sums = [pair[: far.shape[0]], pair[far.shape[0] :]]
        rest = behind(rest, give)
        keep, give, _ = sums_of([[half] for half in rest], weights)
        cut = rest[0].shape[1]
        diagonal = added(keep, swap(give, "core", 1), cut)
        diagonal = [
            jnp.concatenate([block, half], 0)
            for block, half in zip((direct_sums[2][:, :cut], direct_sums[2][:, cut:]), diagonal)
        ]
        sums = [jnp.concatenate([o, s], 0) for o, s in zip(direct_sums, sums)]
        sums = with_fourth([own_sum, *sums], diagonal)
        metas = [held, near, rest[1]]
    else:
        sums = [own_sum]
        for block, o in zip(near, direct_sums):
            keep, give, _ = sums_of([[block]], weights)
            sums += [jnp.concatenate([o, chip_sums(keep, give)], 0)]
        metas = [held, *near]
    metas = [block[:, block.shape[1] - LANES :] for block in metas]
    border = 2 * near_chips * rows
    total = collected([block[border:] for block in sums])
    blocks = [total[low : low + 2 * rows] for low in range(0, total.shape[0], 2 * rows)]
    total = collected(behind([block[:border] for block in sums], total))
    blocks = [total[low : low + 2 * rows] for low in range(0, border, 2 * rows)] + blocks
    total = wide(blocks[0])
    for j in range(1, chips):
        total = total + wide(swap(blocks[j], "chip", j))
    total = total.astype(jnp.bfloat16)
    upper, lower = total[:rows], total[rows:]
    arrived = swap(jnp.where(first, lower, upper), "core", 1)
    kept = jnp.where(first, upper, lower)
    mixed_out = row_major(
        jnp.concatenate([jnp.where(first, kept, arrived), jnp.where(first, arrived, kept)], 1)
    )

    owner_load = planned_load(metas, swap_slot, owners, per_device, top_count)
    return (mixed_out, owner_load)


def solution(mesh):
    groups, owners = mesh.devices.shape
    fine = Mesh(mesh.devices.reshape(groups, owners // 2, 2), ("dp", "chip", "core"))
    rows = P(("dp", "chip", "core"), None)
    return jax.shard_map(
        on_device,
        mesh=fine,
        in_specs=(
            rows,
            rows,
            rows,
            P(("chip", "core"), None, "dp"),
            P(("chip", "core"), "dp", None),
            P(),
        ),
        out_specs=(rows, P()),
        check_vma=False,
    )
```

```python
import jax
import jax.numpy as jnp
from jax import lax
from jax.experimental import pallas as pl
from jax.experimental.pallas import tpu as pltpu
from jax.experimental.layout import Layout, with_layout_constraint
from jax.sharding import Mesh, PartitionSpec as P

LANES = 128
PART = 1024.0
CHUNK = 1024
MOST_ROWS = 512
VMEM_LIMIT = 12 * 2**20
GATE_MOST = 5


def row_major(value):
    return with_layout_constraint(value, Layout(major_to_minor=tuple(range(value.ndim))))


def swap(value, axis, distance):
    size = lax.axis_size(axis)
    pairs = [(i, i ^ distance) for i in range(size)]
    return row_major(lax.ppermute(row_major(value), axis, pairs))


def behind(values, others):
    return lax.optimization_barrier((values, others))[0]


def wide(value):
    return value.astype(jnp.float32)


def collected(blocks):
    total = wide(blocks[0])
    for k, block in enumerate(blocks[1:], 1):
        total = total + wide(swap(block, "dp", k))
    return total.astype(jnp.bfloat16)


def sums_kernel(layout, filling, *refs):
    widths, block_count, top_count = layout
    refs = list(refs)
    place = refs.pop(0)
    sides = [[[refs.pop(0) for _ in range(block_count)] for _ in widths] for _ in range(2)]
    if filling:
        up_hbm, down_hbm, keep_ref, give_ref, up, down, acc, hidden, sems = refs
    else:
        up, down, keep_ref, give_ref, acc, hidden = refs
    core, first_expert = place[0], place[1]
    per_device, width, both_width = up.shape
    half_width = both_width // 2
    part = width // 2
    bases = [core * part, (1 - core) * part]
    arrivals = {}
    if filling:
        copies = []
        for side in range(2):
            for low in range(0, part, CHUNK):
                for s in range(per_device):
                    at = pl.ds(pl.multiple_of(bases[side] + low, CHUNK), CHUNK)
                    copies.append((up_hbm.at[s, at], up.at[s, at], (side, low)))
        deep = down.shape[0]
        for low in range(0, deep, half_width):
            at = pl.ds(low, half_width)
            copies.append((down_hbm.at[at], down.at[at], "down"))
        for number, (source, target, key) in enumerate(copies):
            copy = pltpu.make_async_copy(source, target, sems.at[number])
            copy.start()
            arrivals.setdefault(key, []).append(copy)

    def arrive(key):
        for copy in arrivals.get(key, ()):
            copy.wait()

    acc[...] = jnp.zeros_like(acc)
    for side in range(2):
        offset = 0
        for blocks, seg_width in zip(sides[side], widths):
            for low in range(0, seg_width, CHUNK):
                arrive((side, offset + low))
                held = [block[:, low : low + CHUNK] for block in blocks]
                held = held[0] if len(held) == 1 else jnp.concatenate(held, 0)
                rows = pl.ds(pl.multiple_of(bases[side] + offset + low, CHUNK), CHUNK)
                for s in range(per_device):
                    acc[s] += jnp.dot(held, up[s, rows], preferred_element_type=jnp.float32)
            offset += seg_width

    last = widths[-1]
    meta = [block[:, last:].astype(jnp.float32) for block in sides[0][-1]]
    meta = meta[0] if len(meta) == 1 else jnp.concatenate(meta, 0)
    gates = sum(pltpu.roll(meta, LANES - k * top_count, 1) for k in (1, 2, 3))
    lanes = lax.broadcasted_iota(jnp.int32, meta.shape, 1)
    for s in range(per_device):
        chosen = (meta.astype(jnp.int32) == first_expert + s) & (lanes < top_count)
        own_gate = jnp.sum(jnp.where(chosen, gates, 0.0), 1, keepdims=True)
        gate_half, up_half = acc[s, :, :half_width], acc[s, :, half_width:]
        unit = gate_half * (1.0 / (1.0 + jnp.exp(-gate_half))) * up_half
        hidden[:, s * half_width : (s + 1) * half_width] = (unit * own_gate).astype(jnp.bfloat16)

    arrive("down")
    for base, out in ((bases[1], give_ref), (bases[0], keep_ref)):
        for low in range(0, part, CHUNK):
            columns = pl.ds(pl.multiple_of(base + low, CHUNK), CHUNK)
            out[:, low : low + CHUNK] = jnp.dot(
                hidden[...], down[:, columns], preferred_element_type=jnp.float32
            ).astype(jnp.bfloat16)


def gated_sums(place, top_count, own, other, up, down, filling):
    widths = tuple(segment[0].shape[1] for segment in other)
    block_count = len(own[0])
    count = sum(block.shape[0] for block in own[0])
    per_device, width, both_width = up.shape
    operands = [block for segments in (own, other) for segment in segments for block in segment]
    in_vmem = pl.BlockSpec(memory_space=pltpu.VMEM)
    operands = [pltpu.with_memory_space_constraint(x, pltpu.VMEM) for x in operands]
    out_shape = [pltpu.VMEM((count, width // 2), jnp.bfloat16)] * 2
    scratch = [
        pltpu.VMEM((per_device, count, both_width), jnp.float32),
        pltpu.VMEM((count, down.shape[0]), jnp.bfloat16),
    ]
    if filling:
        weights = [pltpu.with_memory_space_constraint(w, pltpu.HBM) for w in (up, down)]
        weight_specs = [pl.BlockSpec(memory_space=pl.ANY)] * 2
        out_shape += [pltpu.VMEM(up.shape, up.dtype), pltpu.VMEM(down.shape, down.dtype)]
        scratch += [pltpu.SemaphoreType.DMA((per_device * (width // CHUNK + 1),))]
        moved = up.nbytes + down.nbytes
    else:
        weights = [pltpu.with_memory_space_constraint(w, pltpu.VMEM) for w in (up, down)]
        weight_specs = [in_vmem] * 2
        moved = 0
    return pl.pallas_call(
        lambda *refs: sums_kernel((widths, block_count, top_count), filling, *refs),
        in_specs=[pl.BlockSpec(memory_space=pltpu.SMEM)]
        + [in_vmem] * len(operands)
        + weight_specs,
        out_specs=[in_vmem] * len(out_shape),
        out_shape=out_shape,
        scratch_shapes=scratch,
        compiler_params=pltpu.CompilerParams(vmem_limit_bytes=VMEM_LIMIT),
        cost_estimate=pl.CostEstimate(
            flops=2 * count * (up.size + down.size),
            bytes_accessed=moved,
            transcendentals=count * down.shape[0],
        ),
    )(place, *operands, *weights)


def first_kernel(place, *refs):
    sources, (keep_ref, give_ref, tokens, ids, gates, turned, sems) = refs[:3], refs[3:]
    copies = [
        pltpu.make_async_copy(source, target, sems.at[number])
        for number, (source, target) in enumerate(zip(sources, (tokens, ids, gates)))
    ]
    for copy in copies:
        copy.start()
    for copy in copies:
        copy.wait()
    core = place[0]
    part = tokens.shape[1] // 2
    top_count, rows = ids.shape
    turned[...] = jnp.zeros_like(turned)
    left = gates[...]
    parts = [ids[...].astype(jnp.float32)]
    for _ in range(3):
        parts.append(left.astype(jnp.bfloat16).astype(jnp.float32))
        left = left - parts[-1]
    for number, values in enumerate(parts):
        turned[number * top_count : (number + 1) * top_count, :rows] = values
    routing = turned[...].T[:rows].astype(jnp.bfloat16)
    for half, out in ((core, keep_ref), (1 - core, give_ref)):
        out[:, :part] = tokens[:, pl.ds(pl.multiple_of(half * part, LANES), part)]
        out[:, part:] = routing


def first_halves(place, tokens, expert_ids, gate_probs):
    rows, width = tokens.shape
    sources = [tokens, expert_ids.T, gate_probs.T]
    return pl.pallas_call(
        first_kernel,
        in_specs=[pl.BlockSpec(memory_space=pltpu.SMEM)]
        + [pl.BlockSpec(memory_space=pl.ANY)] * 3,
        out_specs=[pl.BlockSpec(memory_space=pltpu.VMEM)] * 2,
        out_shape=[pltpu.VMEM((rows, width // 2 + LANES), jnp.bfloat16)] * 2,
        scratch_shapes=[pltpu.VMEM(x.shape, x.dtype) for x in sources]
        + [pltpu.VMEM((LANES, LANES), jnp.float32), pltpu.SemaphoreType.DMA((3,))],
        compiler_params=pltpu.CompilerParams(vmem_limit_bytes=VMEM_LIMIT),
    )(place, *(pltpu.with_memory_space_constraint(x, pltpu.HBM) for x in sources))


def added_kernel(kept_ref, taken_ref, *blocks):
    low = 0
    for block in blocks:
        rows = slice(low, low + block.shape[0])
        total = kept_ref[rows].astype(jnp.float32) + taken_ref[rows].astype(jnp.float32)
        block[...] = total.astype(jnp.bfloat16)
        low += block.shape[0]


def added(kept, taken, counts):
    in_vmem = pl.BlockSpec(memory_space=pltpu.VMEM)
    return pl.pallas_call(
        added_kernel,
        in_specs=[in_vmem] * 2,
        out_specs=[in_vmem] * len(counts),
        out_shape=[pltpu.VMEM((count, kept.shape[1]), jnp.bfloat16) for count in counts],
        compiler_params=pltpu.CompilerParams(vmem_limit_bytes=VMEM_LIMIT),
    )(*(pltpu.with_memory_space_constraint(x, pltpu.VMEM) for x in (kept, taken)))


def load_kernel(layout, swap_slot, *refs):
    owners, per_device, top_count, step, scale = layout
    *metas, load_ref = refs
    experts_all = owners * per_device
    high, low = [], []
    for meta in metas:
        values = meta[...].astype(jnp.float32)
        lanes = lax.broadcasted_iota(jnp.int32, values.shape, 1)
        gates = sum(pltpu.roll(values, LANES - k * top_count, 1) for k in (1, 2, 3))
        amounts = jnp.round(gates * step)
        upper = jnp.floor(amounts * (1.0 / PART))
        lower = amounts - upper * PART
        ids = jnp.where(lanes < top_count, values, -1.0)
        high.append([])
        low.append([])
        for e in range(experts_all):
            chosen = ids == e
            high[-1].append(jnp.sum(jnp.where(chosen, upper, 0.0), 0, keepdims=True))
            low[-1].append(jnp.sum(jnp.where(chosen, lower, 0.0), 0, keepdims=True))
    sums = []
    for part in (high, low):
        rows = [sum(block[e] for block in part) for e in range(experts_all)]
        sums.append(jnp.sum(jnp.concatenate(rows, 0), 1, keepdims=True))
    totals = (sums[0] * PART + sums[1]) * (1.0 / step)
    expert = lax.broadcasted_iota(jnp.int32, (experts_all, LANES), 0)
    owner = lax.broadcasted_iota(jnp.int32, (experts_all, LANES), 1)
    home = expert // per_device
    slot = jnp.zeros_like(home)
    for h in range(owners):
        slot = jnp.where(home == h, swap_slot[h], slot)
    partner = (home + owners // 2) % owners
    holder = jnp.where(expert % per_device == slot, partner, home)
    load_ref[...] = jnp.sum(jnp.where(holder == owner, totals, 0.0), 0, keepdims=True) * scale


def planned_load(metas, swap_slot, owners, per_device, top_count):
    count = sum(meta.shape[0] for meta in metas)
    step = 2.0 ** (31 - (count * GATE_MOST).bit_length())
    layout = (owners, per_device, top_count, step, owners / count)
    in_vmem = pl.BlockSpec(memory_space=pltpu.VMEM)
    load = pl.pallas_call(
        lambda *refs: load_kernel(layout, *refs),
        in_specs=[pl.BlockSpec(memory_space=pltpu.SMEM)] + [in_vmem] * len(metas),
        out_specs=in_vmem,
        out_shape=jax.ShapeDtypeStruct((1, LANES), jnp.float32),
        compiler_params=pltpu.CompilerParams(vmem_limit_bytes=VMEM_LIMIT),
    )(swap_slot, *metas)
    return load[0, :owners]


def on_device(tokens, expert_ids, gate_probs, in_weight, out_weight, swap_slot):
    groups, chips = lax.axis_size("dp"), lax.axis_size("chip")
    owners = 2 * chips
    near_chips = chips // 2
    per_device = in_weight.shape[0]
    rows, width = tokens.shape
    part = width // 2
    top_count = expert_ids.shape[1]
    half_width = out_weight.shape[1]
    core = lax.axis_index("core")
    first = core == 0
    first_expert = (lax.axis_index("chip") * 2 + core) * per_device
    place = jnp.stack([core, first_expert]).astype(jnp.int32)

    keep, give = first_halves(place, tokens, expert_ids, gate_probs)
    taken = swap(give, "core", 1)
    chip_rows = row_major(
        jnp.concatenate([jnp.where(first, keep, taken), jnp.where(first, taken, keep)], 0)
    )

    def sums_of(blocks, weights, filling=False):
        own = row_major(jnp.concatenate(blocks, 0))
        other = swap(own[:, :part], "core", 1)
        keep, give, *filled = gated_sums(
            place, top_count, [[own]], [[other]], *weights, filling
        )
        return keep, give, filled or weights

    def chip_sums(keep, give, blocks):
        return added(keep, swap(give, "core", 1), [block.shape[0] for block in blocks])

    chip_blocks = [chip_rows] + [swap(chip_rows, "chip", j) for j in range(1, chips)]
    low = [row_major(jnp.concatenate(chip_blocks[:near_chips], 0))]
    low += [swap(low[0], "dp", k) for k in range(1, groups)]
    high = [row_major(jnp.concatenate(chip_blocks[near_chips:], 0))]
    high += [swap(high[0], "dp", k) for k in range(1, groups)]
    sets = [[*low, high[0]], high[1:]]
    if sum(block.shape[0] for block in sets[0]) > MOST_ROWS:
        sets = [[block] for blocks in sets for block in blocks]
    weights = (in_weight, out_weight.reshape(per_device * half_width, width))
    sums, give = [], None
    for number, blocks in enumerate(sets):
        if number:
            blocks = behind(blocks, give)
        keep, give, weights = sums_of(blocks, weights, filling=number == 0)
        sums += chip_sums(keep, give, blocks)
    total = collected(sums[groups:])
    blocks = [total[at : at + 2 * rows] for at in range(0, total.shape[0], 2 * rows)]
    total = collected(behind(sums[:groups], total))
    blocks = [total[at : at + 2 * rows] for at in range(0, total.shape[0], 2 * rows)] + blocks
    metas = [block[:, part:] for block in low + high]
    total = wide(blocks[0])
    for j in range(1, chips):
        total = total + wide(swap(blocks[j], "chip", j))
    total = total.astype(jnp.bfloat16)
    upper, lower = total[:rows], total[rows:]
    arrived = swap(jnp.where(first, lower, upper), "core", 1)
    kept = jnp.where(first, upper, lower)
    mixed_out = row_major(
        jnp.concatenate([jnp.where(first, kept, arrived), jnp.where(first, arrived, kept)], 1)
    )

    owner_load = planned_load(metas, swap_slot, owners, per_device, top_count)
    return (mixed_out, owner_load)


def solution(mesh):
    groups, owners = mesh.devices.shape
    fine = Mesh(mesh.devices.reshape(groups, owners // 2, 2), ("dp", "chip", "core"))
    rows = P(("dp", "chip", "core"), None)
    return jax.shard_map(
        on_device,
        mesh=fine,
        in_specs=(
            rows,
            rows,
            rows,
            P(("chip", "core"), None, "dp"),
            P(("chip", "core"), "dp", None),
            P(),
        ),
        out_specs=(rows, P()),
        check_vma=False,
    )
```

```python
import jax
import jax.numpy as jnp
from jax import lax
from jax.experimental import pallas as pl
from jax.experimental.pallas import tpu as pltpu
from jax.experimental.layout import Layout, with_layout_constraint
from jax.sharding import Mesh, PartitionSpec as P

LANES = 128
PART = 1024.0
CHUNK = 1024
MOST_ROWS = 512
VMEM_LIMIT = 12 * 2**20
GATE_MOST = 5


def row_major(value):
    return with_layout_constraint(value, Layout(major_to_minor=tuple(range(value.ndim))))


def swap(value, axis, distance):
    size = lax.axis_size(axis)
    pairs = [(i, i ^ distance) for i in range(size)]
    return row_major(lax.ppermute(row_major(value), axis, pairs))


def cut_of(block):
    return block.shape[1] // (2 * LANES) * LANES


def spread_near(block):
    size = lax.axis_size("dp")
    return [swap(block, "dp", k) for k in range(1, 3 if size == 4 else size)]


def spread_rest(near):
    if lax.axis_size("dp") != 4:
        return []
    cut = cut_of(near[0])
    return [swap(near[0][:, :cut], "dp", 2), swap(near[1][:, cut:], "dp", 1)]


def behind(values, others):
    return lax.optimization_barrier((values, others))[0]


def wide(value):
    return value.astype(jnp.float32)


def with_fourth(blocks, halves):
    own, one, two = blocks
    cut = cut_of(own)
    upper, lower = swap(halves[0], "dp", 2), swap(halves[1], "dp", 1)
    one = jnp.concatenate(
        [(wide(one[:, :cut]) + wide(upper)).astype(jnp.bfloat16), one[:, cut:]], 1
    )
    two = jnp.concatenate(
        [two[:, :cut], (wide(two[:, cut:]) + wide(lower)).astype(jnp.bfloat16)], 1
    )
    return [own, one, two]


def collected(blocks):
    total = wide(blocks[0])
    for k, block in enumerate(blocks[1:], 1):
        total = total + wide(swap(block, "dp", k))
    return total.astype(jnp.bfloat16)


def load_weights_kernel(up_ref, down_ref, _, up_out, down_out, mark_ref, sems):
    copies = [
        pltpu.make_async_copy(up_ref, up_out, sems.at[0]),
        pltpu.make_async_copy(down_ref, down_out, sems.at[1]),
    ]
    for copy in copies:
        copy.start()
    mark_ref[...] = jnp.zeros_like(mark_ref)
    for copy in copies:
        copy.wait()


def loaded(up, down, after):
    return pl.pallas_call(
        load_weights_kernel,
        in_specs=[pl.BlockSpec(memory_space=pl.ANY)] * 3,
        out_specs=[pl.BlockSpec(memory_space=pltpu.VMEM)] * 3,
        out_shape=[
            pltpu.VMEM(up.shape, up.dtype),
            pltpu.VMEM(down.shape, down.dtype),
            pltpu.VMEM((8, LANES), jnp.float32),
        ],
        scratch_shapes=[pltpu.SemaphoreType.DMA((2,))],
        compiler_params=pltpu.CompilerParams(vmem_limit_bytes=VMEM_LIMIT),
        cost_estimate=pl.CostEstimate(
            flops=0, bytes_accessed=up.nbytes + down.nbytes, transcendentals=0
        ),
    )(*(pltpu.with_memory_space_constraint(x, pltpu.HBM) for x in (up, down)), after)


def joined(blocks):
    return blocks[0] if len(blocks) == 1 else jnp.concatenate(blocks, 0)


def add_up(acc, segments, widths, up, base):
    for blocks, width in zip(segments, widths):
        for low in range(0, width, CHUNK):
            held = joined([block[:, low : low + CHUNK] for block in blocks])
            rows = pl.ds(pl.multiple_of(base, CHUNK), CHUNK)
            for s in range(up.shape[0]):
                acc[s] += jnp.dot(held, up[s, rows], preferred_element_type=jnp.float32)
            base = base + CHUNK


def make_hidden(hidden, acc, routed, width, first_expert, top_count):
    meta = joined([block[:, width:].astype(jnp.float32) for block in routed])
    gates = sum(pltpu.roll(meta, LANES - k * top_count, 1) for k in (1, 2, 3))
    lanes = lax.broadcasted_iota(jnp.int32, meta.shape, 1)
    half_width = acc.shape[2] // 2
    for s in range(acc.shape[0]):
        chosen = (meta.astype(jnp.int32) == first_expert + s) & (lanes < top_count)
        own_gate = jnp.sum(jnp.where(chosen, gates, 0.0), 1, keepdims=True)
        gate_half, up_half = acc[s, :, :half_width], acc[s, :, half_width:]
        unit = gate_half * (1.0 / (1.0 + jnp.exp(-gate_half))) * up_half
        hidden[:, s * half_width : (s + 1) * half_width] = (unit * own_gate).astype(jnp.bfloat16)


def multiply_down(out, hidden, down, base):
    for low in range(0, out.shape[1], CHUNK):
        columns = pl.ds(pl.multiple_of(base + low, CHUNK), CHUNK)
        out[:, low : low + CHUNK] = jnp.dot(
            hidden[...], down[:, columns], preferred_element_type=jnp.float32
        ).astype(jnp.bfloat16)


def sums_kernel(top_count, place, own, other, up, down, mark, keep_ref, give_ref, acc, hidden):
    part = other.shape[1]
    bases = [place[0] * part, (1 - place[0]) * part]
    acc[...] = jnp.zeros_like(acc)
    add_up(acc, [[own]], [part], up, bases[0])
    add_up(acc, [[other]], [part], up, bases[1])
    make_hidden(hidden, acc, [own], part, place[1], top_count)
    multiply_down(give_ref, hidden, down, bases[1])
    multiply_down(keep_ref, hidden, down, bases[0])


def own_kernel(place, first, second, up, acc):
    cut = first.shape[1]
    acc[...] = jnp.zeros_like(acc)
    add_up(acc, [[first], [second]], [cut, cut], up, place[0] * 2 * cut)


def give_kernel(top_count, place, routed, first, second, held, up, down, give_ref, hidden, acc):
    cut = first.shape[1]
    base = (1 - place[0]) * 2 * cut
    acc[...] = held[...]
    add_up(acc, [[first], [second]], [cut, cut], up, base)
    make_hidden(hidden, acc, [routed], cut, place[1], top_count)
    multiply_down(give_ref, hidden, down, base)


def keep_kernel(place, hidden, down, keep_ref):
    multiply_down(keep_ref, hidden, down, place[0] * keep_ref.shape[1])


def call(kernel, operands, out_shape, scratch_shapes=(), flops=0, unplaced=0):
    in_vmem = pl.BlockSpec(memory_space=pltpu.VMEM)
    place, *arrays = operands
    split = len(arrays) - unplaced
    return pl.pallas_call(
        kernel,
        in_specs=[pl.BlockSpec(memory_space=pltpu.SMEM)]
        + [in_vmem] * split
        + [pl.BlockSpec(memory_space=pl.ANY)] * unplaced,
        out_specs=[in_vmem] * len(out_shape),
        out_shape=out_shape,
        scratch_shapes=list(scratch_shapes),
        compiler_params=pltpu.CompilerParams(vmem_limit_bytes=VMEM_LIMIT),
        cost_estimate=pl.CostEstimate(flops=flops, bytes_accessed=0, transcendentals=0),
    )(
        place,
        *(pltpu.with_memory_space_constraint(x, pltpu.VMEM) for x in arrays[:split]),
        *arrays[split:],
    )


def gated_sums(place, top_count, own, other, up, down, mark):
    count, part = other.shape
    out = pltpu.VMEM((count, part), jnp.bfloat16)
    return call(
        lambda *refs: sums_kernel(top_count, *refs),
        [place, own, other, up, down, mark],
        [out, out],
        [
            pltpu.VMEM((up.shape[0], count, up.shape[2]), jnp.float32),
            pltpu.VMEM((count, down.shape[0]), jnp.bfloat16),
        ],
        flops=2 * count * (up.size + down.size),
        unplaced=1,
    )


def gated_sums_in_halves(place, top_count, own, other, up, down):
    count, cut = own[0].shape
    acc_shape = (up.shape[0], count, up.shape[2])
    (held,) = call(
        own_kernel,
        [place, own[0], own[1][:, :cut], up],
        [pltpu.VMEM(acc_shape, jnp.float32)],
        flops=count * up.size,
    )
    give, hidden = call(
        lambda *refs: give_kernel(top_count, *refs),
        [place, own[1], *other, held, up, down],
        [
            pltpu.VMEM((count, 2 * cut), jnp.bfloat16),
            pltpu.VMEM((count, down.shape[0]), jnp.bfloat16),
        ],
        [pltpu.VMEM(acc_shape, jnp.float32)],
        flops=count * (up.size + down.size),
    )
    (keep,) = call(
        keep_kernel,
        [place, hidden, down],
        [pltpu.VMEM((count, 2 * cut), jnp.bfloat16)],
        flops=count * down.size,
    )
    return keep, give


def first_kernel(place, *refs):
    sources, (keep_ref, give_ref, tokens, ids, gates, turned, sems) = refs[:3], refs[3:]
    copies = [
        pltpu.make_async_copy(source, target, sems.at[number])
        for number, (source, target) in enumerate(zip(sources, (tokens, ids, gates)))
    ]
    for copy in copies:
        copy.start()
    for copy in copies:
        copy.wait()
    core = place[0]
    part = tokens.shape[1] // 2
    top_count, rows = ids.shape
    turned[...] = jnp.zeros_like(turned)
    left = gates[...]
    parts = [ids[...].astype(jnp.float32)]
    for _ in range(3):
        parts.append(left.astype(jnp.bfloat16).astype(jnp.float32))
        left = left - parts[-1]
    for number, values in enumerate(parts):
        turned[number * top_count : (number + 1) * top_count, :rows] = values
    routing = turned[...].T[:rows].astype(jnp.bfloat16)
    for half, out in ((core, keep_ref), (1 - core, give_ref)):
        out[:, :part] = tokens[:, pl.ds(pl.multiple_of(half * part, LANES), part)]
        out[:, part:] = routing


def first_halves(place, tokens, expert_ids, gate_probs):
    rows, width = tokens.shape
    sources = [tokens, expert_ids.T, gate_probs.T]
    return pl.pallas_call(
        first_kernel,
        in_specs=[pl.BlockSpec(memory_space=pltpu.SMEM)]
        + [pl.BlockSpec(memory_space=pl.ANY)] * 3,
        out_specs=[pl.BlockSpec(memory_space=pltpu.VMEM)] * 2,
        out_shape=[pltpu.VMEM((rows, width // 2 + LANES), jnp.bfloat16)] * 2,
        scratch_shapes=[pltpu.VMEM(x.shape, x.dtype) for x in sources]
        + [pltpu.VMEM((LANES, LANES), jnp.float32), pltpu.SemaphoreType.DMA((3,))],
        compiler_params=pltpu.CompilerParams(vmem_limit_bytes=VMEM_LIMIT),
    )(place, *(pltpu.with_memory_space_constraint(x, pltpu.HBM) for x in sources))


def added_kernel(kept_ref, taken_ref, left_ref, right_ref):
    total = kept_ref[...].astype(jnp.float32) + taken_ref[...].astype(jnp.float32)
    cut = left_ref.shape[1]
    left_ref[...] = total[:, :cut].astype(jnp.bfloat16)
    right_ref[...] = total[:, cut:].astype(jnp.bfloat16)


def added(kept, taken, cut):
    in_vmem = pl.BlockSpec(memory_space=pltpu.VMEM)
    count, width = kept.shape
    return pl.pallas_call(
        added_kernel,
        in_specs=[in_vmem] * 2,
        out_specs=[in_vmem] * 2,
        out_shape=[
            pltpu.VMEM((count, cut), jnp.bfloat16),
            pltpu.VMEM((count, width - cut), jnp.bfloat16),
        ],
        compiler_params=pltpu.CompilerParams(vmem_limit_bytes=VMEM_LIMIT),
    )(*(pltpu.with_memory_space_constraint(x, pltpu.VMEM) for x in (kept, taken)))


def load_kernel(layout, swap_slot, *refs):
    owners, per_device, top_count, step, scale = layout
    *metas, load_ref = refs
    experts_all = owners * per_device
    high, low = [], []
    for meta in metas:
        values = meta[...].astype(jnp.float32)
        lanes = lax.broadcasted_iota(jnp.int32, values.shape, 1)
        gates = sum(pltpu.roll(values, LANES - k * top_count, 1) for k in (1, 2, 3))
        amounts = jnp.round(gates * step)
        upper = jnp.floor(amounts * (1.0 / PART))
        lower = amounts - upper * PART
        ids = jnp.where(lanes < top_count, values, -1.0)
        high.append([])
        low.append([])
        for e in range(experts_all):
            chosen = ids == e
            high[-1].append(jnp.sum(jnp.where(chosen, upper, 0.0), 0, keepdims=True))
            low[-1].append(jnp.sum(jnp.where(chosen, lower, 0.0), 0, keepdims=True))
    sums = []
    for part in (high, low):
        rows = [sum(block[e] for block in part) for e in range(experts_all)]
        sums.append(jnp.sum(jnp.concatenate(rows, 0), 1, keepdims=True))
    totals = (sums[0] * PART + sums[1]) * (1.0 / step)
    expert = lax.broadcasted_iota(jnp.int32, (experts_all, LANES), 0)
    owner = lax.broadcasted_iota(jnp.int32, (experts_all, LANES), 1)
    home = expert // per_device
    slot = jnp.zeros_like(home)
    for h in range(owners):
        slot = jnp.where(home == h, swap_slot[h], slot)
    partner = (home + owners // 2) % owners
    holder = jnp.where(expert % per_device == slot, partner, home)
    load_ref[...] = jnp.sum(jnp.where(holder == owner, totals, 0.0), 0, keepdims=True) * scale


def planned_load(metas, swap_slot, owners, per_device, top_count):
    count = sum(meta.shape[0] for meta in metas)
    step = 2.0 ** (31 - (count * GATE_MOST).bit_length())
    layout = (owners, per_device, top_count, step, owners / count)
    in_vmem = pl.BlockSpec(memory_space=pltpu.VMEM)
    load = pl.pallas_call(
        lambda *refs: load_kernel(layout, *refs),
        in_specs=[pl.BlockSpec(memory_space=pltpu.SMEM)] + [in_vmem] * len(metas),
        out_specs=in_vmem,
        out_shape=jax.ShapeDtypeStruct((1, LANES), jnp.float32),
        compiler_params=pltpu.CompilerParams(vmem_limit_bytes=VMEM_LIMIT),
    )(swap_slot, *metas)
    return load[0, :owners]


def on_device(tokens, expert_ids, gate_probs, in_weight, out_weight, swap_slot):
    groups, chips = lax.axis_size("dp"), lax.axis_size("chip")
    owners = 2 * chips
    near_chips = chips // 2
    per_device = in_weight.shape[0]
    rows, width = tokens.shape
    part = width // 2
    top_count = expert_ids.shape[1]
    half_width = out_weight.shape[1]
    core = lax.axis_index("core")
    first = core == 0
    first_expert = (lax.axis_index("chip") * 2 + core) * per_device
    place = jnp.stack([core, first_expert]).astype(jnp.int32)

    keep, give = first_halves(place, tokens, expert_ids, gate_probs)
    taken = swap(give, "core", 1)
    chip_rows = row_major(
        jnp.concatenate([jnp.where(first, keep, taken), jnp.where(first, taken, keep)], 0)
    )

    def sums_of(own):
        other = swap(own[:, :part], "core", 1)
        return gated_sums(place, top_count, own, other, *weights, mark)

    def chip_sums(keep, give):
        return (wide(keep) + wide(swap(give, "core", 1))).astype(jnp.bfloat16)

    chip_blocks = [chip_rows] + [swap(chip_rows, "chip", j) for j in range(1, chips)]
    direct = [swap(chip_rows, "dp", k) for k in range(1, groups)]
    *weights, mark = loaded(
        in_weight, out_weight.reshape(per_device * half_width, width), chip_blocks[1]
    )
    chip_blocks[1:], mark = lax.optimization_barrier((chip_blocks[1:], mark))
    far = row_major(jnp.concatenate(chip_blocks[1:], 0))
    held = row_major(jnp.concatenate([*chip_blocks, *direct], 0))
    near = spread_near(far)
    if held.shape[0] > MOST_ROWS:
        pieces = [sums_of(block) for block in (jnp.concatenate(chip_blocks, 0), *direct)]
        keep, give = (jnp.concatenate(piece, 0) for piece in zip(*pieces))
    else:
        keep, give = sums_of(held)
    near = behind(near, give)
    rest = spread_rest(near)
    first_sum = chip_sums(keep, give)
    own_sum = first_sum[: chips * 2 * rows]
    direct_sums = [
        first_sum[low : low + 2 * rows]
        for low in range(chips * 2 * rows, first_sum.shape[0], 2 * rows)
    ]
    if rest:
        near = row_major(jnp.concatenate(near, 0))
        keep, give = sums_of(near)
        pair = chip_sums(keep, give)
        sums = [pair[: far.shape[0]], pair[far.shape[0] :]]
        rest = behind(rest, give)
        cut = rest[0].shape[1]
        other = [swap(half[:, :cut], "core", 1) for half in rest]
        keep, give = gated_sums_in_halves(place, top_count, rest, other, *weights)
        diagonal = added(keep, swap(give, "core", 1), cut)
        diagonal = [
            jnp.concatenate([block, half], 0)
            for block, half in zip((direct_sums[2][:, :cut], direct_sums[2][:, cut:]), diagonal)
        ]
        sums = [jnp.concatenate([o, s], 0) for o, s in zip(direct_sums, sums)]
        sums = with_fourth([own_sum, *sums], diagonal)
        metas = [held, near, rest[1]]
    else:
        sums = [own_sum]
        for block, o in zip(near, direct_sums):
            keep, give = sums_of(block)
            sums += [jnp.concatenate([o, chip_sums(keep, give)], 0)]
        metas = [held, *near]
    metas = [block[:, block.shape[1] - LANES :] for block in metas]
    border = 2 * near_chips * rows
    total = collected([block[border:] for block in sums])
    blocks = [total[low : low + 2 * rows] for low in range(0, total.shape[0], 2 * rows)]
    total = collected(behind([block[:border] for block in sums], total))
    blocks = [total[low : low + 2 * rows] for low in range(0, border, 2 * rows)] + blocks
    total = wide(blocks[0])
    for j in range(1, chips):
        total = total + wide(swap(blocks[j], "chip", j))
    total = total.astype(jnp.bfloat16)
    upper, lower = total[:rows], total[rows:]
    arrived = swap(jnp.where(first, lower, upper), "core", 1)
    kept = jnp.where(first, upper, lower)
    mixed_out = row_major(
        jnp.concatenate([jnp.where(first, kept, arrived), jnp.where(first, arrived, kept)], 1)
    )

    owner_load = planned_load(metas, swap_slot, owners, per_device, top_count)
    return (mixed_out, owner_load)


def solution(mesh):
    groups, owners = mesh.devices.shape
    fine = Mesh(mesh.devices.reshape(groups, owners // 2, 2), ("dp", "chip", "core"))
    rows = P(("dp", "chip", "core"), None)
    return jax.shard_map(
        on_device,
        mesh=fine,
        in_specs=(
            rows,
            rows,
            rows,
            P(("chip", "core"), None, "dp"),
            P(("chip", "core"), "dp", None),
            P(),
        ),
        out_specs=(rows, P()),
        check_vma=False,
    )
```

```python
import jax
import jax.numpy as jnp
from jax import lax
from jax.experimental import pallas as pl
from jax.experimental.pallas import tpu as pltpu
from jax.experimental.layout import Layout, with_layout_constraint
from jax.sharding import Mesh, PartitionSpec as P

LANES = 128
PART = 1024.0
CHUNK = 1024
MOST_ROWS = 512
VMEM_LIMIT = 12 * 2**20
GATE_MOST = 5


def row_major(value):
    return with_layout_constraint(value, Layout(major_to_minor=tuple(range(value.ndim))))


def swap(value, axis, distance):
    size = lax.axis_size(axis)
    pairs = [(i, i ^ distance) for i in range(size)]
    return row_major(lax.ppermute(row_major(value), axis, pairs))


def cut_of(block):
    return block.shape[1] // (2 * LANES) * LANES


def spread_near(block):
    size = lax.axis_size("dp")
    return [swap(block, "dp", k) for k in range(1, 3 if size == 4 else size)]


def spread_rest(near):
    if lax.axis_size("dp") != 4:
        return []
    cut = cut_of(near[0])
    return [swap(near[0][:, :cut], "dp", 2), swap(near[1][:, cut:], "dp", 1)]


def behind(values, others):
    return lax.optimization_barrier((values, others))[0]


def wide(value):
    return value.astype(jnp.float32)


def with_fourth(blocks, halves):
    own, one, two = blocks
    cut = cut_of(own)
    upper, lower = swap(halves[0], "dp", 2), swap(halves[1], "dp", 1)
    one = jnp.concatenate(
        [(wide(one[:, :cut]) + wide(upper)).astype(jnp.bfloat16), one[:, cut:]], 1
    )
    two = jnp.concatenate(
        [two[:, :cut], (wide(two[:, cut:]) + wide(lower)).astype(jnp.bfloat16)], 1
    )
    return [own, one, two]


def received(blocks):
    return [swap(block, "dp", k) for k, block in enumerate(blocks[1:], 1)]


def collected(own, others):
    return sum([wide(block) for block in others], wide(own)).astype(jnp.bfloat16)


def load_weight_kernel(weight_ref, _, weight_out, mark_ref, sem):
    copy = pltpu.make_async_copy(weight_ref, weight_out, sem)
    copy.start()
    mark_ref[...] = jnp.zeros_like(mark_ref)
    copy.wait()


def loaded(weight, after):
    return pl.pallas_call(
        load_weight_kernel,
        in_specs=[pl.BlockSpec(memory_space=pl.ANY)] * 2,
        out_specs=[pl.BlockSpec(memory_space=pltpu.VMEM)] * 2,
        out_shape=[
            pltpu.VMEM(weight.shape, weight.dtype),
            pltpu.VMEM((8, LANES), jnp.float32),
        ],
        scratch_shapes=[pltpu.SemaphoreType.DMA],
        compiler_params=pltpu.CompilerParams(vmem_limit_bytes=VMEM_LIMIT),
        cost_estimate=pl.CostEstimate(flops=0, bytes_accessed=weight.nbytes, transcendentals=0),
    )(pltpu.with_memory_space_constraint(weight, pltpu.HBM), after)


def joined(blocks):
    return blocks[0] if len(blocks) == 1 else jnp.concatenate(blocks, 0)


def add_up(acc, segments, widths, up, base):
    for blocks, width in zip(segments, widths):
        for low in range(0, width, CHUNK):
            held = joined([block[:, low : low + CHUNK] for block in blocks])
            rows = pl.ds(pl.multiple_of(base, CHUNK), CHUNK)
            for s in range(up.shape[0]):
                acc[s] += jnp.dot(held, up[s, rows], preferred_element_type=jnp.float32)
            base = base + CHUNK


def make_hidden(hidden, acc, routed, width, first_expert, top_count):
    meta = joined([block[:, width:].astype(jnp.float32) for block in routed])
    gates = sum(pltpu.roll(meta, LANES - k * top_count, 1) for k in (1, 2, 3))
    lanes = lax.broadcasted_iota(jnp.int32, meta.shape, 1)
    half_width = acc.shape[2] // 2
    for s in range(acc.shape[0]):
        chosen = (meta.astype(jnp.int32) == first_expert + s) & (lanes < top_count)
        own_gate = jnp.sum(jnp.where(chosen, gates, 0.0), 1, keepdims=True)
        gate_half, up_half = acc[s, :, :half_width], acc[s, :, half_width:]
        unit = gate_half * (1.0 / (1.0 + jnp.exp(-gate_half))) * up_half
        hidden[:, s * half_width : (s + 1) * half_width] = (unit * own_gate).astype(jnp.bfloat16)


def multiply_down(out, hidden, down, base):
    for low in range(0, out.shape[1], CHUNK):
        columns = pl.ds(pl.multiple_of(base + low, CHUNK), CHUNK)
        out[:, low : low + CHUNK] = jnp.dot(
            hidden[...], down[:, columns], preferred_element_type=jnp.float32
        ).astype(jnp.bfloat16)


def sums_kernel(top_count, filling, place, own, other, up, *refs):
    if filling:
        down_ref, _, keep_ref, give_ref, down, acc, hidden, sem = refs
        copy = pltpu.make_async_copy(down_ref, down, sem)
        copy.start()
    else:
        down, keep_ref, give_ref, acc, hidden = refs
    part = other.shape[1]
    bases = [place[0] * part, (1 - place[0]) * part]
    acc[...] = jnp.zeros_like(acc)
    add_up(acc, [[own]], [part], up, bases[0])
    add_up(acc, [[other]], [part], up, bases[1])
    make_hidden(hidden, acc, [own], part, place[1], top_count)
    if filling:
        copy.wait()
    multiply_down(give_ref, hidden, down, bases[1])
    multiply_down(keep_ref, hidden, down, bases[0])


def own_kernel(place, first, second, up, acc):
    cut = first.shape[1]
    acc[...] = jnp.zeros_like(acc)
    add_up(acc, [[first], [second]], [cut, cut], up, place[0] * 2 * cut)


def give_kernel(top_count, place, routed, first, second, held, up, down, give_ref, hidden, acc):
    cut = first.shape[1]
    base = (1 - place[0]) * 2 * cut
    acc[...] = held[...]
    add_up(acc, [[first], [second]], [cut, cut], up, base)
    make_hidden(hidden, acc, [routed], cut, place[1], top_count)
    multiply_down(give_ref, hidden, down, base)


def keep_kernel(place, hidden, down, keep_ref):
    multiply_down(keep_ref, hidden, down, place[0] * keep_ref.shape[1])


def call(kernel, operands, out_shape, scratch_shapes=(), flops=0, unplaced=0):
    in_vmem = pl.BlockSpec(memory_space=pltpu.VMEM)
    place, *arrays = operands
    split = len(arrays) - unplaced
    return pl.pallas_call(
        kernel,
        in_specs=[pl.BlockSpec(memory_space=pltpu.SMEM)]
        + [in_vmem] * split
        + [pl.BlockSpec(memory_space=pl.ANY)] * unplaced,
        out_specs=[in_vmem] * len(out_shape),
        out_shape=out_shape,
        scratch_shapes=list(scratch_shapes),
        compiler_params=pltpu.CompilerParams(vmem_limit_bytes=VMEM_LIMIT),
        cost_estimate=pl.CostEstimate(flops=flops, bytes_accessed=0, transcendentals=0),
    )(
        place,
        *(pltpu.with_memory_space_constraint(x, pltpu.VMEM) for x in arrays[:split]),
        *arrays[split:],
    )


def gated_sums(place, top_count, own, other, up, down, mark=None):
    count, part = other.shape
    filling = mark is not None
    out = pltpu.VMEM((count, part), jnp.bfloat16)
    out_shape = [out, out]
    scratch = [
        pltpu.VMEM((up.shape[0], count, up.shape[2]), jnp.float32),
        pltpu.VMEM((count, down.shape[0]), jnp.bfloat16),
    ]
    operands = [place, own, other, up, down]
    if filling:
        operands[-1:] = [pltpu.with_memory_space_constraint(down, pltpu.HBM), mark]
        out_shape.append(pltpu.VMEM(down.shape, down.dtype))
        scratch.append(pltpu.SemaphoreType.DMA)
    return call(
        lambda *refs: sums_kernel(top_count, filling, *refs),
        operands,
        out_shape,
        scratch,
        flops=2 * count * (up.size + down.size),
        unplaced=2 if filling else 0,
    )


def gated_sums_in_halves(place, top_count, own, other, up, down):
    count, cut = own[0].shape
    acc_shape = (up.shape[0], count, up.shape[2])
    (held,) = call(
        own_kernel,
        [place, own[0], own[1][:, :cut], up],
        [pltpu.VMEM(acc_shape, jnp.float32)],
        flops=count * up.size,
    )
    give, hidden = call(
        lambda *refs: give_kernel(top_count, *refs),
        [place, own[1], *other, held, up, down],
        [
            pltpu.VMEM((count, 2 * cut), jnp.bfloat16),
            pltpu.VMEM((count, down.shape[0]), jnp.bfloat16),
        ],
        [pltpu.VMEM(acc_shape, jnp.float32)],
        flops=count * (up.size + down.size),
    )
    (keep,) = call(
        keep_kernel,
        [place, hidden, down],
        [pltpu.VMEM((count, 2 * cut), jnp.bfloat16)],
        flops=count * down.size,
    )
    return keep, give


def first_kernel(place, *refs):
    sources, (keep_ref, give_ref, tokens, ids, gates, turned, sems) = refs[:3], refs[3:]
    copies = [
        pltpu.make_async_copy(source, target, sems.at[number])
        for number, (source, target) in enumerate(zip(sources, (tokens, ids, gates)))
    ]
    for copy in copies:
        copy.start()
    for copy in copies:
        copy.wait()
    core = place[0]
    part = tokens.shape[1] // 2
    top_count, rows = ids.shape
    turned[...] = jnp.zeros_like(turned)
    left = gates[...]
    parts = [ids[...].astype(jnp.float32)]
    for _ in range(3):
        parts.append(left.astype(jnp.bfloat16).astype(jnp.float32))
        left = left - parts[-1]
    for number, values in enumerate(parts):
        turned[number * top_count : (number + 1) * top_count, :rows] = values
    routing = turned[...].T[:rows].astype(jnp.bfloat16)
    for half, out in ((core, keep_ref), (1 - core, give_ref)):
        out[:, :part] = tokens[:, pl.ds(pl.multiple_of(half * part, LANES), part)]
        out[:, part:] = routing


def first_halves(place, tokens, expert_ids, gate_probs):
    rows, width = tokens.shape
    sources = [tokens, expert_ids.T, gate_probs.T]
    return pl.pallas_call(
        first_kernel,
        in_specs=[pl.BlockSpec(memory_space=pltpu.SMEM)]
        + [pl.BlockSpec(memory_space=pl.ANY)] * 3,
        out_specs=[pl.BlockSpec(memory_space=pltpu.VMEM)] * 2,
        out_shape=[pltpu.VMEM((rows, width // 2 + LANES), jnp.bfloat16)] * 2,
        scratch_shapes=[pltpu.VMEM(x.shape, x.dtype) for x in sources]
        + [pltpu.VMEM((LANES, LANES), jnp.float32), pltpu.SemaphoreType.DMA((3,))],
        compiler_params=pltpu.CompilerParams(vmem_limit_bytes=VMEM_LIMIT),
    )(place, *(pltpu.with_memory_space_constraint(x, pltpu.HBM) for x in sources))


def added_kernel(kept_ref, taken_ref, left_ref, right_ref):
    total = kept_ref[...].astype(jnp.float32) + taken_ref[...].astype(jnp.float32)
    cut = left_ref.shape[1]
    left_ref[...] = total[:, :cut].astype(jnp.bfloat16)
    right_ref[...] = total[:, cut:].astype(jnp.bfloat16)


def added(kept, taken, cut):
    in_vmem = pl.BlockSpec(memory_space=pltpu.VMEM)
    count, width = kept.shape
    return pl.pallas_call(
        added_kernel,
        in_specs=[in_vmem] * 2,
        out_specs=[in_vmem] * 2,
        out_shape=[
            pltpu.VMEM((count, cut), jnp.bfloat16),
            pltpu.VMEM((count, width - cut), jnp.bfloat16),
        ],
        compiler_params=pltpu.CompilerParams(vmem_limit_bytes=VMEM_LIMIT),
    )(*(pltpu.with_memory_space_constraint(x, pltpu.VMEM) for x in (kept, taken)))


def load_kernel(layout, swap_slot, *refs):
    owners, per_device, top_count, step, scale = layout
    *metas, _, load_ref = refs
    experts_all = owners * per_device
    high, low = [], []
    for meta in metas:
        values = meta[...].astype(jnp.float32)
        lanes = lax.broadcasted_iota(jnp.int32, values.shape, 1)
        gates = sum(pltpu.roll(values, LANES - k * top_count, 1) for k in (1, 2, 3))
        amounts = jnp.round(gates * step)
        upper = jnp.floor(amounts * (1.0 / PART))
        lower = amounts - upper * PART
        ids = jnp.where(lanes < top_count, values, -1.0)
        high.append([])
        low.append([])
        for e in range(experts_all):
            chosen = ids == e
            high[-1].append(jnp.sum(jnp.where(chosen, upper, 0.0), 0, keepdims=True))
            low[-1].append(jnp.sum(jnp.where(chosen, lower, 0.0), 0, keepdims=True))
    sums = []
    for part in (high, low):
        rows = [sum(block[e] for block in part) for e in range(experts_all)]
        sums.append(jnp.sum(jnp.concatenate(rows, 0), 1, keepdims=True))
    totals = (sums[0] * PART + sums[1]) * (1.0 / step)
    expert = lax.broadcasted_iota(jnp.int32, (experts_all, LANES), 0)
    owner = lax.broadcasted_iota(jnp.int32, (experts_all, LANES), 1)
    home = expert // per_device
    slot = jnp.zeros_like(home)
    for h in range(owners):
        slot = jnp.where(home == h, swap_slot[h], slot)
    partner = (home + owners // 2) % owners
    holder = jnp.where(expert % per_device == slot, partner, home)
    load_ref[...] = jnp.sum(jnp.where(holder == owner, totals, 0.0), 0, keepdims=True) * scale


def planned_load(metas, swap_slot, owners, per_device, top_count, after):
    count = sum(meta.shape[0] for meta in metas)
    step = 2.0 ** (31 - (count * GATE_MOST).bit_length())
    layout = (owners, per_device, top_count, step, owners / count)
    in_vmem = pl.BlockSpec(memory_space=pltpu.VMEM)
    load = pl.pallas_call(
        lambda *refs: load_kernel(layout, *refs),
        in_specs=[pl.BlockSpec(memory_space=pltpu.SMEM)]
        + [in_vmem] * len(metas)
        + [pl.BlockSpec(memory_space=pl.ANY)],
        out_specs=in_vmem,
        out_shape=jax.ShapeDtypeStruct((1, LANES), jnp.float32),
        compiler_params=pltpu.CompilerParams(vmem_limit_bytes=VMEM_LIMIT),
        cost_estimate=pl.CostEstimate(
            flops=0, bytes_accessed=sum(meta.nbytes for meta in metas), transcendentals=0
        ),
    )(swap_slot, *metas, after)
    return load


def on_device(tokens, expert_ids, gate_probs, in_weight, out_weight, swap_slot):
    groups, chips = lax.axis_size("dp"), lax.axis_size("chip")
    owners = 2 * chips
    near_chips = chips // 2
    per_device = in_weight.shape[0]
    rows, width = tokens.shape
    part = width // 2
    top_count = expert_ids.shape[1]
    half_width = out_weight.shape[1]
    core = lax.axis_index("core")
    first = core == 0
    first_expert = (lax.axis_index("chip") * 2 + core) * per_device
    place = jnp.stack([core, first_expert]).astype(jnp.int32)

    keep, give = first_halves(place, tokens, expert_ids, gate_probs)
    taken = swap(give, "core", 1)
    chip_rows = row_major(
        jnp.concatenate([jnp.where(first, keep, taken), jnp.where(first, taken, keep)], 0)
    )

    def sums_of(own, weights, *mark):
        other = swap(own[:, :part], "core", 1)
        return gated_sums(place, top_count, own, other, *weights, *mark)

    def chip_sums(keep, give):
        return (wide(keep) + wide(swap(give, "core", 1))).astype(jnp.bfloat16)

    chip_blocks = [chip_rows] + [swap(chip_rows, "chip", j) for j in range(1, chips)]
    direct = [swap(chip_rows, "dp", k) for k in range(1, groups)]
    up, mark = loaded(in_weight, chip_blocks[1])
    chip_blocks[1:], mark = lax.optimization_barrier((chip_blocks[1:], mark))
    far = row_major(jnp.concatenate(chip_blocks[1:], 0))
    held = row_major(jnp.concatenate([*chip_blocks, *direct], 0))
    near = spread_near(far)
    weights = [up, out_weight.reshape(per_device * half_width, width)]
    pieces = [held]
    if held.shape[0] > MOST_ROWS:
        pieces = [row_major(jnp.concatenate(chip_blocks, 0)), *direct]
    keep, give, weights[1] = sums_of(pieces[0], weights, mark)
    later = [sums_of(piece, weights) for piece in pieces[1:]]
    if later:
        keep, give = (jnp.concatenate(x, 0) for x in zip((keep, give), *later))
    first_sum = chip_sums(keep, give)
    near = behind(near, give)
    rest = spread_rest(near)
    own_sum = first_sum[: chips * 2 * rows]
    direct_sums = [
        first_sum[low : low + 2 * rows]
        for low in range(chips * 2 * rows, first_sum.shape[0], 2 * rows)
    ]
    if rest:
        near = row_major(jnp.concatenate(near, 0))
        keep, give = sums_of(near, weights)
        pair = chip_sums(keep, give)
        sums = [pair[: far.shape[0]], pair[far.shape[0] :]]
        rest = behind(rest, give)
        cut = rest[0].shape[1]
        other = [swap(half[:, :cut], "core", 1) for half in rest]
        keep, give = gated_sums_in_halves(place, top_count, rest, other, *weights)
        diagonal = added(keep, swap(give, "core", 1), cut)
        diagonal = [
            jnp.concatenate([block, half], 0)
            for block, half in zip((direct_sums[2][:, :cut], direct_sums[2][:, cut:]), diagonal)
        ]
        sums = [jnp.concatenate([o, s], 0) for o, s in zip(direct_sums, sums)]
        sums = with_fourth([own_sum, *sums], diagonal)
        metas = [held, near, rest[1]]
    else:
        sums = [own_sum]
        for block, o in zip(near, direct_sums):
            keep, give = sums_of(block, weights)
            sums += [jnp.concatenate([o, chip_sums(keep, give)], 0)]
        metas = [held, *near]
    metas = [block[:, block.shape[1] - LANES :] for block in metas]
    border = 2 * near_chips * rows
    high = [block[border:] for block in sums]
    low = [block[:border] for block in sums]
    total = collected(high[0], received(high))
    blocks = [total[at : at + 2 * rows] for at in range(0, total.shape[0], 2 * rows)]
    load = planned_load(metas, swap_slot, owners, per_device, top_count, blocks[0])
    low = behind(low, total)
    total = collected(low[0], received(low))
    blocks = [total[at : at + 2 * rows] for at in range(0, border, 2 * rows)] + blocks
    total = wide(blocks[0])
    for j in range(1, chips):
        total = total + wide(swap(blocks[j], "chip", j))
    total = total.astype(jnp.bfloat16)
    upper, lower = total[:rows], total[rows:]
    arrived = swap(jnp.where(first, lower, upper), "core", 1)
    kept = jnp.where(first, upper, lower)
    mixed_out = row_major(
        jnp.concatenate([jnp.where(first, kept, arrived), jnp.where(first, arrived, kept)], 1)
    )

    return (mixed_out, load[0, :owners])


def solution(mesh):
    groups, owners = mesh.devices.shape
    fine = Mesh(mesh.devices.reshape(groups, owners // 2, 2), ("dp", "chip", "core"))
    rows = P(("dp", "chip", "core"), None)
    return jax.shard_map(
        on_device,
        mesh=fine,
        in_specs=(
            rows,
            rows,
            rows,
            P(("chip", "core"), None, "dp"),
            P(("chip", "core"), "dp", None),
            P(),
        ),
        out_specs=(rows, P()),
        check_vma=False,
    )
```

```python
import jax
import jax.numpy as jnp
from jax import lax
from jax.experimental import pallas as pl
from jax.experimental.pallas import tpu as pltpu
from jax.experimental.layout import Layout, with_layout_constraint
from jax.sharding import Mesh, PartitionSpec as P

LANES = 128
PART = 1024.0
CHUNK = 1024
MOST_ROWS = 512
VMEM_LIMIT = 12 * 2**20
GATE_MOST = 5


def row_major(value):
    return with_layout_constraint(value, Layout(major_to_minor=tuple(range(value.ndim))))


def swap(value, axis, distance):
    size = lax.axis_size(axis)
    pairs = [(i, i ^ distance) for i in range(size)]
    return row_major(lax.ppermute(row_major(value), axis, pairs))


def spread_near(block):
    size = lax.axis_size("dp")
    return [swap(block, "dp", k) for k in range(1, 3 if size == 4 else size)]


def cross(value):
    pairs = []
    for i in range(4):
        pairs += [(2 * i, 2 * (i ^ 2)), (2 * i + 1, 2 * (i ^ 1) + 1)]
    return row_major(lax.ppermute(row_major(value), ("dp", "core"), pairs))


def behind(values, others):
    return lax.optimization_barrier((values, others))[0]


def wide(value):
    return value.astype(jnp.float32)


def with_fourth(one, two, fourth, first):
    came = wide(cross(fourth))
    return (
        jnp.where(first, wide(one) + came, wide(one)).astype(jnp.bfloat16),
        jnp.where(first, wide(two), wide(two) + came).astype(jnp.bfloat16),
    )


def received(blocks):
    return [swap(block, "dp", k) for k, block in enumerate(blocks[1:], 1)]


def collected(own, others):
    return sum([wide(block) for block in others], wide(own)).astype(jnp.bfloat16)


def load_weight_kernel(weight_ref, _, weight_out, mark_ref, sem):
    copy = pltpu.make_async_copy(weight_ref, weight_out, sem)
    copy.start()
    mark_ref[...] = jnp.zeros_like(mark_ref)
    copy.wait()


def loaded(weight, after):
    return pl.pallas_call(
        load_weight_kernel,
        in_specs=[pl.BlockSpec(memory_space=pl.ANY)] * 2,
        out_specs=[pl.BlockSpec(memory_space=pltpu.VMEM)] * 2,
        out_shape=[
            pltpu.VMEM(weight.shape, weight.dtype),
            pltpu.VMEM((8, LANES), jnp.float32),
        ],
        scratch_shapes=[pltpu.SemaphoreType.DMA],
        compiler_params=pltpu.CompilerParams(vmem_limit_bytes=VMEM_LIMIT),
        cost_estimate=pl.CostEstimate(flops=0, bytes_accessed=weight.nbytes, transcendentals=0),
    )(pltpu.with_memory_space_constraint(weight, pltpu.HBM), after)


def joined(blocks):
    return blocks[0] if len(blocks) == 1 else jnp.concatenate(blocks, 0)


def add_up(acc, segments, widths, up, base):
    for blocks, width in zip(segments, widths):
        for low in range(0, width, CHUNK):
            held = joined([block[:, low : low + CHUNK] for block in blocks])
            rows = pl.ds(pl.multiple_of(base, CHUNK), CHUNK)
            for s in range(up.shape[0]):
                acc[s] += jnp.dot(held, up[s, rows], preferred_element_type=jnp.float32)
            base = base + CHUNK


def make_hidden(hidden, acc, routed, width, first_expert, top_count):
    meta = joined([block[:, width:].astype(jnp.float32) for block in routed])
    gates = sum(pltpu.roll(meta, LANES - k * top_count, 1) for k in (1, 2, 3))
    lanes = lax.broadcasted_iota(jnp.int32, meta.shape, 1)
    half_width = acc.shape[2] // 2
    for s in range(acc.shape[0]):
        chosen = (meta.astype(jnp.int32) == first_expert + s) & (lanes < top_count)
        own_gate = jnp.sum(jnp.where(chosen, gates, 0.0), 1, keepdims=True)
        gate_half, up_half = acc[s, :, :half_width], acc[s, :, half_width:]
        unit = gate_half * (1.0 / (1.0 + jnp.exp(-gate_half))) * up_half
        hidden[:, s * half_width : (s + 1) * half_width] = (unit * own_gate).astype(jnp.bfloat16)


def multiply_down(out, hidden, down, base):
    for low in range(0, out.shape[1], CHUNK):
        columns = pl.ds(pl.multiple_of(base + low, CHUNK), CHUNK)
        out[:, low : low + CHUNK] = jnp.dot(
            hidden[...], down[:, columns], preferred_element_type=jnp.float32
        ).astype(jnp.bfloat16)


def sums_kernel(top_count, filling, place, own, other, up, *refs):
    if filling:
        down_ref, _, keep_ref, give_ref, down, acc, hidden, sem = refs
        copy = pltpu.make_async_copy(down_ref, down, sem)
        copy.start()
    else:
        down, keep_ref, give_ref, acc, hidden = refs
    part = other.shape[1]
    bases = [place[0] * part, (1 - place[0]) * part]
    acc[...] = jnp.zeros_like(acc)
    add_up(acc, [[own]], [part], up, bases[0])
    add_up(acc, [[other]], [part], up, bases[1])
    make_hidden(hidden, acc, [own], part, place[1], top_count)
    if filling:
        copy.wait()
    multiply_down(give_ref, hidden, down, bases[1])
    multiply_down(keep_ref, hidden, down, bases[0])


def own_kernel(place, own, up, acc):
    part = up.shape[1] // 2
    acc[...] = jnp.zeros_like(acc)
    add_up(acc, [[own]], [part], up, place[0] * part)


def give_kernel(top_count, place, own, other, held, up, down, give_ref, hidden, acc):
    part = other.shape[1]
    base = (1 - place[0]) * part
    acc[...] = held[...]
    add_up(acc, [[other]], [part], up, base)
    make_hidden(hidden, acc, [own], part, place[1], top_count)
    multiply_down(give_ref, hidden, down, base)


def keep_kernel(place, hidden, down, keep_ref):
    multiply_down(keep_ref, hidden, down, place[0] * keep_ref.shape[1])


def call(kernel, operands, out_shape, scratch_shapes=(), flops=0, unplaced=0):
    in_vmem = pl.BlockSpec(memory_space=pltpu.VMEM)
    place, *arrays = operands
    split = len(arrays) - unplaced
    return pl.pallas_call(
        kernel,
        in_specs=[pl.BlockSpec(memory_space=pltpu.SMEM)]
        + [in_vmem] * split
        + [pl.BlockSpec(memory_space=pl.ANY)] * unplaced,
        out_specs=[in_vmem] * len(out_shape),
        out_shape=out_shape,
        scratch_shapes=list(scratch_shapes),
        compiler_params=pltpu.CompilerParams(vmem_limit_bytes=VMEM_LIMIT),
        cost_estimate=pl.CostEstimate(flops=flops, bytes_accessed=0, transcendentals=0),
    )(
        place,
        *(pltpu.with_memory_space_constraint(x, pltpu.VMEM) for x in arrays[:split]),
        *arrays[split:],
    )


def gated_sums(place, top_count, own, other, up, down, mark=None):
    count, part = other.shape
    filling = mark is not None
    out = pltpu.VMEM((count, part), jnp.bfloat16)
    out_shape = [out, out]
    scratch = [
        pltpu.VMEM((up.shape[0], count, up.shape[2]), jnp.float32),
        pltpu.VMEM((count, down.shape[0]), jnp.bfloat16),
    ]
    operands = [place, own, other, up, down]
    if filling:
        operands[-1:] = [pltpu.with_memory_space_constraint(down, pltpu.HBM), mark]
        out_shape.append(pltpu.VMEM(down.shape, down.dtype))
        scratch.append(pltpu.SemaphoreType.DMA)
    return call(
        lambda *refs: sums_kernel(top_count, filling, *refs),
        operands,
        out_shape,
        scratch,
        flops=2 * count * (up.size + down.size),
        unplaced=2 if filling else 0,
    )


def gated_sums_in_steps(place, top_count, own, other, up, down):
    count, part = other.shape
    acc_shape = (up.shape[0], count, up.shape[2])
    (held,) = call(
        own_kernel,
        [place, own, up],
        [pltpu.VMEM(acc_shape, jnp.float32)],
        flops=count * up.size,
    )
    give, hidden = call(
        lambda *refs: give_kernel(top_count, *refs),
        [place, own, other, held, up, down],
        [
            pltpu.VMEM((count, part), jnp.bfloat16),
            pltpu.VMEM((count, down.shape[0]), jnp.bfloat16),
        ],
        [pltpu.VMEM(acc_shape, jnp.float32)],
        flops=count * (up.size + down.size),
    )
    (keep,) = call(
        keep_kernel,
        [place, hidden, down],
        [pltpu.VMEM((count, part), jnp.bfloat16)],
        flops=count * down.size,
    )
    return keep, give


def first_kernel(place, *refs):
    sources, (keep_ref, give_ref, tokens, ids, gates, turned, sems) = refs[:3], refs[3:]
    copies = [
        pltpu.make_async_copy(source, target, sems.at[number])
        for number, (source, target) in enumerate(zip(sources, (tokens, ids, gates)))
    ]
    for copy in copies:
        copy.start()
    for copy in copies:
        copy.wait()
    core = place[0]
    part = tokens.shape[1] // 2
    top_count, rows = ids.shape
    turned[...] = jnp.zeros_like(turned)
    left = gates[...]
    parts = [ids[...].astype(jnp.float32)]
    for _ in range(3):
        parts.append(left.astype(jnp.bfloat16).astype(jnp.float32))
        left = left - parts[-1]
    for number, values in enumerate(parts):
        turned[number * top_count : (number + 1) * top_count, :rows] = values
    routing = turned[...].T[:rows].astype(jnp.bfloat16)
    for half, out in ((core, keep_ref), (1 - core, give_ref)):
        out[:, :part] = tokens[:, pl.ds(pl.multiple_of(half * part, LANES), part)]
        out[:, part:] = routing


def first_halves(place, tokens, expert_ids, gate_probs):
    rows, width = tokens.shape
    sources = [tokens, expert_ids.T, gate_probs.T]
    return pl.pallas_call(
        first_kernel,
        in_specs=[pl.BlockSpec(memory_space=pltpu.SMEM)]
        + [pl.BlockSpec(memory_space=pl.ANY)] * 3,
        out_specs=[pl.BlockSpec(memory_space=pltpu.VMEM)] * 2,
        out_shape=[pltpu.VMEM((rows, width // 2 + LANES), jnp.bfloat16)] * 2,
        scratch_shapes=[pltpu.VMEM(x.shape, x.dtype) for x in sources]
        + [pltpu.VMEM((LANES, LANES), jnp.float32), pltpu.SemaphoreType.DMA((3,))],
        compiler_params=pltpu.CompilerParams(vmem_limit_bytes=VMEM_LIMIT),
    )(place, *(pltpu.with_memory_space_constraint(x, pltpu.HBM) for x in sources))


def added_kernel(kept_ref, taken_ref, total_ref):
    total = kept_ref[...].astype(jnp.float32) + taken_ref[...].astype(jnp.float32)
    total_ref[...] = total.astype(jnp.bfloat16)


def added(kept, taken):
    in_vmem = pl.BlockSpec(memory_space=pltpu.VMEM)
    return pl.pallas_call(
        added_kernel,
        in_specs=[in_vmem] * 2,
        out_specs=in_vmem,
        out_shape=pltpu.VMEM(kept.shape, jnp.bfloat16),
        compiler_params=pltpu.CompilerParams(vmem_limit_bytes=VMEM_LIMIT),
    )(*(pltpu.with_memory_space_constraint(x, pltpu.VMEM) for x in (kept, taken)))


def load_kernel(layout, swap_slot, *refs):
    owners, per_device, top_count, step, scale = layout
    *metas, _, load_ref = refs
    experts_all = owners * per_device
    high, low = [], []
    for meta in metas:
        values = meta[...].astype(jnp.float32)
        lanes = lax.broadcasted_iota(jnp.int32, values.shape, 1)
        gates = sum(pltpu.roll(values, LANES - k * top_count, 1) for k in (1, 2, 3))
        amounts = jnp.round(gates * step)
        upper = jnp.floor(amounts * (1.0 / PART))
        lower = amounts - upper * PART
        ids = jnp.where(lanes < top_count, values, -1.0)
        high.append([])
        low.append([])
        for e in range(experts_all):
            chosen = ids == e
            high[-1].append(jnp.sum(jnp.where(chosen, upper, 0.0), 0, keepdims=True))
            low[-1].append(jnp.sum(jnp.where(chosen, lower, 0.0), 0, keepdims=True))
    sums = []
    for part in (high, low):
        rows = [sum(block[e] for block in part) for e in range(experts_all)]
        sums.append(jnp.sum(jnp.concatenate(rows, 0), 1, keepdims=True))
    totals = (sums[0] * PART + sums[1]) * (1.0 / step)
    expert = lax.broadcasted_iota(jnp.int32, (experts_all, LANES), 0)
    owner = lax.broadcasted_iota(jnp.int32, (experts_all, LANES), 1)
    home = expert // per_device
    slot = jnp.zeros_like(home)
    for h in range(owners):
        slot = jnp.where(home == h, swap_slot[h], slot)
    partner = (home + owners // 2) % owners
    holder = jnp.where(expert % per_device == slot, partner, home)
    load_ref[...] = jnp.sum(jnp.where(holder == owner, totals, 0.0), 0, keepdims=True) * scale


def planned_load(metas, swap_slot, owners, per_device, top_count, after):
    count = sum(meta.shape[0] for meta in metas)
    step = 2.0 ** (31 - (count * GATE_MOST).bit_length())
    layout = (owners, per_device, top_count, step, owners / count)
    in_vmem = pl.BlockSpec(memory_space=pltpu.VMEM)
    load = pl.pallas_call(
        lambda *refs: load_kernel(layout, *refs),
        in_specs=[pl.BlockSpec(memory_space=pltpu.SMEM)]
        + [in_vmem] * len(metas)
        + [pl.BlockSpec(memory_space=pl.ANY)],
        out_specs=in_vmem,
        out_shape=jax.ShapeDtypeStruct((1, LANES), jnp.float32),
        compiler_params=pltpu.CompilerParams(vmem_limit_bytes=VMEM_LIMIT),
        cost_estimate=pl.CostEstimate(
            flops=0, bytes_accessed=sum(meta.nbytes for meta in metas), transcendentals=0
        ),
    )(swap_slot, *metas, after)
    return load


def on_device(tokens, expert_ids, gate_probs, in_weight, out_weight, swap_slot):
    groups, chips = lax.axis_size("dp"), lax.axis_size("chip")
    owners = 2 * chips
    near_chips = chips // 2
    per_device = in_weight.shape[0]
    rows, width = tokens.shape
    part = width // 2
    top_count = expert_ids.shape[1]
    half_width = out_weight.shape[1]
    core = lax.axis_index("core")
    first = core == 0
    first_expert = (lax.axis_index("chip") * 2 + core) * per_device
    place = jnp.stack([core, first_expert]).astype(jnp.int32)

    keep, give = first_halves(place, tokens, expert_ids, gate_probs)
    taken = swap(give, "core", 1)
    chip_rows = row_major(
        jnp.concatenate([jnp.where(first, keep, taken), jnp.where(first, taken, keep)], 0)
    )

    def sums_of(own, weights, *mark):
        other = swap(own[:, :part], "core", 1)
        return gated_sums(place, top_count, own, other, *weights, *mark)

    def chip_sums(keep, give):
        return (wide(keep) + wide(swap(give, "core", 1))).astype(jnp.bfloat16)

    chip_blocks = [chip_rows] + [swap(chip_rows, "chip", j) for j in range(1, chips)]
    direct = [swap(chip_rows, "dp", k) for k in range(1, groups)]
    up, mark = loaded(in_weight, chip_blocks[1])
    chip_blocks[1:], mark = lax.optimization_barrier((chip_blocks[1:], mark))
    far = row_major(jnp.concatenate(chip_blocks[1:], 0))
    held = row_major(jnp.concatenate([*chip_blocks, *direct], 0))
    near = spread_near(far)
    weights = [up, out_weight.reshape(per_device * half_width, width)]
    pieces = [held]
    if held.shape[0] > MOST_ROWS:
        pieces = [row_major(jnp.concatenate(chip_blocks, 0)), *direct]
    keep, give, weights[1] = sums_of(pieces[0], weights, mark)
    later = [sums_of(piece, weights) for piece in pieces[1:]]
    if later:
        keep, give = (jnp.concatenate(x, 0) for x in zip((keep, give), *later))
    first_sum = chip_sums(keep, give)
    near = behind(near, give)
    own_sum = first_sum[: chips * 2 * rows]
    direct_sums = [
        first_sum[low : low + 2 * rows]
        for low in range(chips * 2 * rows, first_sum.shape[0], 2 * rows)
    ]
    if groups == 4:
        rest = cross(jnp.where(first, near[0], near[1]))
        near = row_major(jnp.concatenate(near, 0))
        keep, give = sums_of(near, weights)
        pair = chip_sums(keep, give)
        rest = behind(rest, give)
        other = swap(rest[:, :part], "core", 1)
        keep, give = gated_sums_in_steps(place, top_count, rest, other, *weights)
        sums = [pair[: far.shape[0]], pair[far.shape[0] :], added(keep, swap(give, "core", 1))]
        sums = [jnp.concatenate([o, s], 0) for o, s in zip(direct_sums, sums)]
        sums = [own_sum, *with_fourth(*sums, first)]
        metas = [held, near, rest]
    else:
        sums = [own_sum]
        for block, o in zip(near, direct_sums):
            keep, give = sums_of(block, weights)
            sums += [jnp.concatenate([o, chip_sums(keep, give)], 0)]
        metas = [held, *near]
    metas = [block[:, block.shape[1] - LANES :] for block in metas]
    border = 2 * near_chips * rows
    high = [block[border:] for block in sums]
    low = [block[:border] for block in sums]
    total = collected(high[0], received(high))
    blocks = [total[at : at + 2 * rows] for at in range(0, total.shape[0], 2 * rows)]
    load = planned_load(metas, swap_slot, owners, per_device, top_count, blocks[0])
    low = behind(low, total)
    total = collected(low[0], received(low))
    blocks = [total[at : at + 2 * rows] for at in range(0, border, 2 * rows)] + blocks
    total = wide(blocks[0])
    for j in range(1, chips):
        total = total + wide(swap(blocks[j], "chip", j))
    total = total.astype(jnp.bfloat16)
    upper, lower = total[:rows], total[rows:]
    arrived = swap(jnp.where(first, lower, upper), "core", 1)
    kept = jnp.where(first, upper, lower)
    mixed_out = row_major(
        jnp.concatenate([jnp.where(first, kept, arrived), jnp.where(first, arrived, kept)], 1)
    )

    return (mixed_out, load[0, :owners])


def solution(mesh):
    groups, owners = mesh.devices.shape
    fine = Mesh(mesh.devices.reshape(groups, owners // 2, 2), ("dp", "chip", "core"))
    rows = P(("dp", "chip", "core"), None)
    return jax.shard_map(
        on_device,
        mesh=fine,
        in_specs=(
            rows,
            rows,
            rows,
            P(("chip", "core"), None, "dp"),
            P(("chip", "core"), "dp", None),
            P(),
        ),
        out_specs=(rows, P()),
        check_vma=False,
    )
```

```python
import jax
import jax.numpy as jnp
from jax import lax
from jax.experimental import pallas as pl
from jax.experimental.pallas import tpu as pltpu
from jax.experimental.layout import Layout, with_layout_constraint
from jax.sharding import Mesh, PartitionSpec as P

LANES = 128
PART = 1024.0
CHUNK = 1024
MOST_ROWS = 512
VMEM_LIMIT = 12 * 2**20
GATE_MOST = 5


def row_major(value):
    return with_layout_constraint(value, Layout(major_to_minor=tuple(range(value.ndim))))


def swap(value, axis, distance):
    size = lax.axis_size(axis)
    pairs = [(i, i ^ distance) for i in range(size)]
    return row_major(lax.ppermute(row_major(value), axis, pairs))


def spread_near(block):
    size = lax.axis_size("dp")
    return [swap(block, "dp", k) for k in range(1, 3 if size == 4 else size)]


def cross(value):
    pairs = []
    for i in range(4):
        pairs += [(2 * i, 2 * (i ^ 2)), (2 * i + 1, 2 * (i ^ 1) + 1)]
    return row_major(lax.ppermute(row_major(value), ("dp", "core"), pairs))


def behind(values, others):
    return lax.optimization_barrier((values, others))[0]


def wide(value):
    return value.astype(jnp.float32)


def with_fourth(one, two, fourth, first):
    came = wide(cross(fourth))
    return (
        jnp.where(first, wide(one) + came, wide(one)).astype(jnp.bfloat16),
        jnp.where(first, wide(two), wide(two) + came).astype(jnp.bfloat16),
    )


def received(blocks):
    return [swap(block, "dp", k) for k, block in enumerate(blocks[1:], 1)]


def collected(own, others):
    return sum([wide(block) for block in others], wide(own)).astype(jnp.bfloat16)


def load_weight_kernel(weight_ref, _, weight_out, mark_ref, sem):
    copy = pltpu.make_async_copy(weight_ref, weight_out, sem)
    copy.start()
    mark_ref[...] = jnp.zeros_like(mark_ref)
    copy.wait()


def loaded(weight, after):
    return pl.pallas_call(
        load_weight_kernel,
        in_specs=[pl.BlockSpec(memory_space=pl.ANY)] * 2,
        out_specs=[pl.BlockSpec(memory_space=pltpu.VMEM)] * 2,
        out_shape=[
            pltpu.VMEM(weight.shape, weight.dtype),
            pltpu.VMEM((8, LANES), jnp.float32),
        ],
        scratch_shapes=[pltpu.SemaphoreType.DMA],
        compiler_params=pltpu.CompilerParams(vmem_limit_bytes=VMEM_LIMIT),
        cost_estimate=pl.CostEstimate(flops=0, bytes_accessed=weight.nbytes, transcendentals=0),
    )(pltpu.with_memory_space_constraint(weight, pltpu.HBM), after)


def joined(blocks):
    return blocks[0] if len(blocks) == 1 else jnp.concatenate(blocks, 0)


def add_up(acc, segments, widths, up, base):
    for blocks, width in zip(segments, widths):
        for low in range(0, width, CHUNK):
            held = joined([block[:, low : low + CHUNK] for block in blocks])
            rows = pl.ds(pl.multiple_of(base, CHUNK), CHUNK)
            for s in range(up.shape[0]):
                acc[s] += jnp.dot(held, up[s, rows], preferred_element_type=jnp.float32)
            base = base + CHUNK


def make_hidden(hidden, acc, routed, width, first_expert, top_count):
    meta = joined([block[:, width:].astype(jnp.float32) for block in routed])
    gates = sum(pltpu.roll(meta, LANES - k * top_count, 1) for k in (1, 2, 3))
    lanes = lax.broadcasted_iota(jnp.int32, meta.shape, 1)
    half_width = acc.shape[2] // 2
    for s in range(acc.shape[0]):
        chosen = (meta.astype(jnp.int32) == first_expert + s) & (lanes < top_count)
        own_gate = jnp.sum(jnp.where(chosen, gates, 0.0), 1, keepdims=True)
        gate_half, up_half = acc[s, :, :half_width], acc[s, :, half_width:]
        unit = gate_half * (1.0 / (1.0 + jnp.exp(-gate_half))) * up_half
        hidden[:, s * half_width : (s + 1) * half_width] = (unit * own_gate).astype(jnp.bfloat16)


def multiply_down(out, hidden, down, base):
    for low in range(0, out.shape[1], CHUNK):
        columns = pl.ds(pl.multiple_of(base + low, CHUNK), CHUNK)
        out[:, low : low + CHUNK] = jnp.dot(
            hidden[...], down[:, columns], preferred_element_type=jnp.float32
        ).astype(jnp.bfloat16)


def sums_kernel(top_count, filling, place, own, other, up, *refs):
    if filling:
        down_ref, _, keep_ref, give_ref, down, acc, hidden, sem = refs
        copy = pltpu.make_async_copy(down_ref, down, sem)
        copy.start()
    else:
        down, keep_ref, give_ref, acc, hidden = refs
    part = other.shape[1]
    bases = [place[0] * part, (1 - place[0]) * part]
    acc[...] = jnp.zeros_like(acc)
    add_up(acc, [[own]], [part], up, bases[0])
    add_up(acc, [[other]], [part], up, bases[1])
    make_hidden(hidden, acc, [own], part, place[1], top_count)
    if filling:
        copy.wait()
    multiply_down(give_ref, hidden, down, bases[1])
    multiply_down(keep_ref, hidden, down, bases[0])


def own_kernel(place, own, up, acc):
    part = up.shape[1] // 2
    acc[...] = jnp.zeros_like(acc)
    add_up(acc, [[own]], [part], up, place[0] * part)


def give_kernel(top_count, place, own, other, held, up, down, give_ref, hidden, acc):
    part = other.shape[1]
    base = (1 - place[0]) * part
    acc[...] = held[...]
    add_up(acc, [[other]], [part], up, base)
    make_hidden(hidden, acc, [own], part, place[1], top_count)
    multiply_down(give_ref, hidden, down, base)


def keep_kernel(place, hidden, down, keep_ref):
    multiply_down(keep_ref, hidden, down, place[0] * keep_ref.shape[1])


def call(kernel, operands, out_shape, scratch_shapes=(), flops=0, unplaced=0):
    in_vmem = pl.BlockSpec(memory_space=pltpu.VMEM)
    place, *arrays = operands
    split = len(arrays) - unplaced
    return pl.pallas_call(
        kernel,
        in_specs=[pl.BlockSpec(memory_space=pltpu.SMEM)]
        + [in_vmem] * split
        + [pl.BlockSpec(memory_space=pl.ANY)] * unplaced,
        out_specs=[in_vmem] * len(out_shape),
        out_shape=out_shape,
        scratch_shapes=list(scratch_shapes),
        compiler_params=pltpu.CompilerParams(vmem_limit_bytes=VMEM_LIMIT),
        cost_estimate=pl.CostEstimate(flops=flops, bytes_accessed=0, transcendentals=0),
    )(
        place,
        *(pltpu.with_memory_space_constraint(x, pltpu.VMEM) for x in arrays[:split]),
        *arrays[split:],
    )


def gated_sums(place, top_count, own, other, up, down, mark=None):
    count, part = other.shape
    filling = mark is not None
    out = pltpu.VMEM((count, part), jnp.bfloat16)
    out_shape = [out, out]
    scratch = [
        pltpu.VMEM((up.shape[0], count, up.shape[2]), jnp.float32),
        pltpu.VMEM((count, down.shape[0]), jnp.bfloat16),
    ]
    operands = [place, own, other, up, down]
    if filling:
        operands[-1:] = [pltpu.with_memory_space_constraint(down, pltpu.HBM), mark]
        out_shape.append(pltpu.VMEM(down.shape, down.dtype))
        scratch.append(pltpu.SemaphoreType.DMA)
    return call(
        lambda *refs: sums_kernel(top_count, filling, *refs),
        operands,
        out_shape,
        scratch,
        flops=2 * count * (up.size + down.size),
        unplaced=2 if filling else 0,
    )


def gated_sums_in_steps(place, top_count, own, other, up, down):
    count, part = other.shape
    acc_shape = (up.shape[0], count, up.shape[2])
    (held,) = call(
        own_kernel,
        [place, own, up],
        [pltpu.VMEM(acc_shape, jnp.float32)],
        flops=count * up.size,
    )
    give, hidden = call(
        lambda *refs: give_kernel(top_count, *refs),
        [place, own, other, held, up, down],
        [
            pltpu.VMEM((count, part), jnp.bfloat16),
            pltpu.VMEM((count, down.shape[0]), jnp.bfloat16),
        ],
        [pltpu.VMEM(acc_shape, jnp.float32)],
        flops=count * (up.size + down.size),
    )
    (keep,) = call(
        keep_kernel,
        [place, hidden, down],
        [pltpu.VMEM((count, part), jnp.bfloat16)],
        flops=count * down.size,
    )
    return keep, give


def first_kernel(place, *refs):
    sources, (keep_ref, give_ref, tokens, ids, gates, turned, sems) = refs[:3], refs[3:]
    copies = [
        pltpu.make_async_copy(source, target, sems.at[number])
        for number, (source, target) in enumerate(zip(sources, (tokens, ids, gates)))
    ]
    for copy in copies:
        copy.start()
    for copy in copies:
        copy.wait()
    core = place[0]
    part = tokens.shape[1] // 2
    top_count, rows = ids.shape
    turned[...] = jnp.zeros_like(turned)
    left = gates[...]
    parts = [ids[...].astype(jnp.float32)]
    for _ in range(3):
        parts.append(left.astype(jnp.bfloat16).astype(jnp.float32))
        left = left - parts[-1]
    for number, values in enumerate(parts):
        turned[number * top_count : (number + 1) * top_count, :rows] = values
    routing = turned[...].T[:rows].astype(jnp.bfloat16)
    for half, out in ((core, keep_ref), (1 - core, give_ref)):
        out[:, :part] = tokens[:, pl.ds(pl.multiple_of(half * part, LANES), part)]
        out[:, part:] = routing


def first_halves(place, tokens, expert_ids, gate_probs):
    rows, width = tokens.shape
    sources = [tokens, expert_ids.T, gate_probs.T]
    return pl.pallas_call(
        first_kernel,
        in_specs=[pl.BlockSpec(memory_space=pltpu.SMEM)]
        + [pl.BlockSpec(memory_space=pl.ANY)] * 3,
        out_specs=[pl.BlockSpec(memory_space=pltpu.VMEM)] * 2,
        out_shape=[pltpu.VMEM((rows, width // 2 + LANES), jnp.bfloat16)] * 2,
        scratch_shapes=[pltpu.VMEM(x.shape, x.dtype) for x in sources]
        + [pltpu.VMEM((LANES, LANES), jnp.float32), pltpu.SemaphoreType.DMA((3,))],
        compiler_params=pltpu.CompilerParams(vmem_limit_bytes=VMEM_LIMIT),
    )(place, *(pltpu.with_memory_space_constraint(x, pltpu.HBM) for x in sources))


def added_kernel(kept_ref, taken_ref, total_ref):
    total = kept_ref[...].astype(jnp.float32) + taken_ref[...].astype(jnp.float32)
    total_ref[...] = total.astype(jnp.bfloat16)


def added(kept, taken):
    in_vmem = pl.BlockSpec(memory_space=pltpu.VMEM)
    return pl.pallas_call(
        added_kernel,
        in_specs=[in_vmem] * 2,
        out_specs=in_vmem,
        out_shape=pltpu.VMEM(kept.shape, jnp.bfloat16),
        compiler_params=pltpu.CompilerParams(vmem_limit_bytes=VMEM_LIMIT),
    )(*(pltpu.with_memory_space_constraint(x, pltpu.VMEM) for x in (kept, taken)))


def load_kernel(layout, swap_slot, *refs):
    owners, per_device, top_count, step, scale = layout
    *metas, _, load_ref = refs
    experts_all = owners * per_device
    high, low = [], []
    for meta in metas:
        values = meta[...].astype(jnp.float32)
        lanes = lax.broadcasted_iota(jnp.int32, values.shape, 1)
        gates = sum(pltpu.roll(values, LANES - k * top_count, 1) for k in (1, 2, 3))
        amounts = jnp.round(gates * step)
        upper = jnp.floor(amounts * (1.0 / PART))
        lower = amounts - upper * PART
        ids = jnp.where(lanes < top_count, values, -1.0)
        high.append([])
        low.append([])
        for e in range(experts_all):
            chosen = ids == e
            high[-1].append(jnp.sum(jnp.where(chosen, upper, 0.0), 0, keepdims=True))
            low[-1].append(jnp.sum(jnp.where(chosen, lower, 0.0), 0, keepdims=True))
    sums = []
    for part in (high, low):
        rows = [sum(block[e] for block in part) for e in range(experts_all)]
        sums.append(jnp.sum(jnp.concatenate(rows, 0), 1, keepdims=True))
    totals = (sums[0] * PART + sums[1]) * (1.0 / step)
    expert = lax.broadcasted_iota(jnp.int32, (experts_all, LANES), 0)
    owner = lax.broadcasted_iota(jnp.int32, (experts_all, LANES), 1)
    home = expert // per_device
    slot = jnp.zeros_like(home)
    for h in range(owners):
        slot = jnp.where(home == h, swap_slot[h], slot)
    partner = (home + owners // 2) % owners
    holder = jnp.where(expert % per_device == slot, partner, home)
    load_ref[...] = jnp.sum(jnp.where(holder == owner, totals, 0.0), 0, keepdims=True) * scale


def planned_load(metas, swap_slot, owners, per_device, top_count, after):
    count = sum(meta.shape[0] for meta in metas)
    step = 2.0 ** (31 - (count * GATE_MOST).bit_length())
    layout = (owners, per_device, top_count, step, owners / count)
    in_vmem = pl.BlockSpec(memory_space=pltpu.VMEM)
    load = pl.pallas_call(
        lambda *refs: load_kernel(layout, *refs),
        in_specs=[pl.BlockSpec(memory_space=pltpu.SMEM)]
        + [in_vmem] * len(metas)
        + [pl.BlockSpec(memory_space=pl.ANY)],
        out_specs=in_vmem,
        out_shape=jax.ShapeDtypeStruct((1, LANES), jnp.float32),
        compiler_params=pltpu.CompilerParams(vmem_limit_bytes=VMEM_LIMIT),
        cost_estimate=pl.CostEstimate(
            flops=0, bytes_accessed=sum(meta.nbytes for meta in metas), transcendentals=0
        ),
    )(swap_slot, *metas, after)
    return load


def on_device(tokens, expert_ids, gate_probs, in_weight, out_weight, swap_slot):
    groups, chips = lax.axis_size("dp"), lax.axis_size("chip")
    owners = 2 * chips
    per_device = in_weight.shape[0]
    rows, width = tokens.shape
    part = width // 2
    top_count = expert_ids.shape[1]
    half_width = out_weight.shape[1]
    core = lax.axis_index("core")
    first = core == 0
    first_expert = (lax.axis_index("chip") * 2 + core) * per_device
    place = jnp.stack([core, first_expert]).astype(jnp.int32)

    keep, give = first_halves(place, tokens, expert_ids, gate_probs)
    taken = swap(give, "core", 1)
    chip_rows = row_major(
        jnp.concatenate([jnp.where(first, keep, taken), jnp.where(first, taken, keep)], 0)
    )

    def sums_of(own, weights, *mark):
        other = swap(own[:, :part], "core", 1)
        return gated_sums(place, top_count, own, other, *weights, *mark)

    def chip_sums(keep, give):
        return (wide(keep) + wide(swap(give, "core", 1))).astype(jnp.bfloat16)

    chip_blocks = [swap(chip_rows, "chip", j) for j in range(chips - 1, 0, -1)]
    chip_blocks = [chip_rows, *chip_blocks[::-1]]
    direct = [swap(chip_rows, "dp", k) for k in range(1, groups)]
    up, mark = loaded(in_weight, direct[0])
    chip_blocks[1:], mark = lax.optimization_barrier((chip_blocks[1:], mark))
    far = row_major(jnp.concatenate(chip_blocks[1:], 0))
    held = row_major(jnp.concatenate([*chip_blocks, *direct], 0))
    near = spread_near(far)
    weights = [up, out_weight.reshape(per_device * half_width, width)]
    pieces = [held]
    if held.shape[0] > MOST_ROWS:
        pieces = [row_major(jnp.concatenate(chip_blocks, 0)), *direct]
    keep, give, weights[1] = sums_of(pieces[0], weights, mark)
    later = [sums_of(piece, weights) for piece in pieces[1:]]
    if later:
        keep, give = (jnp.concatenate(x, 0) for x in zip((keep, give), *later))
    first_sum = chip_sums(keep, give)
    near = behind(near, give)
    border = chips * 2 * rows
    near_sums = [first_sum[: 2 * rows]]
    near_sums += [
        first_sum[low : low + 2 * rows] for low in range(border, first_sum.shape[0], 2 * rows)
    ]
    far_sums = [first_sum[2 * rows : border]]
    if groups == 4:
        rest = cross(jnp.where(first, near[0], near[1]))
        near = row_major(jnp.concatenate(near, 0))
        keep, give = sums_of(near, weights)
        pair = chip_sums(keep, give)
        rest = behind(rest, give)
        other = swap(rest[:, :part], "core", 1)
        keep, give = gated_sums_in_steps(place, top_count, rest, other, *weights)
        fourth = added(keep, swap(give, "core", 1))
        count = far.shape[0]
        far_sums += with_fourth(pair[:count], pair[count:], fourth, first)
        metas = [held, near, rest]
    else:
        far_sums += [chip_sums(*sums_of(block, weights)) for block in near]
        metas = [held, *near]
    metas = [block[:, block.shape[1] - LANES :] for block in metas]
    total = collected(far_sums[0], received(far_sums))
    blocks = [total[at : at + 2 * rows] for at in range(0, total.shape[0], 2 * rows)]
    came = [swap(blocks[j - 1], "chip", j) for j in range(chips - 1, 0, -1)]
    near_sums = behind(near_sums, came[-1])
    came += received(near_sums)
    load = planned_load(metas, swap_slot, owners, per_device, top_count, blocks[0])
    total = collected(near_sums[0], came)
    upper, lower = total[:rows], total[rows:]
    arrived = swap(jnp.where(first, lower, upper), "core", 1)
    kept = jnp.where(first, upper, lower)
    mixed_out = row_major(
        jnp.concatenate([jnp.where(first, kept, arrived), jnp.where(first, arrived, kept)], 1)
    )

    return (mixed_out, load[0, :owners])


def solution(mesh):
    groups, owners = mesh.devices.shape
    fine = Mesh(mesh.devices.reshape(groups, owners // 2, 2), ("dp", "chip", "core"))
    rows = P(("dp", "chip", "core"), None)
    return jax.shard_map(
        on_device,
        mesh=fine,
        in_specs=(
            rows,
            rows,
            rows,
            P(("chip", "core"), None, "dp"),
            P(("chip", "core"), "dp", None),
            P(),
        ),
        out_specs=(rows, P()),
        check_vma=False,
    )
```

```python
import jax
import jax.numpy as jnp
from jax import lax
from jax.experimental import pallas as pl
from jax.experimental.pallas import tpu as pltpu
from jax.experimental.layout import Layout, with_layout_constraint
from jax.sharding import Mesh, PartitionSpec as P

LANES = 128
PART = 1024.0
CHUNK = 1024
MOST_ROWS = 512
VMEM_LIMIT = 12 * 2**20
GATE_MOST = 5


def row_major(value):
    return with_layout_constraint(value, Layout(major_to_minor=tuple(range(value.ndim))))


def swap(value, axis, distance):
    size = lax.axis_size(axis)
    pairs = [(i, i ^ distance) for i in range(size)]
    return row_major(lax.ppermute(row_major(value), axis, pairs))


def spread_near(block):
    size = lax.axis_size("dp")
    return [swap(block, "dp", k) for k in range(1, 3 if size == 4 else size)]


def cross(value):
    pairs = []
    for i in range(4):
        pairs += [(2 * i, 2 * (i ^ 2)), (2 * i + 1, 2 * (i ^ 1) + 1)]
    return row_major(lax.ppermute(row_major(value), ("dp", "core"), pairs))


def behind(values, others):
    return lax.optimization_barrier((values, others))[0]


def wide(value):
    return value.astype(jnp.float32)


def received(blocks):
    return [swap(block, "dp", k) for k, block in enumerate(blocks[1:], 1)]


def collected(own, others):
    return sum([wide(block) for block in others], wide(own)).astype(jnp.bfloat16)


def load_weight_kernel(weight_ref, _, weight_out, mark_ref, sem):
    copy = pltpu.make_async_copy(weight_ref, weight_out, sem)
    copy.start()
    mark_ref[...] = jnp.zeros_like(mark_ref)
    copy.wait()


def loaded(weight, after):
    return pl.pallas_call(
        load_weight_kernel,
        in_specs=[pl.BlockSpec(memory_space=pl.ANY)] * 2,
        out_specs=[pl.BlockSpec(memory_space=pltpu.VMEM)] * 2,
        out_shape=[
            pltpu.VMEM(weight.shape, weight.dtype),
            pltpu.VMEM((8, LANES), jnp.float32),
        ],
        scratch_shapes=[pltpu.SemaphoreType.DMA],
        compiler_params=pltpu.CompilerParams(vmem_limit_bytes=VMEM_LIMIT),
        cost_estimate=pl.CostEstimate(flops=0, bytes_accessed=weight.nbytes, transcendentals=0),
    )(pltpu.with_memory_space_constraint(weight, pltpu.HBM), after)


def joined(blocks):
    return blocks[0] if len(blocks) == 1 else jnp.concatenate(blocks, 0)


def add_up(acc, segments, widths, up, base):
    for blocks, width in zip(segments, widths):
        for low in range(0, width, CHUNK):
            held = joined([block[:, low : low + CHUNK] for block in blocks])
            rows = pl.ds(pl.multiple_of(base, CHUNK), CHUNK)
            for s in range(up.shape[0]):
                acc[s] += jnp.dot(held, up[s, rows], preferred_element_type=jnp.float32)
            base = base + CHUNK


def make_hidden(hidden, acc, routed, width, first_expert, top_count):
    meta = joined([block[:, width:].astype(jnp.float32) for block in routed])
    gates = sum(pltpu.roll(meta, LANES - k * top_count, 1) for k in (1, 2, 3))
    lanes = lax.broadcasted_iota(jnp.int32, meta.shape, 1)
    half_width = acc.shape[2] // 2
    for s in range(acc.shape[0]):
        chosen = (meta.astype(jnp.int32) == first_expert + s) & (lanes < top_count)
        own_gate = jnp.sum(jnp.where(chosen, gates, 0.0), 1, keepdims=True)
        gate_half, up_half = acc[s, :, :half_width], acc[s, :, half_width:]
        unit = gate_half * (1.0 / (1.0 + jnp.exp(-gate_half))) * up_half
        hidden[:, s * half_width : (s + 1) * half_width] = (unit * own_gate).astype(jnp.bfloat16)


def multiply_down(out, hidden, down, base):
    for low in range(0, out.shape[1], CHUNK):
        columns = pl.ds(pl.multiple_of(base + low, CHUNK), CHUNK)
        out[:, low : low + CHUNK] = jnp.dot(
            hidden[...], down[:, columns], preferred_element_type=jnp.float32
        ).astype(jnp.bfloat16)


def sums_kernel(top_count, filling, place, own, other, up, *refs):
    if filling:
        down_ref, _, keep_ref, give_ref, down, acc, hidden, sem = refs
        copy = pltpu.make_async_copy(down_ref, down, sem)
        copy.start()
    else:
        down, keep_ref, give_ref, acc, hidden = refs
    part = other.shape[1]
    bases = [place[0] * part, (1 - place[0]) * part]
    acc[...] = jnp.zeros_like(acc)
    add_up(acc, [[own]], [part], up, bases[0])
    add_up(acc, [[other]], [part], up, bases[1])
    make_hidden(hidden, acc, [own], part, place[1], top_count)
    if filling:
        copy.wait()
    multiply_down(give_ref, hidden, down, bases[1])
    multiply_down(keep_ref, hidden, down, bases[0])


def own_kernel(place, own, up, acc):
    part = up.shape[1] // 2
    acc[...] = jnp.zeros_like(acc)
    add_up(acc, [[own]], [part], up, place[0] * part)


def give_kernel(top_count, place, own, other, held, up, down, give_ref, hidden, acc):
    part = other.shape[1]
    base = (1 - place[0]) * part
    acc[...] = held[...]
    add_up(acc, [[other]], [part], up, base)
    make_hidden(hidden, acc, [own], part, place[1], top_count)
    multiply_down(give_ref, hidden, down, base)


def keep_kernel(place, hidden, down, keep_ref):
    multiply_down(keep_ref, hidden, down, place[0] * keep_ref.shape[1])


def call(kernel, operands, out_shape, scratch_shapes=(), flops=0, unplaced=0):
    in_vmem = pl.BlockSpec(memory_space=pltpu.VMEM)
    place, *arrays = operands
    split = len(arrays) - unplaced
    return pl.pallas_call(
        kernel,
        in_specs=[pl.BlockSpec(memory_space=pltpu.SMEM)]
        + [in_vmem] * split
        + [pl.BlockSpec(memory_space=pl.ANY)] * unplaced,
        out_specs=[in_vmem] * len(out_shape),
        out_shape=out_shape,
        scratch_shapes=list(scratch_shapes),
        compiler_params=pltpu.CompilerParams(vmem_limit_bytes=VMEM_LIMIT),
        cost_estimate=pl.CostEstimate(flops=flops, bytes_accessed=0, transcendentals=0),
    )(
        place,
        *(pltpu.with_memory_space_constraint(x, pltpu.VMEM) for x in arrays[:split]),
        *arrays[split:],
    )


def gated_sums(place, top_count, own, other, up, down, mark=None):
    count, part = other.shape
    filling = mark is not None
    out = pltpu.VMEM((count, part), jnp.bfloat16)
    out_shape = [out, out]
    scratch = [
        pltpu.VMEM((up.shape[0], count, up.shape[2]), jnp.float32),
        pltpu.VMEM((count, down.shape[0]), jnp.bfloat16),
    ]
    operands = [place, own, other, up, down]
    if filling:
        operands[-1:] = [pltpu.with_memory_space_constraint(down, pltpu.HBM), mark]
        out_shape.append(pltpu.VMEM(down.shape, down.dtype))
        scratch.append(pltpu.SemaphoreType.DMA)
    return call(
        lambda *refs: sums_kernel(top_count, filling, *refs),
        operands,
        out_shape,
        scratch,
        flops=2 * count * (up.size + down.size),
        unplaced=2 if filling else 0,
    )


def gated_sums_in_steps(place, top_count, own, other, up, down):
    count, part = other.shape
    acc_shape = (up.shape[0], count, up.shape[2])
    (held,) = call(
        own_kernel,
        [place, own, up],
        [pltpu.VMEM(acc_shape, jnp.float32)],
        flops=count * up.size,
    )
    give, hidden = call(
        lambda *refs: give_kernel(top_count, *refs),
        [place, own, other, held, up, down],
        [
            pltpu.VMEM((count, part), jnp.bfloat16),
            pltpu.VMEM((count, down.shape[0]), jnp.bfloat16),
        ],
        [pltpu.VMEM(acc_shape, jnp.float32)],
        flops=count * (up.size + down.size),
    )
    (keep,) = call(
        keep_kernel,
        [place, hidden, down],
        [pltpu.VMEM((count, part), jnp.bfloat16)],
        flops=count * down.size,
    )
    return keep, give


def first_kernel(place, *refs):
    sources, (keep_ref, give_ref, tokens, ids, gates, turned, sems) = refs[:3], refs[3:]
    copies = [
        pltpu.make_async_copy(source, target, sems.at[number])
        for number, (source, target) in enumerate(zip(sources, (tokens, ids, gates)))
    ]
    for copy in copies:
        copy.start()
    for copy in copies:
        copy.wait()
    core = place[0]
    part = tokens.shape[1] // 2
    top_count, rows = ids.shape
    turned[...] = jnp.zeros_like(turned)
    left = gates[...]
    parts = [ids[...].astype(jnp.float32)]
    for _ in range(3):
        parts.append(left.astype(jnp.bfloat16).astype(jnp.float32))
        left = left - parts[-1]
    for number, values in enumerate(parts):
        turned[number * top_count : (number + 1) * top_count, :rows] = values
    routing = turned[...].T[:rows].astype(jnp.bfloat16)
    for half, out in ((core, keep_ref), (1 - core, give_ref)):
        out[:, :part] = tokens[:, pl.ds(pl.multiple_of(half * part, LANES), part)]
        out[:, part:] = routing


def first_halves(place, tokens, expert_ids, gate_probs):
    rows, width = tokens.shape
    sources = [tokens, expert_ids.T, gate_probs.T]
    return pl.pallas_call(
        first_kernel,
        in_specs=[pl.BlockSpec(memory_space=pltpu.SMEM)]
        + [pl.BlockSpec(memory_space=pl.ANY)] * 3,
        out_specs=[pl.BlockSpec(memory_space=pltpu.VMEM)] * 2,
        out_shape=[pltpu.VMEM((rows, width // 2 + LANES), jnp.bfloat16)] * 2,
        scratch_shapes=[pltpu.VMEM(x.shape, x.dtype) for x in sources]
        + [pltpu.VMEM((LANES, LANES), jnp.float32), pltpu.SemaphoreType.DMA((3,))],
        compiler_params=pltpu.CompilerParams(vmem_limit_bytes=VMEM_LIMIT),
    )(place, *(pltpu.with_memory_space_constraint(x, pltpu.HBM) for x in sources))


def added_kernel(kept_ref, taken_ref, total_ref):
    total = kept_ref[...].astype(jnp.float32) + taken_ref[...].astype(jnp.float32)
    total_ref[...] = total.astype(jnp.bfloat16)


def added(kept, taken):
    in_vmem = pl.BlockSpec(memory_space=pltpu.VMEM)
    return pl.pallas_call(
        added_kernel,
        in_specs=[in_vmem] * 2,
        out_specs=in_vmem,
        out_shape=pltpu.VMEM(kept.shape, jnp.bfloat16),
        compiler_params=pltpu.CompilerParams(vmem_limit_bytes=VMEM_LIMIT),
    )(*(pltpu.with_memory_space_constraint(x, pltpu.VMEM) for x in (kept, taken)))


def load_kernel(layout, swap_slot, *refs):
    owners, per_device, top_count, step, scale = layout
    *metas, _, load_ref = refs
    experts_all = owners * per_device
    high, low = [], []
    for meta in metas:
        values = meta[...].astype(jnp.float32)
        lanes = lax.broadcasted_iota(jnp.int32, values.shape, 1)
        gates = sum(pltpu.roll(values, LANES - k * top_count, 1) for k in (1, 2, 3))
        amounts = jnp.round(gates * step)
        upper = jnp.floor(amounts * (1.0 / PART))
        lower = amounts - upper * PART
        ids = jnp.where(lanes < top_count, values, -1.0)
        high.append([])
        low.append([])
        for e in range(experts_all):
            chosen = ids == e
            high[-1].append(jnp.sum(jnp.where(chosen, upper, 0.0), 0, keepdims=True))
            low[-1].append(jnp.sum(jnp.where(chosen, lower, 0.0), 0, keepdims=True))
    sums = []
    for part in (high, low):
        rows = [sum(block[e] for block in part) for e in range(experts_all)]
        sums.append(jnp.sum(jnp.concatenate(rows, 0), 1, keepdims=True))
    totals = (sums[0] * PART + sums[1]) * (1.0 / step)
    expert = lax.broadcasted_iota(jnp.int32, (experts_all, LANES), 0)
    owner = lax.broadcasted_iota(jnp.int32, (experts_all, LANES), 1)
    home = expert // per_device
    slot = jnp.zeros_like(home)
    for h in range(owners):
        slot = jnp.where(home == h, swap_slot[h], slot)
    partner = (home + owners // 2) % owners
    holder = jnp.where(expert % per_device == slot, partner, home)
    load_ref[...] = jnp.sum(jnp.where(holder == owner, totals, 0.0), 0, keepdims=True) * scale


def planned_load(metas, swap_slot, owners, per_device, top_count, after):
    count = sum(meta.shape[0] for meta in metas)
    step = 2.0 ** (31 - (count * GATE_MOST).bit_length())
    layout = (owners, per_device, top_count, step, owners / count)
    in_vmem = pl.BlockSpec(memory_space=pltpu.VMEM)
    load = pl.pallas_call(
        lambda *refs: load_kernel(layout, *refs),
        in_specs=[pl.BlockSpec(memory_space=pltpu.SMEM)]
        + [in_vmem] * len(metas)
        + [pl.BlockSpec(memory_space=pl.ANY)],
        out_specs=in_vmem,
        out_shape=jax.ShapeDtypeStruct((1, LANES), jnp.float32),
        compiler_params=pltpu.CompilerParams(vmem_limit_bytes=VMEM_LIMIT),
        cost_estimate=pl.CostEstimate(
            flops=0, bytes_accessed=sum(meta.nbytes for meta in metas), transcendentals=0
        ),
    )(swap_slot, *metas, after)
    return load


def on_device(tokens, expert_ids, gate_probs, in_weight, out_weight, swap_slot):
    groups, chips = lax.axis_size("dp"), lax.axis_size("chip")
    owners = 2 * chips
    per_device = in_weight.shape[0]
    rows, width = tokens.shape
    part = width // 2
    top_count = expert_ids.shape[1]
    half_width = out_weight.shape[1]
    core = lax.axis_index("core")
    first = core == 0
    first_expert = (lax.axis_index("chip") * 2 + core) * per_device
    place = jnp.stack([core, first_expert]).astype(jnp.int32)

    keep, give = first_halves(place, tokens, expert_ids, gate_probs)
    taken = swap(give, "core", 1)
    chip_rows = row_major(
        jnp.concatenate([jnp.where(first, keep, taken), jnp.where(first, taken, keep)], 0)
    )

    def sums_of(own, weights, *mark):
        other = swap(own[:, :part], "core", 1)
        return gated_sums(place, top_count, own, other, *weights, *mark)

    def chip_sums(keep, give):
        return (wide(keep) + wide(swap(give, "core", 1))).astype(jnp.bfloat16)

    chip_blocks = [swap(chip_rows, "chip", j) for j in range(chips - 1, 0, -1)]
    chip_blocks = [chip_rows, *chip_blocks[::-1]]
    direct = [swap(chip_rows, "dp", k) for k in range(1, groups)]
    up, mark = loaded(in_weight, direct[0])
    chip_blocks[1:], mark = lax.optimization_barrier((chip_blocks[1:], mark))
    far = row_major(jnp.concatenate(chip_blocks[1:], 0))
    held = row_major(jnp.concatenate([*chip_blocks, *direct], 0))
    near = spread_near(far)
    weights = [up, out_weight.reshape(per_device * half_width, width)]
    pieces = [held]
    if held.shape[0] > MOST_ROWS:
        pieces = [row_major(jnp.concatenate(chip_blocks, 0)), *direct]
    keep, give, weights[1] = sums_of(pieces[0], weights, mark)
    later = [sums_of(piece, weights) for piece in pieces[1:]]
    if later:
        keep, give = (jnp.concatenate(x, 0) for x in zip((keep, give), *later))
    first_sum = chip_sums(keep, give)
    near = behind(near, give)
    border = chips * 2 * rows
    near_sums = [first_sum[: 2 * rows]]
    near_sums += [
        first_sum[low : low + 2 * rows] for low in range(border, first_sum.shape[0], 2 * rows)
    ]
    far_sums = [first_sum[2 * rows : border]]

    def parts(block):
        return [block[low : low + 2 * rows] for low in range(0, block.shape[0], 2 * rows)]

    def along_chips(blocks):
        return [swap(blocks[j - 1], "chip", j) for j in range(chips - 1, 0, -1)]

    if groups == 4:
        rest = cross(jnp.where(first, near[0], near[1]))
        near = row_major(jnp.concatenate(near, 0))
        keep, give = sums_of(near, weights)
        far_sums += [*jnp.split(chip_sums(keep, give), 2)]
        whole = [jnp.concatenate(pair, 0) for pair in zip(near_sums, far_sums)]
        rest = behind(rest, give)
        other = behind(swap(rest[:, :part], "core", 1), whole[1:3])
        keep, give = gated_sums_in_steps(place, top_count, rest, other, *weights)
        fourth = parts(added(keep, swap(give, "core", 1)))
        fourth = collected(near_sums[3], along_chips(fourth))
        came = [swap(fourth, "dp", 3)]
        metas = [held, near, rest]
    else:
        far_sums += [chip_sums(*sums_of(block, weights)) for block in near]
        whole = [jnp.concatenate(pair, 0) for pair in zip(near_sums, far_sums)]
        came = []
        metas = [held, *near]
    metas = [block[:, block.shape[1] - LANES :] for block in metas]
    total = parts(collected(whole[0], received(whole)))
    load = planned_load(metas, swap_slot, owners, per_device, top_count, total[0])
    total = collected(total[0], along_chips(total[1:]) + came)
    upper, lower = total[:rows], total[rows:]
    arrived = swap(jnp.where(first, lower, upper), "core", 1)
    kept = jnp.where(first, upper, lower)
    mixed_out = row_major(
        jnp.concatenate([jnp.where(first, kept, arrived), jnp.where(first, arrived, kept)], 1)
    )

    return (mixed_out, load[0, :owners])


def solution(mesh):
    groups, owners = mesh.devices.shape
    fine = Mesh(mesh.devices.reshape(groups, owners // 2, 2), ("dp", "chip", "core"))
    rows = P(("dp", "chip", "core"), None)
    return jax.shard_map(
        on_device,
        mesh=fine,
        in_specs=(
            rows,
            rows,
            rows,
            P(("chip", "core"), None, "dp"),
            P(("chip", "core"), "dp", None),
            P(),
        ),
        out_specs=(rows, P()),
        check_vma=False,
    )
```

```python
import jax
import jax.numpy as jnp
from jax import lax
from jax.experimental import pallas as pl
from jax.experimental.pallas import tpu as pltpu
from jax.experimental.layout import Layout, with_layout_constraint
from jax.sharding import Mesh, PartitionSpec as P

LANES = 128
PART = 1024.0
CHUNK = 1024
MOST_ROWS = 512
VMEM_LIMIT = 12 * 2**20
GATE_MOST = 5


def row_major(value):
    return with_layout_constraint(value, Layout(major_to_minor=tuple(range(value.ndim))))


def swap(value, axis, distance):
    size = lax.axis_size(axis)
    pairs = [(i, i ^ distance) for i in range(size)]
    return row_major(lax.ppermute(row_major(value), axis, pairs))


def spread_near(block):
    size = lax.axis_size("dp")
    return [swap(block, "dp", k) for k in range(1, 3 if size == 4 else size)]


def cross(value):
    pairs = []
    for i in range(4):
        pairs += [(2 * i, 2 * (i ^ 2)), (2 * i + 1, 2 * (i ^ 1) + 1)]
    return row_major(lax.ppermute(row_major(value), ("dp", "core"), pairs))


def behind(values, others):
    return lax.optimization_barrier((values, others))[0]


def wide(value):
    return value.astype(jnp.float32)


def received(blocks):
    return [swap(block, "dp", k) for k, block in enumerate(blocks[1:], 1)]


def collected(own, others):
    return sum([wide(block) for block in others], wide(own)).astype(jnp.bfloat16)


def load_weight_kernel(weight_ref, _, weight_out, mark_ref, sem):
    copy = pltpu.make_async_copy(weight_ref, weight_out, sem)
    copy.start()
    mark_ref[...] = jnp.zeros_like(mark_ref)
    copy.wait()


def loaded(weight, after):
    return pl.pallas_call(
        load_weight_kernel,
        in_specs=[pl.BlockSpec(memory_space=pl.ANY)] * 2,
        out_specs=[pl.BlockSpec(memory_space=pltpu.VMEM)] * 2,
        out_shape=[
            pltpu.VMEM(weight.shape, weight.dtype),
            pltpu.VMEM((8, LANES), jnp.float32),
        ],
        scratch_shapes=[pltpu.SemaphoreType.DMA],
        compiler_params=pltpu.CompilerParams(vmem_limit_bytes=VMEM_LIMIT),
        cost_estimate=pl.CostEstimate(flops=0, bytes_accessed=weight.nbytes, transcendentals=0),
    )(pltpu.with_memory_space_constraint(weight, pltpu.HBM), after)


def joined(blocks):
    return blocks[0] if len(blocks) == 1 else jnp.concatenate(blocks, 0)


def add_up(acc, segments, widths, up, base):
    for blocks, width in zip(segments, widths):
        for low in range(0, width, CHUNK):
            held = joined([block[:, low : low + CHUNK] for block in blocks])
            rows = pl.ds(pl.multiple_of(base, CHUNK), CHUNK)
            for s in range(up.shape[0]):
                acc[s] += jnp.dot(held, up[s, rows], preferred_element_type=jnp.float32)
            base = base + CHUNK


def make_hidden(hidden, acc, routed, width, first_expert, top_count):
    meta = joined([block[:, width:].astype(jnp.float32) for block in routed])
    gates = sum(pltpu.roll(meta, LANES - k * top_count, 1) for k in (1, 2, 3))
    lanes = lax.broadcasted_iota(jnp.int32, meta.shape, 1)
    half_width = acc.shape[2] // 2
    for s in range(acc.shape[0]):
        chosen = (meta.astype(jnp.int32) == first_expert + s) & (lanes < top_count)
        own_gate = jnp.sum(jnp.where(chosen, gates, 0.0), 1, keepdims=True)
        gate_half, up_half = acc[s, :, :half_width], acc[s, :, half_width:]
        unit = gate_half * (1.0 / (1.0 + jnp.exp(-gate_half))) * up_half
        hidden[:, s * half_width : (s + 1) * half_width] = (unit * own_gate).astype(jnp.bfloat16)


def multiply_down(out, hidden, down, base):
    for low in range(0, out.shape[1], CHUNK):
        columns = pl.ds(pl.multiple_of(base + low, CHUNK), CHUNK)
        out[:, low : low + CHUNK] = jnp.dot(
            hidden[...], down[:, columns], preferred_element_type=jnp.float32
        ).astype(jnp.bfloat16)


def sums_kernel(top_count, filling, place, own, other, up, *refs):
    if filling:
        down_ref, _, keep_ref, give_ref, down, acc, hidden, sem = refs
        copy = pltpu.make_async_copy(down_ref, down, sem)
        copy.start()
    else:
        down, keep_ref, give_ref, acc, hidden = refs
    part = other.shape[1]
    bases = [place[0] * part, (1 - place[0]) * part]
    acc[...] = jnp.zeros_like(acc)
    add_up(acc, [[own]], [part], up, bases[0])
    add_up(acc, [[other]], [part], up, bases[1])
    make_hidden(hidden, acc, [own], part, place[1], top_count)
    if filling:
        copy.wait()
    multiply_down(give_ref, hidden, down, bases[1])
    multiply_down(keep_ref, hidden, down, bases[0])


def own_kernel(place, own, up, acc):
    part = up.shape[1] // 2
    acc[...] = jnp.zeros_like(acc)
    add_up(acc, [[own]], [part], up, place[0] * part)


def give_kernel(top_count, place, own, other, held, up, down, give_ref, hidden, acc):
    part = other.shape[1]
    base = (1 - place[0]) * part
    acc[...] = held[...]
    add_up(acc, [[other]], [part], up, base)
    make_hidden(hidden, acc, [own], part, place[1], top_count)
    multiply_down(give_ref, hidden, down, base)


def keep_kernel(place, hidden, down, keep_ref):
    multiply_down(keep_ref, hidden, down, place[0] * keep_ref.shape[1])


def call(kernel, operands, out_shape, scratch_shapes=(), flops=0, unplaced=0):
    in_vmem = pl.BlockSpec(memory_space=pltpu.VMEM)
    place, *arrays = operands
    split = len(arrays) - unplaced
    return pl.pallas_call(
        kernel,
        in_specs=[pl.BlockSpec(memory_space=pltpu.SMEM)]
        + [in_vmem] * split
        + [pl.BlockSpec(memory_space=pl.ANY)] * unplaced,
        out_specs=[in_vmem] * len(out_shape),
        out_shape=out_shape,
        scratch_shapes=list(scratch_shapes),
        compiler_params=pltpu.CompilerParams(vmem_limit_bytes=VMEM_LIMIT),
        cost_estimate=pl.CostEstimate(flops=flops, bytes_accessed=0, transcendentals=0),
    )(
        place,
        *(pltpu.with_memory_space_constraint(x, pltpu.VMEM) for x in arrays[:split]),
        *arrays[split:],
    )


def gated_sums(place, top_count, own, other, up, down, mark=None):
    count, part = other.shape
    filling = mark is not None
    out = pltpu.VMEM((count, part), jnp.bfloat16)
    out_shape = [out, out]
    scratch = [
        pltpu.VMEM((up.shape[0], count, up.shape[2]), jnp.float32),
        pltpu.VMEM((count, down.shape[0]), jnp.bfloat16),
    ]
    operands = [place, own, other, up, down]
    if filling:
        operands[-1:] = [pltpu.with_memory_space_constraint(down, pltpu.HBM), mark]
        out_shape.append(pltpu.VMEM(down.shape, down.dtype))
        scratch.append(pltpu.SemaphoreType.DMA)
    return call(
        lambda *refs: sums_kernel(top_count, filling, *refs),
        operands,
        out_shape,
        scratch,
        flops=2 * count * (up.size + down.size),
        unplaced=2 if filling else 0,
    )


def gated_sums_in_steps(place, top_count, own, other, up, down):
    count, part = other.shape
    acc_shape = (up.shape[0], count, up.shape[2])
    (held,) = call(
        own_kernel,
        [place, own, up],
        [pltpu.VMEM(acc_shape, jnp.float32)],
        flops=count * up.size,
    )
    give, hidden = call(
        lambda *refs: give_kernel(top_count, *refs),
        [place, own, other, held, up, down],
        [
            pltpu.VMEM((count, part), jnp.bfloat16),
            pltpu.VMEM((count, down.shape[0]), jnp.bfloat16),
        ],
        [pltpu.VMEM(acc_shape, jnp.float32)],
        flops=count * (up.size + down.size),
    )
    (keep,) = call(
        keep_kernel,
        [place, hidden, down],
        [pltpu.VMEM((count, part), jnp.bfloat16)],
        flops=count * down.size,
    )
    return keep, give


def first_kernel(place, *refs):
    sources, (keep_ref, give_ref, tokens, ids, gates, turned, sems) = refs[:3], refs[3:]
    copies = [
        pltpu.make_async_copy(source, target, sems.at[number])
        for number, (source, target) in enumerate(zip(sources, (tokens, ids, gates)))
    ]
    for copy in copies:
        copy.start()
    for copy in copies:
        copy.wait()
    core = place[0]
    part = tokens.shape[1] // 2
    top_count, rows = ids.shape
    turned[...] = jnp.zeros_like(turned)
    left = gates[...]
    parts = [ids[...].astype(jnp.float32)]
    for _ in range(3):
        parts.append(left.astype(jnp.bfloat16).astype(jnp.float32))
        left = left - parts[-1]
    for number, values in enumerate(parts):
        turned[number * top_count : (number + 1) * top_count, :rows] = values
    routing = turned[...].T[:rows].astype(jnp.bfloat16)
    for half, out in ((core, keep_ref), (1 - core, give_ref)):
        out[:, :part] = tokens[:, pl.ds(pl.multiple_of(half * part, LANES), part)]
        out[:, part:] = routing


def first_halves(place, tokens, expert_ids, gate_probs):
    rows, width = tokens.shape
    sources = [tokens, expert_ids.T, gate_probs.T]
    return pl.pallas_call(
        first_kernel,
        in_specs=[pl.BlockSpec(memory_space=pltpu.SMEM)]
        + [pl.BlockSpec(memory_space=pl.ANY)] * 3,
        out_specs=[pl.BlockSpec(memory_space=pltpu.VMEM)] * 2,
        out_shape=[pltpu.VMEM((rows, width // 2 + LANES), jnp.bfloat16)] * 2,
        scratch_shapes=[pltpu.VMEM(x.shape, x.dtype) for x in sources]
        + [pltpu.VMEM((LANES, LANES), jnp.float32), pltpu.SemaphoreType.DMA((3,))],
        compiler_params=pltpu.CompilerParams(vmem_limit_bytes=VMEM_LIMIT),
    )(place, *(pltpu.with_memory_space_constraint(x, pltpu.HBM) for x in sources))


def added_kernel(kept_ref, taken_ref, total_ref):
    total = kept_ref[...].astype(jnp.float32) + taken_ref[...].astype(jnp.float32)
    total_ref[...] = total.astype(jnp.bfloat16)


def added(kept, taken):
    in_vmem = pl.BlockSpec(memory_space=pltpu.VMEM)
    return pl.pallas_call(
        added_kernel,
        in_specs=[in_vmem] * 2,
        out_specs=in_vmem,
        out_shape=pltpu.VMEM(kept.shape, jnp.bfloat16),
        compiler_params=pltpu.CompilerParams(vmem_limit_bytes=VMEM_LIMIT),
    )(*(pltpu.with_memory_space_constraint(x, pltpu.VMEM) for x in (kept, taken)))


def load_kernel(layout, swap_slot, *refs):
    owners, per_device, top_count, step, scale = layout
    *metas, _, load_ref = refs
    experts_all = owners * per_device
    high, low = [], []
    for meta in metas:
        values = meta[...].astype(jnp.float32)
        lanes = lax.broadcasted_iota(jnp.int32, values.shape, 1)
        gates = sum(pltpu.roll(values, LANES - k * top_count, 1) for k in (1, 2, 3))
        amounts = jnp.round(gates * step)
        upper = jnp.floor(amounts * (1.0 / PART))
        lower = amounts - upper * PART
        ids = jnp.where(lanes < top_count, values, -1.0)
        high.append([])
        low.append([])
        for e in range(experts_all):
            chosen = ids == e
            high[-1].append(jnp.sum(jnp.where(chosen, upper, 0.0), 0, keepdims=True))
            low[-1].append(jnp.sum(jnp.where(chosen, lower, 0.0), 0, keepdims=True))
    sums = []
    for part in (high, low):
        rows = [sum(block[e] for block in part) for e in range(experts_all)]
        sums.append(jnp.sum(jnp.concatenate(rows, 0), 1, keepdims=True))
    totals = (sums[0] * PART + sums[1]) * (1.0 / step)
    expert = lax.broadcasted_iota(jnp.int32, (experts_all, LANES), 0)
    owner = lax.broadcasted_iota(jnp.int32, (experts_all, LANES), 1)
    home = expert // per_device
    slot = jnp.zeros_like(home)
    for h in range(owners):
        slot = jnp.where(home == h, swap_slot[h], slot)
    partner = (home + owners // 2) % owners
    holder = jnp.where(expert % per_device == slot, partner, home)
    load_ref[...] = jnp.sum(jnp.where(holder == owner, totals, 0.0), 0, keepdims=True) * scale


def planned_load(metas, swap_slot, owners, per_device, top_count, after):
    count = sum(meta.shape[0] for meta in metas)
    step = 2.0 ** (31 - (count * GATE_MOST).bit_length())
    layout = (owners, per_device, top_count, step, owners / count)
    in_vmem = pl.BlockSpec(memory_space=pltpu.VMEM)
    load = pl.pallas_call(
        lambda *refs: load_kernel(layout, *refs),
        in_specs=[pl.BlockSpec(memory_space=pltpu.SMEM)]
        + [in_vmem] * len(metas)
        + [pl.BlockSpec(memory_space=pl.ANY)],
        out_specs=in_vmem,
        out_shape=jax.ShapeDtypeStruct((1, LANES), jnp.float32),
        compiler_params=pltpu.CompilerParams(vmem_limit_bytes=VMEM_LIMIT),
        cost_estimate=pl.CostEstimate(
            flops=0, bytes_accessed=sum(meta.nbytes for meta in metas), transcendentals=0
        ),
    )(swap_slot, *metas, after)
    return load


def on_device(tokens, expert_ids, gate_probs, in_weight, out_weight, swap_slot):
    groups, chips = lax.axis_size("dp"), lax.axis_size("chip")
    owners = 2 * chips
    per_device = in_weight.shape[0]
    rows, width = tokens.shape
    part = width // 2
    top_count = expert_ids.shape[1]
    half_width = out_weight.shape[1]
    core = lax.axis_index("core")
    first = core == 0
    first_expert = (lax.axis_index("chip") * 2 + core) * per_device
    place = jnp.stack([core, first_expert]).astype(jnp.int32)

    keep, give = first_halves(place, tokens, expert_ids, gate_probs)
    taken = swap(give, "core", 1)
    chip_rows = row_major(
        jnp.concatenate([jnp.where(first, keep, taken), jnp.where(first, taken, keep)], 0)
    )

    def sums_of(own, weights, *mark):
        other = swap(own[:, :part], "core", 1)
        return gated_sums(place, top_count, own, other, *weights, *mark)

    def chip_sums(keep, give):
        return (wide(keep) + wide(swap(give, "core", 1))).astype(jnp.bfloat16)

    chip_blocks = [swap(chip_rows, "chip", j) for j in range(chips - 1, 0, -1)]
    chip_blocks = [chip_rows, *chip_blocks[::-1]]
    direct = [swap(chip_rows, "dp", k) for k in range(1, groups)]
    up, mark = loaded(in_weight, direct[0])
    chip_blocks[1:], mark = lax.optimization_barrier((chip_blocks[1:], mark))
    far = row_major(jnp.concatenate(chip_blocks[1:], 0))
    held = row_major(jnp.concatenate([*chip_blocks, *direct], 0))
    near = spread_near(far)
    weights = [up, out_weight.reshape(per_device * half_width, width)]
    pieces = [held]
    if held.shape[0] > MOST_ROWS:
        pieces = [row_major(jnp.concatenate(chip_blocks, 0)), *direct]
    keep, give, weights[1] = sums_of(pieces[0], weights, mark)
    later = [sums_of(piece, weights) for piece in pieces[1:]]
    if later:
        keep, give = (jnp.concatenate(x, 0) for x in zip((keep, give), *later))
    first_sum = chip_sums(keep, give)
    near = behind(near, give)
    border = chips * 2 * rows
    near_sums = [first_sum[: 2 * rows]]
    near_sums += [
        first_sum[low : low + 2 * rows] for low in range(border, first_sum.shape[0], 2 * rows)
    ]
    far_sums = [first_sum[2 * rows : border]]

    def parts(block):
        return [block[low : low + 2 * rows] for low in range(0, block.shape[0], 2 * rows)]

    def along_chips(blocks):
        return [swap(blocks[j - 1], "chip", j) for j in range(chips - 1, 0, -1)]

    if groups == 4:
        rest = cross(jnp.where(first, near[0], near[1]))
        near = row_major(jnp.concatenate(near, 0))
        keep, give = sums_of(near, weights)
        far_sums += [*jnp.split(chip_sums(keep, give), 2)]
        whole = [jnp.concatenate(pair, 0) for pair in zip(near_sums, far_sums)]
        rest = behind(rest, give)
        other = behind(swap(rest[:, :part], "core", 1), whole[1:3])
        keep, give = gated_sums_in_steps(place, top_count, rest, other, *weights)
        fourth = parts(added(keep, swap(give, "core", 1)))
        fourth = along_chips(fourth)
        metas = [held, near, rest]
    else:
        far_sums += [chip_sums(*sums_of(block, weights)) for block in near]
        whole = [jnp.concatenate(pair, 0) for pair in zip(near_sums, far_sums)]
        fourth = []
        metas = [held, *near]
    metas = [block[:, block.shape[1] - LANES :] for block in metas]
    total = collected(whole[0], received(whole))
    came = []
    if fourth:
        fourth = collected(near_sums[3], behind(fourth, total))
        came = [swap(fourth, "dp", 3)]
    total = parts(total)
    load = planned_load(metas, swap_slot, owners, per_device, top_count, total[0])
    total = collected(total[0], along_chips(total[1:]) + came)
    upper, lower = total[:rows], total[rows:]
    arrived = swap(jnp.where(first, lower, upper), "core", 1)
    kept = jnp.where(first, upper, lower)
    mixed_out = row_major(
        jnp.concatenate([jnp.where(first, kept, arrived), jnp.where(first, arrived, kept)], 1)
    )

    return (mixed_out, load[0, :owners])


def solution(mesh):
    groups, owners = mesh.devices.shape
    fine = Mesh(mesh.devices.reshape(groups, owners // 2, 2), ("dp", "chip", "core"))
    rows = P(("dp", "chip", "core"), None)
    return jax.shard_map(
        on_device,
        mesh=fine,
        in_specs=(
            rows,
            rows,
            rows,
            P(("chip", "core"), None, "dp"),
            P(("chip", "core"), "dp", None),
            P(),
        ),
        out_specs=(rows, P()),
        check_vma=False,
    )
```

```python
import jax
import jax.numpy as jnp
from jax import lax
from jax.experimental import pallas as pl
from jax.experimental.pallas import tpu as pltpu
from jax.experimental.layout import Layout, with_layout_constraint
from jax.sharding import Mesh, PartitionSpec as P

LANES = 128
PART = 1024.0
CHUNK = 1024
MOST_ROWS = 512
VMEM_LIMIT = 12 * 2**20
GATE_MOST = 5


def row_major(value):
    return with_layout_constraint(value, Layout(major_to_minor=tuple(range(value.ndim))))


def swap(value, axis, distance):
    size = lax.axis_size(axis)
    pairs = [(i, i ^ distance) for i in range(size)]
    return row_major(lax.ppermute(row_major(value), axis, pairs))


def spread_near(block):
    size = lax.axis_size("dp")
    return [swap(block, "dp", k) for k in range(1, 3 if size == 4 else size)]


def behind(values, others):
    return lax.optimization_barrier((values, others))[0]


def wide(value):
    return value.astype(jnp.float32)


def received(blocks):
    return [swap(block, "dp", k) for k, block in enumerate(blocks[1:], 1)]


def collected(own, others):
    return sum([wide(block) for block in others], wide(own)).astype(jnp.bfloat16)


def load_weight_kernel(weight_ref, _, weight_out, mark_ref, sem):
    copy = pltpu.make_async_copy(weight_ref, weight_out, sem)
    copy.start()
    mark_ref[...] = jnp.zeros_like(mark_ref)
    copy.wait()


def loaded(weight, after):
    return pl.pallas_call(
        load_weight_kernel,
        in_specs=[pl.BlockSpec(memory_space=pl.ANY)] * 2,
        out_specs=[pl.BlockSpec(memory_space=pltpu.VMEM)] * 2,
        out_shape=[
            pltpu.VMEM(weight.shape, weight.dtype),
            pltpu.VMEM((8, LANES), jnp.float32),
        ],
        scratch_shapes=[pltpu.SemaphoreType.DMA],
        compiler_params=pltpu.CompilerParams(vmem_limit_bytes=VMEM_LIMIT),
        cost_estimate=pl.CostEstimate(flops=0, bytes_accessed=weight.nbytes, transcendentals=0),
    )(pltpu.with_memory_space_constraint(weight, pltpu.HBM), after)


def joined(blocks):
    return blocks[0] if len(blocks) == 1 else jnp.concatenate(blocks, 0)


def add_up(acc, segments, widths, up, base):
    for blocks, width in zip(segments, widths):
        for low in range(0, width, CHUNK):
            held = joined([block[:, low : low + CHUNK] for block in blocks])
            rows = pl.ds(pl.multiple_of(base, CHUNK), CHUNK)
            for s in range(up.shape[0]):
                acc[s] += jnp.dot(held, up[s, rows], preferred_element_type=jnp.float32)
            base = base + CHUNK


def make_hidden(hidden, acc, routed, width, first_expert, top_count):
    meta = joined([block[:, width:].astype(jnp.float32) for block in routed])
    gates = sum(pltpu.roll(meta, LANES - k * top_count, 1) for k in (1, 2, 3))
    lanes = lax.broadcasted_iota(jnp.int32, meta.shape, 1)
    half_width = acc.shape[2] // 2
    for s in range(acc.shape[0]):
        chosen = (meta.astype(jnp.int32) == first_expert + s) & (lanes < top_count)
        own_gate = jnp.sum(jnp.where(chosen, gates, 0.0), 1, keepdims=True)
        gate_half, up_half = acc[s, :, :half_width], acc[s, :, half_width:]
        unit = gate_half * (1.0 / (1.0 + jnp.exp(-gate_half))) * up_half
        hidden[:, s * half_width : (s + 1) * half_width] = (unit * own_gate).astype(jnp.bfloat16)


def multiply_down(out, hidden, down, base):
    for low in range(0, out.shape[1], CHUNK):
        columns = pl.ds(pl.multiple_of(base + low, CHUNK), CHUNK)
        out[:, low : low + CHUNK] = jnp.dot(
            hidden[...], down[:, columns], preferred_element_type=jnp.float32
        ).astype(jnp.bfloat16)


def sums_kernel(top_count, filling, place, own, other, up, *refs):
    if filling:
        down_ref, _, keep_ref, give_ref, down, acc, hidden, sem = refs
        copy = pltpu.make_async_copy(down_ref, down, sem)
        copy.start()
    else:
        down, keep_ref, give_ref, acc, hidden = refs
    part = other.shape[1]
    bases = [place[0] * part, (1 - place[0]) * part]
    acc[...] = jnp.zeros_like(acc)
    add_up(acc, [[own]], [part], up, bases[0])
    add_up(acc, [[other]], [part], up, bases[1])
    make_hidden(hidden, acc, [own], part, place[1], top_count)
    if filling:
        copy.wait()
    multiply_down(give_ref, hidden, down, bases[1])
    multiply_down(keep_ref, hidden, down, bases[0])


def own_kernel(place, own, up, acc):
    part = up.shape[1] // 2
    acc[...] = jnp.zeros_like(acc)
    add_up(acc, [[own]], [part], up, place[0] * part)


def give_kernel(top_count, place, own, other, held, up, down, give_ref, hidden, acc):
    part = other.shape[1]
    base = (1 - place[0]) * part
    acc[...] = held[...]
    add_up(acc, [[other]], [part], up, base)
    make_hidden(hidden, acc, [own], part, place[1], top_count)
    multiply_down(give_ref, hidden, down, base)


def keep_kernel(place, hidden, down, keep_ref):
    multiply_down(keep_ref, hidden, down, place[0] * keep_ref.shape[1])


def call(kernel, operands, out_shape, scratch_shapes=(), flops=0, unplaced=0):
    in_vmem = pl.BlockSpec(memory_space=pltpu.VMEM)
    place, *arrays = operands
    split = len(arrays) - unplaced
    return pl.pallas_call(
        kernel,
        in_specs=[pl.BlockSpec(memory_space=pltpu.SMEM)]
        + [in_vmem] * split
        + [pl.BlockSpec(memory_space=pl.ANY)] * unplaced,
        out_specs=[in_vmem] * len(out_shape),
        out_shape=out_shape,
        scratch_shapes=list(scratch_shapes),
        compiler_params=pltpu.CompilerParams(vmem_limit_bytes=VMEM_LIMIT),
        cost_estimate=pl.CostEstimate(flops=flops, bytes_accessed=0, transcendentals=0),
    )(
        place,
        *(pltpu.with_memory_space_constraint(x, pltpu.VMEM) for x in arrays[:split]),
        *arrays[split:],
    )


def gated_sums(place, top_count, own, other, up, down, mark=None):
    count, part = other.shape
    filling = mark is not None
    out = pltpu.VMEM((count, part), jnp.bfloat16)
    out_shape = [out, out]
    scratch = [
        pltpu.VMEM((up.shape[0], count, up.shape[2]), jnp.float32),
        pltpu.VMEM((count, down.shape[0]), jnp.bfloat16),
    ]
    operands = [place, own, other, up, down]
    if filling:
        operands[-1:] = [pltpu.with_memory_space_constraint(down, pltpu.HBM), mark]
        out_shape.append(pltpu.VMEM(down.shape, down.dtype))
        scratch.append(pltpu.SemaphoreType.DMA)
    return call(
        lambda *refs: sums_kernel(top_count, filling, *refs),
        operands,
        out_shape,
        scratch,
        flops=2 * count * (up.size + down.size),
        unplaced=2 if filling else 0,
    )


def gated_sums_in_steps(place, top_count, own, other, up, down):
    count, part = other.shape
    acc_shape = (up.shape[0], count, up.shape[2])
    (held,) = call(
        own_kernel,
        [place, own, up],
        [pltpu.VMEM(acc_shape, jnp.float32)],
        flops=count * up.size,
    )
    give, hidden = call(
        lambda *refs: give_kernel(top_count, *refs),
        [place, own, other, held, up, down],
        [
            pltpu.VMEM((count, part), jnp.bfloat16),
            pltpu.VMEM((count, down.shape[0]), jnp.bfloat16),
        ],
        [pltpu.VMEM(acc_shape, jnp.float32)],
        flops=count * (up.size + down.size),
    )
    (keep,) = call(
        keep_kernel,
        [place, hidden, down],
        [pltpu.VMEM((count, part), jnp.bfloat16)],
        flops=count * down.size,
    )
    return keep, give


def first_kernel(place, *refs):
    sources, (keep_ref, give_ref, tokens, ids, gates, turned, sems) = refs[:3], refs[3:]
    copies = [
        pltpu.make_async_copy(source, target, sems.at[number])
        for number, (source, target) in enumerate(zip(sources, (tokens, ids, gates)))
    ]
    for copy in copies:
        copy.start()
    for copy in copies:
        copy.wait()
    core = place[0]
    part = tokens.shape[1] // 2
    top_count, rows = ids.shape
    turned[...] = jnp.zeros_like(turned)
    left = gates[...]
    parts = [ids[...].astype(jnp.float32)]
    for _ in range(3):
        parts.append(left.astype(jnp.bfloat16).astype(jnp.float32))
        left = left - parts[-1]
    for number, values in enumerate(parts):
        turned[number * top_count : (number + 1) * top_count, :rows] = values
    routing = turned[...].T[:rows].astype(jnp.bfloat16)
    for half, out in ((core, keep_ref), (1 - core, give_ref)):
        out[:, :part] = tokens[:, pl.ds(pl.multiple_of(half * part, LANES), part)]
        out[:, part:] = routing


def first_halves(place, tokens, expert_ids, gate_probs):
    rows, width = tokens.shape
    sources = [tokens, expert_ids.T, gate_probs.T]
    return pl.pallas_call(
        first_kernel,
        in_specs=[pl.BlockSpec(memory_space=pltpu.SMEM)]
        + [pl.BlockSpec(memory_space=pl.ANY)] * 3,
        out_specs=[pl.BlockSpec(memory_space=pltpu.VMEM)] * 2,
        out_shape=[pltpu.VMEM((rows, width // 2 + LANES), jnp.bfloat16)] * 2,
        scratch_shapes=[pltpu.VMEM(x.shape, x.dtype) for x in sources]
        + [pltpu.VMEM((LANES, LANES), jnp.float32), pltpu.SemaphoreType.DMA((3,))],
        compiler_params=pltpu.CompilerParams(vmem_limit_bytes=VMEM_LIMIT),
    )(place, *(pltpu.with_memory_space_constraint(x, pltpu.HBM) for x in sources))


def added_kernel(kept_ref, taken_ref, total_ref):
    total = kept_ref[...].astype(jnp.float32) + taken_ref[...].astype(jnp.float32)
    total_ref[...] = total.astype(jnp.bfloat16)


def added(kept, taken):
    in_vmem = pl.BlockSpec(memory_space=pltpu.VMEM)
    return pl.pallas_call(
        added_kernel,
        in_specs=[in_vmem] * 2,
        out_specs=in_vmem,
        out_shape=pltpu.VMEM(kept.shape, jnp.bfloat16),
        compiler_params=pltpu.CompilerParams(vmem_limit_bytes=VMEM_LIMIT),
    )(*(pltpu.with_memory_space_constraint(x, pltpu.VMEM) for x in (kept, taken)))


def load_kernel(layout, swap_slot, *refs):
    owners, per_device, top_count, step, scale = layout
    *metas, _, load_ref = refs
    experts_all = owners * per_device
    high, low = [], []
    for meta in metas:
        values = meta[...].astype(jnp.float32)
        lanes = lax.broadcasted_iota(jnp.int32, values.shape, 1)
        gates = sum(pltpu.roll(values, LANES - k * top_count, 1) for k in (1, 2, 3))
        amounts = jnp.round(gates * step)
        upper = jnp.floor(amounts * (1.0 / PART))
        lower = amounts - upper * PART
        ids = jnp.where(lanes < top_count, values, -1.0)
        high.append([])
        low.append([])
        for e in range(experts_all):
            chosen = ids == e
            high[-1].append(jnp.sum(jnp.where(chosen, upper, 0.0), 0, keepdims=True))
            low[-1].append(jnp.sum(jnp.where(chosen, lower, 0.0), 0, keepdims=True))
    sums = []
    for part in (high, low):
        rows = [sum(block[e] for block in part) for e in range(experts_all)]
        sums.append(jnp.sum(jnp.concatenate(rows, 0), 1, keepdims=True))
    totals = (sums[0] * PART + sums[1]) * (1.0 / step)
    expert = lax.broadcasted_iota(jnp.int32, (experts_all, LANES), 0)
    owner = lax.broadcasted_iota(jnp.int32, (experts_all, LANES), 1)
    home = expert // per_device
    slot = jnp.zeros_like(home)
    for h in range(owners):
        slot = jnp.where(home == h, swap_slot[h], slot)
    partner = (home + owners // 2) % owners
    holder = jnp.where(expert % per_device == slot, partner, home)
    load_ref[...] = jnp.sum(jnp.where(holder == owner, totals, 0.0), 0, keepdims=True) * scale


def planned_load(metas, swap_slot, owners, per_device, top_count, after):
    count = sum(meta.shape[0] for meta in metas)
    step = 2.0 ** (31 - (count * GATE_MOST).bit_length())
    layout = (owners, per_device, top_count, step, owners / count)
    in_vmem = pl.BlockSpec(memory_space=pltpu.VMEM)
    load = pl.pallas_call(
        lambda *refs: load_kernel(layout, *refs),
        in_specs=[pl.BlockSpec(memory_space=pltpu.SMEM)]
        + [in_vmem] * len(metas)
        + [pl.BlockSpec(memory_space=pl.ANY)],
        out_specs=in_vmem,
        out_shape=jax.ShapeDtypeStruct((1, LANES), jnp.float32),
        compiler_params=pltpu.CompilerParams(vmem_limit_bytes=VMEM_LIMIT),
        cost_estimate=pl.CostEstimate(
            flops=0, bytes_accessed=sum(meta.nbytes for meta in metas), transcendentals=0
        ),
    )(swap_slot, *metas, after)
    return load


def on_device(tokens, expert_ids, gate_probs, in_weight, out_weight, swap_slot):
    groups, chips = lax.axis_size("dp"), lax.axis_size("chip")
    owners = 2 * chips
    per_device = in_weight.shape[0]
    rows, width = tokens.shape
    part = width // 2
    top_count = expert_ids.shape[1]
    half_width = out_weight.shape[1]
    core = lax.axis_index("core")
    first = core == 0
    first_expert = (lax.axis_index("chip") * 2 + core) * per_device
    place = jnp.stack([core, first_expert]).astype(jnp.int32)

    keep, give = first_halves(place, tokens, expert_ids, gate_probs)
    taken = swap(give, "core", 1)
    chip_rows = row_major(
        jnp.concatenate([jnp.where(first, keep, taken), jnp.where(first, taken, keep)], 0)
    )

    def sums_of(own, weights, *mark):
        other = swap(own[:, :part], "core", 1)
        return gated_sums(place, top_count, own, other, *weights, *mark)

    def chip_sums(keep, give):
        return (wide(keep) + wide(swap(give, "core", 1))).astype(jnp.bfloat16)

    chip_blocks = [swap(chip_rows, "chip", j) for j in range(chips - 1, 0, -1)]
    chip_blocks = [chip_rows, *chip_blocks[::-1]]
    direct = [swap(chip_rows, "dp", k) for k in range(1, groups)]
    up, mark = loaded(in_weight, direct[0])
    chip_blocks[1:], mark = lax.optimization_barrier((chip_blocks[1:], mark))
    far = row_major(jnp.concatenate(chip_blocks[1:], 0))
    held = row_major(jnp.concatenate([*chip_blocks, *direct], 0))
    near = spread_near(far)
    if groups == 4:
        fourth_rows = [swap(direct[2], "chip", j) for j in range(chips - 1, 0, -1)]
        fourth_rows = jnp.concatenate(fourth_rows[::-1], 0)
    weights = [up, out_weight.reshape(per_device * half_width, width)]
    pieces = [held]
    if held.shape[0] > MOST_ROWS:
        pieces = [row_major(jnp.concatenate(chip_blocks, 0)), *direct]
    keep, give, weights[1] = sums_of(pieces[0], weights, mark)
    later = [sums_of(piece, weights) for piece in pieces[1:]]
    if later:
        keep, give = (jnp.concatenate(x, 0) for x in zip((keep, give), *later))
    first_sum = chip_sums(keep, give)
    near = behind(near, give)
    border = chips * 2 * rows
    near_sums = [first_sum[: 2 * rows]]
    near_sums += [
        first_sum[low : low + 2 * rows] for low in range(border, first_sum.shape[0], 2 * rows)
    ]
    far_sums = [first_sum[2 * rows : border]]

    def parts(block):
        return [block[low : low + 2 * rows] for low in range(0, block.shape[0], 2 * rows)]

    def along_chips(blocks):
        return [swap(blocks[j - 1], "chip", j) for j in range(chips - 1, 0, -1)]

    if groups == 4:
        rest = row_major(jnp.concatenate([*near, fourth_rows], 0))
        other = swap(rest[:, :part], "core", 1)
        keep, give = gated_sums_in_steps(place, top_count, rest, other, *weights)
        pair = added(keep, swap(give, "core", 1))
        far_sums += [*jnp.split(pair, 3)]
        whole = [jnp.concatenate(blocks, 0) for blocks in zip(near_sums, far_sums[:3])]
        fourth = parts(far_sums[3])
        fourth = along_chips(fourth)
        metas = [held, rest]
    else:
        far_sums += [chip_sums(*sums_of(block, weights)) for block in near]
        whole = [jnp.concatenate(pair, 0) for pair in zip(near_sums, far_sums)]
        fourth = []
        metas = [held, *near]
    metas = [block[:, block.shape[1] - LANES :] for block in metas]
    total = collected(whole[0], received(whole))
    came = []
    if fourth:
        fourth = collected(near_sums[3], behind(fourth, total))
        came = [swap(fourth, "dp", 3)]
    total = parts(total)
    load = planned_load(metas, swap_slot, owners, per_device, top_count, total[0])
    total = collected(total[0], along_chips(total[1:]) + came)
    upper, lower = total[:rows], total[rows:]
    arrived = swap(jnp.where(first, lower, upper), "core", 1)
    kept = jnp.where(first, upper, lower)
    mixed_out = row_major(
        jnp.concatenate([jnp.where(first, kept, arrived), jnp.where(first, arrived, kept)], 1)
    )

    return (mixed_out, load[0, :owners])


def solution(mesh):
    groups, owners = mesh.devices.shape
    fine = Mesh(mesh.devices.reshape(groups, owners // 2, 2), ("dp", "chip", "core"))
    rows = P(("dp", "chip", "core"), None)
    return jax.shard_map(
        on_device,
        mesh=fine,
        in_specs=(
            rows,
            rows,
            rows,
            P(("chip", "core"), None, "dp"),
            P(("chip", "core"), "dp", None),
            P(),
        ),
        out_specs=(rows, P()),
        check_vma=False,
    )
```

```python
import jax
import jax.numpy as jnp
from jax import lax
from jax.experimental import pallas as pl
from jax.experimental.pallas import tpu as pltpu
from jax.experimental.layout import Layout, with_layout_constraint
from jax.sharding import Mesh, PartitionSpec as P

LANES = 128
PART = 1024.0
CHUNK = 1024
MOST_ROWS = 512
VMEM_LIMIT = 12 * 2**20
GATE_MOST = 5


def row_major(value):
    return with_layout_constraint(value, Layout(major_to_minor=tuple(range(value.ndim))))


def swap(value, axis, distance):
    size = lax.axis_size(axis)
    pairs = [(i, i ^ distance) for i in range(size)]
    return row_major(lax.ppermute(row_major(value), axis, pairs))


def spread_near(block):
    size = lax.axis_size("dp")
    return [swap(block, "dp", k) for k in range(1, 3 if size == 4 else size)]


def behind(values, others):
    return lax.optimization_barrier((values, others))[0]


def wide(value):
    return value.astype(jnp.float32)


def received(blocks):
    return [swap(block, "dp", k) for k, block in enumerate(blocks[1:], 1)]


def collected(own, others):
    return sum([wide(block) for block in others], wide(own)).astype(jnp.bfloat16)


def load_weight_kernel(weight_ref, _, weight_out, mark_ref, sem):
    copy = pltpu.make_async_copy(weight_ref, weight_out, sem)
    copy.start()
    mark_ref[...] = jnp.zeros_like(mark_ref)
    copy.wait()


def loaded(weight, after):
    return pl.pallas_call(
        load_weight_kernel,
        in_specs=[pl.BlockSpec(memory_space=pl.ANY)] * 2,
        out_specs=[pl.BlockSpec(memory_space=pltpu.VMEM)] * 2,
        out_shape=[
            pltpu.VMEM(weight.shape, weight.dtype),
            pltpu.VMEM((8, LANES), jnp.float32),
        ],
        scratch_shapes=[pltpu.SemaphoreType.DMA],
        compiler_params=pltpu.CompilerParams(vmem_limit_bytes=VMEM_LIMIT),
        cost_estimate=pl.CostEstimate(flops=0, bytes_accessed=weight.nbytes, transcendentals=0),
    )(pltpu.with_memory_space_constraint(weight, pltpu.HBM), after)


def joined(blocks):
    return blocks[0] if len(blocks) == 1 else jnp.concatenate(blocks, 0)


def add_up(acc, segments, widths, up, base):
    for blocks, width in zip(segments, widths):
        for low in range(0, width, CHUNK):
            held = joined([block[:, low : low + CHUNK] for block in blocks])
            rows = pl.ds(pl.multiple_of(base, CHUNK), CHUNK)
            for s in range(up.shape[0]):
                acc[s] += jnp.dot(held, up[s, rows], preferred_element_type=jnp.float32)
            base = base + CHUNK


def make_hidden(hidden, acc, routed, width, first_expert, top_count):
    meta = joined([block[:, width:].astype(jnp.float32) for block in routed])
    gates = sum(pltpu.roll(meta, LANES - k * top_count, 1) for k in (1, 2, 3))
    lanes = lax.broadcasted_iota(jnp.int32, meta.shape, 1)
    half_width = acc.shape[2] // 2
    for s in range(acc.shape[0]):
        chosen = (meta.astype(jnp.int32) == first_expert + s) & (lanes < top_count)
        own_gate = jnp.sum(jnp.where(chosen, gates, 0.0), 1, keepdims=True)
        gate_half, up_half = acc[s, :, :half_width], acc[s, :, half_width:]
        unit = gate_half * (1.0 / (1.0 + jnp.exp(-gate_half))) * up_half
        hidden[:, s * half_width : (s + 1) * half_width] = (unit * own_gate).astype(jnp.bfloat16)


def multiply_down(out, hidden, down, base):
    for low in range(0, out.shape[1], CHUNK):
        columns = pl.ds(pl.multiple_of(base + low, CHUNK), CHUNK)
        out[:, low : low + CHUNK] = jnp.dot(
            hidden[...], down[:, columns], preferred_element_type=jnp.float32
        ).astype(jnp.bfloat16)


def sums_kernel(top_count, filling, place, own, other, up, *refs):
    if filling:
        down_ref, _, keep_ref, give_ref, down, acc, hidden, sem = refs
        copy = pltpu.make_async_copy(down_ref, down, sem)
        copy.start()
    else:
        down, keep_ref, give_ref, acc, hidden = refs
    part = other.shape[1]
    bases = [place[0] * part, (1 - place[0]) * part]
    acc[...] = jnp.zeros_like(acc)
    add_up(acc, [[own]], [part], up, bases[0])
    add_up(acc, [[other]], [part], up, bases[1])
    make_hidden(hidden, acc, [own], part, place[1], top_count)
    if filling:
        copy.wait()
    multiply_down(give_ref, hidden, down, bases[1])
    multiply_down(keep_ref, hidden, down, bases[0])


def own_kernel(place, own, up, acc):
    part = up.shape[1] // 2
    acc[...] = jnp.zeros_like(acc)
    add_up(acc, [[own]], [part], up, place[0] * part)


def give_kernel(top_count, place, own, other, held, up, down, give_ref, hidden, acc):
    part = other.shape[1]
    base = (1 - place[0]) * part
    acc[...] = held[...]
    add_up(acc, [[other]], [part], up, base)
    make_hidden(hidden, acc, [own], part, place[1], top_count)
    multiply_down(give_ref, hidden, down, base)


def keep_kernel(place, hidden, down, keep_ref):
    multiply_down(keep_ref, hidden, down, place[0] * keep_ref.shape[1])


def call(kernel, operands, out_shape, scratch_shapes=(), flops=0, unplaced=0):
    in_vmem = pl.BlockSpec(memory_space=pltpu.VMEM)
    place, *arrays = operands
    split = len(arrays) - unplaced
    return pl.pallas_call(
        kernel,
        in_specs=[pl.BlockSpec(memory_space=pltpu.SMEM)]
        + [in_vmem] * split
        + [pl.BlockSpec(memory_space=pl.ANY)] * unplaced,
        out_specs=[in_vmem] * len(out_shape),
        out_shape=out_shape,
        scratch_shapes=list(scratch_shapes),
        compiler_params=pltpu.CompilerParams(vmem_limit_bytes=VMEM_LIMIT),
        cost_estimate=pl.CostEstimate(flops=flops, bytes_accessed=0, transcendentals=0),
    )(
        place,
        *(pltpu.with_memory_space_constraint(x, pltpu.VMEM) for x in arrays[:split]),
        *arrays[split:],
    )


def gated_sums(place, top_count, own, other, up, down, mark=None):
    count, part = other.shape
    filling = mark is not None
    out = pltpu.VMEM((count, part), jnp.bfloat16)
    out_shape = [out, out]
    scratch = [
        pltpu.VMEM((up.shape[0], count, up.shape[2]), jnp.float32),
        pltpu.VMEM((count, down.shape[0]), jnp.bfloat16),
    ]
    operands = [place, own, other, up, down]
    if filling:
        operands[-1:] = [pltpu.with_memory_space_constraint(down, pltpu.HBM), mark]
        out_shape.append(pltpu.VMEM(down.shape, down.dtype))
        scratch.append(pltpu.SemaphoreType.DMA)
    return call(
        lambda *refs: sums_kernel(top_count, filling, *refs),
        operands,
        out_shape,
        scratch,
        flops=2 * count * (up.size + down.size),
        unplaced=2 if filling else 0,
    )


def gated_sums_in_steps(place, top_count, own, other, up, down):
    count, part = other.shape
    acc_shape = (up.shape[0], count, up.shape[2])
    (held,) = call(
        own_kernel,
        [place, own, up],
        [pltpu.VMEM(acc_shape, jnp.float32)],
        flops=count * up.size,
    )
    give, hidden = call(
        lambda *refs: give_kernel(top_count, *refs),
        [place, own, other, held, up, down],
        [
            pltpu.VMEM((count, part), jnp.bfloat16),
            pltpu.VMEM((count, down.shape[0]), jnp.bfloat16),
        ],
        [pltpu.VMEM(acc_shape, jnp.float32)],
        flops=count * (up.size + down.size),
    )
    (keep,) = call(
        keep_kernel,
        [place, hidden, down],
        [pltpu.VMEM((count, part), jnp.bfloat16)],
        flops=count * down.size,
    )
    return keep, give


def first_kernel(place, *refs):
    sources, (keep_ref, give_ref, tokens, ids, gates, turned, sems) = refs[:3], refs[3:]
    copies = [
        pltpu.make_async_copy(source, target, sems.at[number])
        for number, (source, target) in enumerate(zip(sources, (tokens, ids, gates)))
    ]
    for copy in copies:
        copy.start()
    for copy in copies:
        copy.wait()
    core = place[0]
    part = tokens.shape[1] // 2
    top_count, rows = ids.shape
    turned[...] = jnp.zeros_like(turned)
    left = gates[...]
    parts = [ids[...].astype(jnp.float32)]
    for _ in range(3):
        parts.append(left.astype(jnp.bfloat16).astype(jnp.float32))
        left = left - parts[-1]
    for number, values in enumerate(parts):
        turned[number * top_count : (number + 1) * top_count, :rows] = values
    routing = turned[...].T[:rows].astype(jnp.bfloat16)
    for half, out in ((core, keep_ref), (1 - core, give_ref)):
        out[:, :part] = tokens[:, pl.ds(pl.multiple_of(half * part, LANES), part)]
        out[:, part:] = routing


def first_halves(place, tokens, expert_ids, gate_probs):
    rows, width = tokens.shape
    sources = [tokens, expert_ids.T, gate_probs.T]
    return pl.pallas_call(
        first_kernel,
        in_specs=[pl.BlockSpec(memory_space=pltpu.SMEM)]
        + [pl.BlockSpec(memory_space=pl.ANY)] * 3,
        out_specs=[pl.BlockSpec(memory_space=pltpu.VMEM)] * 2,
        out_shape=[pltpu.VMEM((rows, width // 2 + LANES), jnp.bfloat16)] * 2,
        scratch_shapes=[pltpu.VMEM(x.shape, x.dtype) for x in sources]
        + [pltpu.VMEM((LANES, LANES), jnp.float32), pltpu.SemaphoreType.DMA((3,))],
        compiler_params=pltpu.CompilerParams(vmem_limit_bytes=VMEM_LIMIT),
    )(place, *(pltpu.with_memory_space_constraint(x, pltpu.HBM) for x in sources))


def added_kernel(kept_ref, taken_ref, total_ref):
    total = kept_ref[...].astype(jnp.float32) + taken_ref[...].astype(jnp.float32)
    total_ref[...] = total.astype(jnp.bfloat16)


def added(kept, taken):
    in_vmem = pl.BlockSpec(memory_space=pltpu.VMEM)
    return pl.pallas_call(
        added_kernel,
        in_specs=[in_vmem] * 2,
        out_specs=in_vmem,
        out_shape=pltpu.VMEM(kept.shape, jnp.bfloat16),
        compiler_params=pltpu.CompilerParams(vmem_limit_bytes=VMEM_LIMIT),
    )(*(pltpu.with_memory_space_constraint(x, pltpu.VMEM) for x in (kept, taken)))


def load_kernel(layout, swap_slot, *refs):
    owners, per_device, top_count, step, scale = layout
    *metas, _, load_ref = refs
    experts_all = owners * per_device
    high, low = [], []
    for meta in metas:
        values = meta[...].astype(jnp.float32)
        lanes = lax.broadcasted_iota(jnp.int32, values.shape, 1)
        gates = sum(pltpu.roll(values, LANES - k * top_count, 1) for k in (1, 2, 3))
        amounts = jnp.round(gates * step)
        upper = jnp.floor(amounts * (1.0 / PART))
        lower = amounts - upper * PART
        ids = jnp.where(lanes < top_count, values, -1.0)
        high.append([])
        low.append([])
        for e in range(experts_all):
            chosen = ids == e
            high[-1].append(jnp.sum(jnp.where(chosen, upper, 0.0), 0, keepdims=True))
            low[-1].append(jnp.sum(jnp.where(chosen, lower, 0.0), 0, keepdims=True))
    sums = []
    for part in (high, low):
        rows = [sum(block[e] for block in part) for e in range(experts_all)]
        sums.append(jnp.sum(jnp.concatenate(rows, 0), 1, keepdims=True))
    totals = (sums[0] * PART + sums[1]) * (1.0 / step)
    expert = lax.broadcasted_iota(jnp.int32, (experts_all, LANES), 0)
    owner = lax.broadcasted_iota(jnp.int32, (experts_all, LANES), 1)
    home = expert // per_device
    slot = jnp.zeros_like(home)
    for h in range(owners):
        slot = jnp.where(home == h, swap_slot[h], slot)
    partner = (home + owners // 2) % owners
    holder = jnp.where(expert % per_device == slot, partner, home)
    load_ref[...] = jnp.sum(jnp.where(holder == owner, totals, 0.0), 0, keepdims=True) * scale


def planned_load(metas, swap_slot, owners, per_device, top_count, after):
    count = sum(meta.shape[0] for meta in metas)
    step = 2.0 ** (31 - (count * GATE_MOST).bit_length())
    layout = (owners, per_device, top_count, step, owners / count)
    in_vmem = pl.BlockSpec(memory_space=pltpu.VMEM)
    load = pl.pallas_call(
        lambda *refs: load_kernel(layout, *refs),
        in_specs=[pl.BlockSpec(memory_space=pltpu.SMEM)]
        + [in_vmem] * len(metas)
        + [pl.BlockSpec(memory_space=pl.ANY)],
        out_specs=in_vmem,
        out_shape=jax.ShapeDtypeStruct((1, LANES), jnp.float32),
        compiler_params=pltpu.CompilerParams(vmem_limit_bytes=VMEM_LIMIT),
        cost_estimate=pl.CostEstimate(
            flops=0, bytes_accessed=sum(meta.nbytes for meta in metas), transcendentals=0
        ),
    )(swap_slot, *metas, after)
    return load


def on_device(tokens, expert_ids, gate_probs, in_weight, out_weight, swap_slot):
    groups, chips = lax.axis_size("dp"), lax.axis_size("chip")
    owners = 2 * chips
    per_device = in_weight.shape[0]
    rows, width = tokens.shape
    part = width // 2
    top_count = expert_ids.shape[1]
    half_width = out_weight.shape[1]
    core = lax.axis_index("core")
    first = core == 0
    first_expert = (lax.axis_index("chip") * 2 + core) * per_device
    place = jnp.stack([core, first_expert]).astype(jnp.int32)

    keep, give = first_halves(place, tokens, expert_ids, gate_probs)
    taken = swap(give, "core", 1)
    chip_rows = row_major(
        jnp.concatenate([jnp.where(first, keep, taken), jnp.where(first, taken, keep)], 0)
    )

    def sums_of(own, weights, *mark):
        other = swap(own[:, :part], "core", 1)
        return gated_sums(place, top_count, own, other, *weights, *mark)

    def chip_sums(keep, give):
        return (wide(keep) + wide(swap(give, "core", 1))).astype(jnp.bfloat16)

    chip_blocks = [swap(chip_rows, "chip", j) for j in range(chips - 1, 0, -1)]
    chip_blocks = [chip_rows, *chip_blocks[::-1]]
    direct = [swap(chip_rows, "dp", k) for k in range(1, groups)]
    up, mark = loaded(in_weight, direct[0])
    chip_blocks[1:], mark = lax.optimization_barrier((chip_blocks[1:], mark))
    far = row_major(jnp.concatenate(chip_blocks[1:], 0))
    held = row_major(jnp.concatenate([*chip_blocks, *direct], 0))
    near = spread_near(far)
    if groups == 4:
        fourth_rows = [swap(direct[2], "chip", j) for j in range(chips - 1, 0, -1)]
        fourth_rows = jnp.concatenate(fourth_rows[::-1], 0)
    weights = [up, out_weight.reshape(per_device * half_width, width)]
    pieces = [held]
    if held.shape[0] > MOST_ROWS:
        pieces = [row_major(jnp.concatenate(chip_blocks, 0)), *direct]
    keep, give, weights[1] = sums_of(pieces[0], weights, mark)
    later = [sums_of(piece, weights) for piece in pieces[1:]]
    if later:
        keep, give = (jnp.concatenate(x, 0) for x in zip((keep, give), *later))
    first_sum = chip_sums(keep, give)
    near = behind(near, give)
    border = chips * 2 * rows
    near_sums = [first_sum[: 2 * rows]]
    near_sums += [
        first_sum[low : low + 2 * rows] for low in range(border, first_sum.shape[0], 2 * rows)
    ]
    far_sums = [first_sum[2 * rows : border]]

    def parts(block):
        return [block[low : low + 2 * rows] for low in range(0, block.shape[0], 2 * rows)]

    def along_chips(blocks):
        return [swap(blocks[j - 1], "chip", j) for j in range(chips - 1, 0, -1)]

    if groups == 4:
        rest = row_major(jnp.concatenate([*near, fourth_rows], 0))
        other = swap(rest[:, :part], "core", 1)
        keep, give = gated_sums_in_steps(place, top_count, rest, other, *weights)
        pair = added(keep, swap(give, "core", 1))
        far_sums += [*jnp.split(pair, 3)]
        whole = [jnp.concatenate(blocks, 0) for blocks in zip(near_sums, far_sums[:3])]
        fourth = parts(far_sums[3])
        fourth = along_chips(fourth)
        metas = [held, rest]
    else:
        far_sums += [chip_sums(*sums_of(block, weights)) for block in near]
        whole = [jnp.concatenate(pair, 0) for pair in zip(near_sums, far_sums)]
        fourth = []
        metas = [held, *near]
    metas = [block[:, block.shape[1] - LANES :] for block in metas]
    total = parts(collected(whole[0], received(whole)))
    came = along_chips(total[1:])
    if fourth:
        fourth = collected(near_sums[3], behind(fourth, came[-1]))
        came.append(swap(fourth, "dp", 3))
    load = planned_load(metas, swap_slot, owners, per_device, top_count, total[0])
    total = collected(total[0], came)
    upper, lower = total[:rows], total[rows:]
    arrived = swap(jnp.where(first, lower, upper), "core", 1)
    kept = jnp.where(first, upper, lower)
    mixed_out = row_major(
        jnp.concatenate([jnp.where(first, kept, arrived), jnp.where(first, arrived, kept)], 1)
    )

    return (mixed_out, load[0, :owners])


def solution(mesh):
    groups, owners = mesh.devices.shape
    fine = Mesh(mesh.devices.reshape(groups, owners // 2, 2), ("dp", "chip", "core"))
    rows = P(("dp", "chip", "core"), None)
    return jax.shard_map(
        on_device,
        mesh=fine,
        in_specs=(
            rows,
            rows,
            rows,
            P(("chip", "core"), None, "dp"),
            P(("chip", "core"), "dp", None),
            P(),
        ),
        out_specs=(rows, P()),
        check_vma=False,
    )
```

```python
import jax
import jax.numpy as jnp
from jax import lax
from jax.experimental import pallas as pl
from jax.experimental.pallas import tpu as pltpu
from jax.experimental.layout import Layout, with_layout_constraint
from jax.sharding import Mesh, PartitionSpec as P

LANES = 128
PART = 1024.0
CHUNK = 1024
MOST_ROWS = 512
VMEM_LIMIT = 12 * 2**20
GATE_MOST = 5


def row_major(value):
    return with_layout_constraint(value, Layout(major_to_minor=tuple(range(value.ndim))))


def swap(value, axis, distance):
    size = lax.axis_size(axis)
    pairs = [(i, i ^ distance) for i in range(size)]
    return row_major(lax.ppermute(row_major(value), axis, pairs))


def spread_near(block):
    size = lax.axis_size("dp")
    return [swap(block, "dp", k) for k in range(1, 3 if size == 4 else size)]


def behind(values, others):
    return lax.optimization_barrier((values, others))[0]


def wide(value):
    return value.astype(jnp.float32)


def received(blocks):
    return [swap(block, "dp", k) for k, block in enumerate(blocks[1:], 1)]


def collected(own, others):
    return sum([wide(block) for block in others], wide(own)).astype(jnp.bfloat16)


def load_weights_kernel(up_ref, down_ref, _, up_out, down_out, mark_ref, sems):
    copies = [
        pltpu.make_async_copy(up_ref, up_out, sems.at[0]),
        pltpu.make_async_copy(down_ref, down_out, sems.at[1]),
    ]
    for copy in copies:
        copy.start()
    mark_ref[...] = jnp.zeros_like(mark_ref)
    for copy in copies:
        copy.wait()


def loaded(up, down, after):
    return pl.pallas_call(
        load_weights_kernel,
        in_specs=[pl.BlockSpec(memory_space=pl.ANY)] * 3,
        out_specs=[pl.BlockSpec(memory_space=pltpu.VMEM)] * 3,
        out_shape=[
            pltpu.VMEM(up.shape, up.dtype),
            pltpu.VMEM(down.shape, down.dtype),
            pltpu.VMEM((8, LANES), jnp.float32),
        ],
        scratch_shapes=[pltpu.SemaphoreType.DMA((2,))],
        compiler_params=pltpu.CompilerParams(vmem_limit_bytes=VMEM_LIMIT),
        cost_estimate=pl.CostEstimate(
            flops=0, bytes_accessed=up.nbytes + down.nbytes, transcendentals=0
        ),
    )(*(pltpu.with_memory_space_constraint(x, pltpu.HBM) for x in (up, down)), after)


def joined(blocks):
    return blocks[0] if len(blocks) == 1 else jnp.concatenate(blocks, 0)


def add_up(acc, segments, widths, up, base):
    for blocks, width in zip(segments, widths):
        for low in range(0, width, CHUNK):
            held = joined([block[:, low : low + CHUNK] for block in blocks])
            rows = pl.ds(pl.multiple_of(base, CHUNK), CHUNK)
            for s in range(up.shape[0]):
                acc[s] += jnp.dot(held, up[s, rows], preferred_element_type=jnp.float32)
            base = base + CHUNK


def make_hidden(hidden, acc, routed, width, first_expert, top_count):
    meta = joined([block[:, width:].astype(jnp.float32) for block in routed])
    gates = sum(pltpu.roll(meta, LANES - k * top_count, 1) for k in (1, 2, 3))
    lanes = lax.broadcasted_iota(jnp.int32, meta.shape, 1)
    half_width = acc.shape[2] // 2
    for s in range(acc.shape[0]):
        chosen = (meta.astype(jnp.int32) == first_expert + s) & (lanes < top_count)
        own_gate = jnp.sum(jnp.where(chosen, gates, 0.0), 1, keepdims=True)
        gate_half, up_half = acc[s, :, :half_width], acc[s, :, half_width:]
        unit = gate_half * (1.0 / (1.0 + jnp.exp(-gate_half))) * up_half
        hidden[:, s * half_width : (s + 1) * half_width] = (unit * own_gate).astype(jnp.bfloat16)


def multiply_down(out, hidden, down, base):
    for low in range(0, out.shape[1], CHUNK):
        columns = pl.ds(pl.multiple_of(base + low, CHUNK), CHUNK)
        out[:, low : low + CHUNK] = jnp.dot(
            hidden[...], down[:, columns], preferred_element_type=jnp.float32
        ).astype(jnp.bfloat16)


def sums_kernel(top_count, place, own, other, up, down, *refs):
    keep_ref, give_ref, acc, hidden = refs[-4:]
    part = other.shape[1]
    bases = [place[0] * part, (1 - place[0]) * part]
    acc[...] = jnp.zeros_like(acc)
    add_up(acc, [[own]], [part], up, bases[0])
    add_up(acc, [[other]], [part], up, bases[1])
    make_hidden(hidden, acc, [own], part, place[1], top_count)
    multiply_down(give_ref, hidden, down, bases[1])
    multiply_down(keep_ref, hidden, down, bases[0])


def own_kernel(place, own, up, acc):
    part = up.shape[1] // 2
    acc[...] = jnp.zeros_like(acc)
    add_up(acc, [[own]], [part], up, place[0] * part)


def give_kernel(top_count, place, own, other, held, up, down, give_ref, hidden, acc):
    part = other.shape[1]
    base = (1 - place[0]) * part
    acc[...] = held[...]
    add_up(acc, [[other]], [part], up, base)
    make_hidden(hidden, acc, [own], part, place[1], top_count)
    multiply_down(give_ref, hidden, down, base)


def keep_kernel(place, hidden, down, keep_ref):
    multiply_down(keep_ref, hidden, down, place[0] * keep_ref.shape[1])


def call(kernel, operands, out_shape, scratch_shapes=(), flops=0, unplaced=0):
    in_vmem = pl.BlockSpec(memory_space=pltpu.VMEM)
    place, *arrays = operands
    split = len(arrays) - unplaced
    return pl.pallas_call(
        kernel,
        in_specs=[pl.BlockSpec(memory_space=pltpu.SMEM)]
        + [in_vmem] * split
        + [pl.BlockSpec(memory_space=pl.ANY)] * unplaced,
        out_specs=[in_vmem] * len(out_shape),
        out_shape=out_shape,
        scratch_shapes=list(scratch_shapes),
        compiler_params=pltpu.CompilerParams(vmem_limit_bytes=VMEM_LIMIT),
        cost_estimate=pl.CostEstimate(flops=flops, bytes_accessed=0, transcendentals=0),
    )(
        place,
        *(pltpu.with_memory_space_constraint(x, pltpu.VMEM) for x in arrays[:split]),
        *arrays[split:],
    )


def gated_sums(place, top_count, own, other, up, down, *mark):
    count, part = other.shape
    out = pltpu.VMEM((count, part), jnp.bfloat16)
    return call(
        lambda *refs: sums_kernel(top_count, *refs),
        [place, own, other, up, down, *mark],
        [out, out],
        [
            pltpu.VMEM((up.shape[0], count, up.shape[2]), jnp.float32),
            pltpu.VMEM((count, down.shape[0]), jnp.bfloat16),
        ],
        flops=2 * count * (up.size + down.size),
        unplaced=len(mark),
    )


def gated_sums_in_steps(place, top_count, own, other, up, down):
    count, part = other.shape
    acc_shape = (up.shape[0], count, up.shape[2])
    (held,) = call(
        own_kernel,
        [place, own, up],
        [pltpu.VMEM(acc_shape, jnp.float32)],
        flops=count * up.size,
    )
    give, hidden = call(
        lambda *refs: give_kernel(top_count, *refs),
        [place, own, other, held, up, down],
        [
            pltpu.VMEM((count, part), jnp.bfloat16),
            pltpu.VMEM((count, down.shape[0]), jnp.bfloat16),
        ],
        [pltpu.VMEM(acc_shape, jnp.float32)],
        flops=count * (up.size + down.size),
    )
    (keep,) = call(
        keep_kernel,
        [place, hidden, down],
        [pltpu.VMEM((count, part), jnp.bfloat16)],
        flops=count * down.size,
    )
    return keep, give


def first_kernel(place, *refs):
    sources, (keep_ref, give_ref, tokens, ids, gates, turned, sems) = refs[:3], refs[3:]
    copies = [
        pltpu.make_async_copy(source, target, sems.at[number])
        for number, (source, target) in enumerate(zip(sources, (tokens, ids, gates)))
    ]
    for copy in copies:
        copy.start()
    for copy in copies:
        copy.wait()
    core = place[0]
    part = tokens.shape[1] // 2
    top_count, rows = ids.shape
    turned[...] = jnp.zeros_like(turned)
    left = gates[...]
    parts = [ids[...].astype(jnp.float32)]
    for _ in range(3):
        parts.append(left.astype(jnp.bfloat16).astype(jnp.float32))
        left = left - parts[-1]
    for number, values in enumerate(parts):
        turned[number * top_count : (number + 1) * top_count, :rows] = values
    routing = turned[...].T[:rows].astype(jnp.bfloat16)
    for half, out in ((core, keep_ref), (1 - core, give_ref)):
        out[:, :part] = tokens[:, pl.ds(pl.multiple_of(half * part, LANES), part)]
        out[:, part:] = routing


def first_halves(place, tokens, expert_ids, gate_probs):
    rows, width = tokens.shape
    sources = [tokens, expert_ids.T, gate_probs.T]
    return pl.pallas_call(
        first_kernel,
        in_specs=[pl.BlockSpec(memory_space=pltpu.SMEM)]
        + [pl.BlockSpec(memory_space=pl.ANY)] * 3,
        out_specs=[pl.BlockSpec(memory_space=pltpu.VMEM)] * 2,
        out_shape=[pltpu.VMEM((rows, width // 2 + LANES), jnp.bfloat16)] * 2,
        scratch_shapes=[pltpu.VMEM(x.shape, x.dtype) for x in sources]
        + [pltpu.VMEM((LANES, LANES), jnp.float32), pltpu.SemaphoreType.DMA((3,))],
        compiler_params=pltpu.CompilerParams(vmem_limit_bytes=VMEM_LIMIT),
    )(place, *(pltpu.with_memory_space_constraint(x, pltpu.HBM) for x in sources))


def added_kernel(kept_ref, taken_ref, total_ref):
    total = kept_ref[...].astype(jnp.float32) + taken_ref[...].astype(jnp.float32)
    total_ref[...] = total.astype(jnp.bfloat16)


def added(kept, taken):
    in_vmem = pl.BlockSpec(memory_space=pltpu.VMEM)
    return pl.pallas_call(
        added_kernel,
        in_specs=[in_vmem] * 2,
        out_specs=in_vmem,
        out_shape=pltpu.VMEM(kept.shape, jnp.bfloat16),
        compiler_params=pltpu.CompilerParams(vmem_limit_bytes=VMEM_LIMIT),
    )(*(pltpu.with_memory_space_constraint(x, pltpu.VMEM) for x in (kept, taken)))


def load_kernel(layout, swap_slot, *refs):
    owners, per_device, top_count, step, scale = layout
    *metas, _, load_ref = refs
    experts_all = owners * per_device
    high, low = [], []
    for meta in metas:
        values = meta[...].astype(jnp.float32)
        lanes = lax.broadcasted_iota(jnp.int32, values.shape, 1)
        gates = sum(pltpu.roll(values, LANES - k * top_count, 1) for k in (1, 2, 3))
        amounts = jnp.round(gates * step)
        upper = jnp.floor(amounts * (1.0 / PART))
        lower = amounts - upper * PART
        ids = jnp.where(lanes < top_count, values, -1.0)
        high.append([])
        low.append([])
        for e in range(experts_all):
            chosen = ids == e
            high[-1].append(jnp.sum(jnp.where(chosen, upper, 0.0), 0, keepdims=True))
            low[-1].append(jnp.sum(jnp.where(chosen, lower, 0.0), 0, keepdims=True))
    sums = []
    for part in (high, low):
        rows = [sum(block[e] for block in part) for e in range(experts_all)]
        sums.append(jnp.sum(jnp.concatenate(rows, 0), 1, keepdims=True))
    totals = (sums[0] * PART + sums[1]) * (1.0 / step)
    expert = lax.broadcasted_iota(jnp.int32, (experts_all, LANES), 0)
    owner = lax.broadcasted_iota(jnp.int32, (experts_all, LANES), 1)
    home = expert // per_device
    slot = jnp.zeros_like(home)
    for h in range(owners):
        slot = jnp.where(home == h, swap_slot[h], slot)
    partner = (home + owners // 2) % owners
    holder = jnp.where(expert % per_device == slot, partner, home)
    load_ref[...] = jnp.sum(jnp.where(holder == owner, totals, 0.0), 0, keepdims=True) * scale


def planned_load(metas, swap_slot, owners, per_device, top_count, after):
    count = sum(meta.shape[0] for meta in metas)
    step = 2.0 ** (31 - (count * GATE_MOST).bit_length())
    layout = (owners, per_device, top_count, step, owners / count)
    in_vmem = pl.BlockSpec(memory_space=pltpu.VMEM)
    load = pl.pallas_call(
        lambda *refs: load_kernel(layout, *refs),
        in_specs=[pl.BlockSpec(memory_space=pltpu.SMEM)]
        + [in_vmem] * len(metas)
        + [pl.BlockSpec(memory_space=pl.ANY)],
        out_specs=in_vmem,
        out_shape=jax.ShapeDtypeStruct((1, LANES), jnp.float32),
        compiler_params=pltpu.CompilerParams(vmem_limit_bytes=VMEM_LIMIT),
        cost_estimate=pl.CostEstimate(
            flops=0, bytes_accessed=sum(meta.nbytes for meta in metas), transcendentals=0
        ),
    )(swap_slot, *metas, after)
    return load


def on_device(tokens, expert_ids, gate_probs, in_weight, out_weight, swap_slot):
    groups, chips = lax.axis_size("dp"), lax.axis_size("chip")
    owners = 2 * chips
    per_device = in_weight.shape[0]
    rows, width = tokens.shape
    part = width // 2
    top_count = expert_ids.shape[1]
    half_width = out_weight.shape[1]
    core = lax.axis_index("core")
    first = core == 0
    first_expert = (lax.axis_index("chip") * 2 + core) * per_device
    place = jnp.stack([core, first_expert]).astype(jnp.int32)

    keep, give = first_halves(place, tokens, expert_ids, gate_probs)
    taken = swap(give, "core", 1)
    chip_rows = row_major(
        jnp.concatenate([jnp.where(first, keep, taken), jnp.where(first, taken, keep)], 0)
    )

    def sums_of(own, weights, *mark):
        other = swap(own[:, :part], "core", 1)
        return gated_sums(place, top_count, own, other, *weights, *mark)

    def chip_sums(keep, give):
        return (wide(keep) + wide(swap(give, "core", 1))).astype(jnp.bfloat16)

    chip_blocks = [swap(chip_rows, "chip", j) for j in range(chips - 1, 0, -1)]
    chip_blocks = [chip_rows, *chip_blocks[::-1]]
    direct = [swap(chip_rows, "dp", k) for k in range(1, groups)]
    *weights, mark = loaded(
        in_weight, out_weight.reshape(per_device * half_width, width), direct[0]
    )
    chip_blocks[1:], mark = lax.optimization_barrier((chip_blocks[1:], mark))
    far = row_major(jnp.concatenate(chip_blocks[1:], 0))
    held = row_major(jnp.concatenate([*chip_blocks, *direct], 0))
    near = spread_near(far)
    if groups == 4:
        fourth_rows = [swap(direct[2], "chip", j) for j in range(chips - 1, 0, -1)]
        fourth_rows = jnp.concatenate(fourth_rows[::-1], 0)
    pieces = [held]
    if held.shape[0] > MOST_ROWS:
        pieces = [row_major(jnp.concatenate(chip_blocks, 0)), *direct]
    keep, give = sums_of(pieces[0], weights, mark)
    later = [sums_of(piece, weights) for piece in pieces[1:]]
    if later:
        keep, give = (jnp.concatenate(x, 0) for x in zip((keep, give), *later))
    first_sum = chip_sums(keep, give)
    near = behind(near, give)
    border = chips * 2 * rows
    near_sums = [first_sum[: 2 * rows]]
    near_sums += [
        first_sum[low : low + 2 * rows] for low in range(border, first_sum.shape[0], 2 * rows)
    ]
    far_sums = [first_sum[2 * rows : border]]

    def parts(block):
        return [block[low : low + 2 * rows] for low in range(0, block.shape[0], 2 * rows)]

    def along_chips(blocks):
        return [swap(blocks[j - 1], "chip", j) for j in range(chips - 1, 0, -1)]

    if groups == 4:
        rest = row_major(jnp.concatenate([*near, fourth_rows], 0))
        other = swap(rest[:, :part], "core", 1)
        keep, give = gated_sums_in_steps(place, top_count, rest, other, *weights)
        pair = added(keep, swap(give, "core", 1))
        far_sums += [*jnp.split(pair, 3)]
        whole = [jnp.concatenate(blocks, 0) for blocks in zip(near_sums, far_sums[:3])]
        fourth = parts(far_sums[3])
        fourth = along_chips(fourth)
        metas = [held, rest]
    else:
        far_sums += [chip_sums(*sums_of(block, weights)) for block in near]
        whole = [jnp.concatenate(pair, 0) for pair in zip(near_sums, far_sums)]
        fourth = []
        metas = [held, *near]
    metas = [block[:, block.shape[1] - LANES :] for block in metas]
    total = parts(collected(whole[0], received(whole)))
    came = along_chips(total[1:])
    if fourth:
        fourth = collected(near_sums[3], behind(fourth, came[-1]))
        came.append(swap(fourth, "dp", 3))
    load = planned_load(metas, swap_slot, owners, per_device, top_count, total[0])
    total = collected(total[0], came)
    upper, lower = total[:rows], total[rows:]
    arrived = swap(jnp.where(first, lower, upper), "core", 1)
    kept = jnp.where(first, upper, lower)
    mixed_out = row_major(
        jnp.concatenate([jnp.where(first, kept, arrived), jnp.where(first, arrived, kept)], 1)
    )

    return (mixed_out, load[0, :owners])


def solution(mesh):
    groups, owners = mesh.devices.shape
    fine = Mesh(mesh.devices.reshape(groups, owners // 2, 2), ("dp", "chip", "core"))
    rows = P(("dp", "chip", "core"), None)
    return jax.shard_map(
        on_device,
        mesh=fine,
        in_specs=(
            rows,
            rows,
            rows,
            P(("chip", "core"), None, "dp"),
            P(("chip", "core"), "dp", None),
            P(),
        ),
        out_specs=(rows, P()),
        check_vma=False,
    )
```

```python
import jax
import jax.numpy as jnp
from jax import lax
from jax.experimental import pallas as pl
from jax.experimental.pallas import tpu as pltpu
from jax.experimental.layout import Layout, with_layout_constraint
from jax.sharding import Mesh, PartitionSpec as P

LANES = 128
DOWN_PARTS = 4
PART = 1024.0
CHUNK = 1024
MOST_ROWS = 512
VMEM_LIMIT = 12 * 2**20
GATE_MOST = 5


def row_major(value):
    return with_layout_constraint(value, Layout(major_to_minor=tuple(range(value.ndim))))


def swap(value, axis, distance):
    size = lax.axis_size(axis)
    pairs = [(i, i ^ distance) for i in range(size)]
    return row_major(lax.ppermute(row_major(value), axis, pairs))


def spread_near(block):
    size = lax.axis_size("dp")
    return [swap(block, "dp", k) for k in range(1, 3 if size == 4 else size)]


def behind(values, others):
    return lax.optimization_barrier((values, others))[0]


def wide(value):
    return value.astype(jnp.float32)


def received(blocks):
    return [swap(block, "dp", k) for k, block in enumerate(blocks[1:], 1)]


def collected(own, others):
    return sum([wide(block) for block in others], wide(own)).astype(jnp.bfloat16)


def load_weight_kernel(weight_ref, _, weight_out, mark_ref, sem):
    copies = piecewise(weight_ref.at, weight_out.at, sem, [(e, k) for e in range(weight_ref.shape[0]) for k in range(0, weight_ref.shape[1], CHUNK)])
    mark_ref[...] = jnp.zeros_like(mark_ref)
    for copy in copies:
        copy.wait()


def piecewise(source, target, sems, places):
    copies = [
        pltpu.make_async_copy(source[e, pl.ds(k, CHUNK)], target[e, pl.ds(k, CHUNK)], sems.at[n])
        for n, (e, k) in enumerate(places)
    ]
    for copy in copies:
        copy.start()
    return copies


def loaded(weight, after):
    return pl.pallas_call(
        load_weight_kernel,
        in_specs=[pl.BlockSpec(memory_space=pl.ANY)] * 2,
        out_specs=[pl.BlockSpec(memory_space=pltpu.VMEM)] * 2,
        out_shape=[
            pltpu.VMEM(weight.shape, weight.dtype),
            pltpu.VMEM((8, LANES), jnp.float32),
        ],
        scratch_shapes=[
            pltpu.SemaphoreType.DMA((weight.shape[0] * weight.shape[1] // CHUNK,))
        ],
        compiler_params=pltpu.CompilerParams(vmem_limit_bytes=VMEM_LIMIT),
        cost_estimate=pl.CostEstimate(flops=0, bytes_accessed=weight.nbytes, transcendentals=0),
    )(pltpu.with_memory_space_constraint(weight, pltpu.HBM), after)


def joined(blocks):
    return blocks[0] if len(blocks) == 1 else jnp.concatenate(blocks, 0)


def add_up(acc, segments, widths, up, base):
    for blocks, width in zip(segments, widths):
        for low in range(0, width, CHUNK):
            held = joined([block[:, low : low + CHUNK] for block in blocks])
            rows = pl.ds(pl.multiple_of(base, CHUNK), CHUNK)
            for s in range(up.shape[0]):
                acc[s] += jnp.dot(held, up[s, rows], preferred_element_type=jnp.float32)
            base = base + CHUNK


def make_hidden(hidden, acc, routed, width, first_expert, top_count):
    meta = joined([block[:, width:].astype(jnp.float32) for block in routed])
    gates = sum(pltpu.roll(meta, LANES - k * top_count, 1) for k in (1, 2, 3))
    lanes = lax.broadcasted_iota(jnp.int32, meta.shape, 1)
    half_width = acc.shape[2] // 2
    for s in range(acc.shape[0]):
        chosen = (meta.astype(jnp.int32) == first_expert + s) & (lanes < top_count)
        own_gate = jnp.sum(jnp.where(chosen, gates, 0.0), 1, keepdims=True)
        gate_half, up_half = acc[s, :, :half_width], acc[s, :, half_width:]
        unit = gate_half * (1.0 / (1.0 + jnp.exp(-gate_half))) * up_half
        hidden[:, s * half_width : (s + 1) * half_width] = (unit * own_gate).astype(jnp.bfloat16)


def multiply_down(out, hidden, down, base):
    for low in range(0, out.shape[1], CHUNK):
        columns = pl.ds(pl.multiple_of(base + low, CHUNK), CHUNK)
        out[:, low : low + CHUNK] = jnp.dot(
            hidden[...], down[:, columns], preferred_element_type=jnp.float32
        ).astype(jnp.bfloat16)


def sums_kernel(top_count, filling, place, own, other, up, *refs):
    if filling:
        down_ref, _, keep_ref, give_ref, down, acc, hidden, sem = refs
        step = down.shape[0] // DOWN_PARTS
        copies = [
            pltpu.make_async_copy(
                down_ref.at[pl.ds(n * step, step)], down.at[pl.ds(n * step, step)], sem.at[n]
            )
            for n in range(DOWN_PARTS)
        ]
        for copy in copies:
            copy.start()
    else:
        down, keep_ref, give_ref, acc, hidden = refs
    part = other.shape[1]
    bases = [place[0] * part, (1 - place[0]) * part]
    acc[...] = jnp.zeros_like(acc)
    add_up(acc, [[own]], [part], up, bases[0])
    add_up(acc, [[other]], [part], up, bases[1])
    make_hidden(hidden, acc, [own], part, place[1], top_count)
    if filling:
        for copy in copies:
            copy.wait()
    multiply_down(give_ref, hidden, down, bases[1])
    multiply_down(keep_ref, hidden, down, bases[0])


def own_kernel(place, own, up, acc):
    part = up.shape[1] // 2
    acc[...] = jnp.zeros_like(acc)
    add_up(acc, [[own]], [part], up, place[0] * part)


def give_kernel(top_count, place, own, other, held, up, down, give_ref, hidden, acc):
    part = other.shape[1]
    base = (1 - place[0]) * part
    acc[...] = held[...]
    add_up(acc, [[other]], [part], up, base)
    make_hidden(hidden, acc, [own], part, place[1], top_count)
    multiply_down(give_ref, hidden, down, base)


def keep_kernel(place, hidden, down, keep_ref):
    multiply_down(keep_ref, hidden, down, place[0] * keep_ref.shape[1])


def call(kernel, operands, out_shape, scratch_shapes=(), flops=0, unplaced=0):
    in_vmem = pl.BlockSpec(memory_space=pltpu.VMEM)
    place, *arrays = operands
    split = len(arrays) - unplaced
    return pl.pallas_call(
        kernel,
        in_specs=[pl.BlockSpec(memory_space=pltpu.SMEM)]
        + [in_vmem] * split
        + [pl.BlockSpec(memory_space=pl.ANY)] * unplaced,
        out_specs=[in_vmem] * len(out_shape),
        out_shape=out_shape,
        scratch_shapes=list(scratch_shapes),
        compiler_params=pltpu.CompilerParams(vmem_limit_bytes=VMEM_LIMIT),
        cost_estimate=pl.CostEstimate(flops=flops, bytes_accessed=0, transcendentals=0),
    )(
        place,
        *(pltpu.with_memory_space_constraint(x, pltpu.VMEM) for x in arrays[:split]),
        *arrays[split:],
    )


def gated_sums(place, top_count, own, other, up, down, mark=None):
    count, part = other.shape
    filling = mark is not None
    out = pltpu.VMEM((count, part), jnp.bfloat16)
    out_shape = [out, out]
    scratch = [
        pltpu.VMEM((up.shape[0], count, up.shape[2]), jnp.float32),
        pltpu.VMEM((count, down.shape[0]), jnp.bfloat16),
    ]
    operands = [place, own, other, up, down]
    if filling:
        operands[-1:] = [pltpu.with_memory_space_constraint(down, pltpu.HBM), mark]
        out_shape.append(pltpu.VMEM(down.shape, down.dtype))
        scratch.append(pltpu.SemaphoreType.DMA((DOWN_PARTS,)))
    return call(
        lambda *refs: sums_kernel(top_count, filling, *refs),
        operands,
        out_shape,
        scratch,
        flops=2 * count * (up.size + down.size),
        unplaced=2 if filling else 0,
    )


def gated_sums_in_steps(place, top_count, own, other, up, down):
    count, part = other.shape
    acc_shape = (up.shape[0], count, up.shape[2])
    (held,) = call(
        own_kernel,
        [place, own, up],
        [pltpu.VMEM(acc_shape, jnp.float32)],
        flops=count * up.size,
    )
    give, hidden = call(
        lambda *refs: give_kernel(top_count, *refs),
        [place, own, other, held, up, down],
        [
            pltpu.VMEM((count, part), jnp.bfloat16),
            pltpu.VMEM((count, down.shape[0]), jnp.bfloat16),
        ],
        [pltpu.VMEM(acc_shape, jnp.float32)],
        flops=count * (up.size + down.size),
    )
    (keep,) = call(
        keep_kernel,
        [place, hidden, down],
        [pltpu.VMEM((count, part), jnp.bfloat16)],
        flops=count * down.size,
    )
    return keep, give


def first_kernel(place, *refs):
    sources, (keep_ref, give_ref, tokens, ids, gates, turned, sems) = refs[:3], refs[3:]
    copies = [
        pltpu.make_async_copy(source, target, sems.at[number])
        for number, (source, target) in enumerate(zip(sources, (tokens, ids, gates)))
    ]
    for copy in copies:
        copy.start()
    for copy in copies:
        copy.wait()
    core = place[0]
    part = tokens.shape[1] // 2
    top_count, rows = ids.shape
    turned[...] = jnp.zeros_like(turned)
    left = gates[...]
    parts = [ids[...].astype(jnp.float32)]
    for _ in range(3):
        parts.append(left.astype(jnp.bfloat16).astype(jnp.float32))
        left = left - parts[-1]
    for number, values in enumerate(parts):
        turned[number * top_count : (number + 1) * top_count, :rows] = values
    routing = turned[...].T[:rows].astype(jnp.bfloat16)
    for half, out in ((core, keep_ref), (1 - core, give_ref)):
        out[:, :part] = tokens[:, pl.ds(pl.multiple_of(half * part, LANES), part)]
        out[:, part:] = routing


def first_halves(place, tokens, expert_ids, gate_probs):
    rows, width = tokens.shape
    sources = [tokens, expert_ids.T, gate_probs.T]
    return pl.pallas_call(
        first_kernel,
        in_specs=[pl.BlockSpec(memory_space=pltpu.SMEM)]
        + [pl.BlockSpec(memory_space=pl.ANY)] * 3,
        out_specs=[pl.BlockSpec(memory_space=pltpu.VMEM)] * 2,
        out_shape=[pltpu.VMEM((rows, width // 2 + LANES), jnp.bfloat16)] * 2,
        scratch_shapes=[pltpu.VMEM(x.shape, x.dtype) for x in sources]
        + [pltpu.VMEM((LANES, LANES), jnp.float32), pltpu.SemaphoreType.DMA((3,))],
        compiler_params=pltpu.CompilerParams(vmem_limit_bytes=VMEM_LIMIT),
    )(place, *(pltpu.with_memory_space_constraint(x, pltpu.HBM) for x in sources))


def added_kernel(kept_ref, taken_ref, total_ref):
    total = kept_ref[...].astype(jnp.float32) + taken_ref[...].astype(jnp.float32)
    total_ref[...] = total.astype(jnp.bfloat16)


def added(kept, taken):
    in_vmem = pl.BlockSpec(memory_space=pltpu.VMEM)
    return pl.pallas_call(
        added_kernel,
        in_specs=[in_vmem] * 2,
        out_specs=in_vmem,
        out_shape=pltpu.VMEM(kept.shape, jnp.bfloat16),
        compiler_params=pltpu.CompilerParams(vmem_limit_bytes=VMEM_LIMIT),
    )(*(pltpu.with_memory_space_constraint(x, pltpu.VMEM) for x in (kept, taken)))


def load_kernel(layout, swap_slot, *refs):
    owners, per_device, top_count, step, scale = layout
    *metas, _, load_ref = refs
    experts_all = owners * per_device
    high, low = [], []
    for meta in metas:
        values = meta[...].astype(jnp.float32)
        lanes = lax.broadcasted_iota(jnp.int32, values.shape, 1)
        gates = sum(pltpu.roll(values, LANES - k * top_count, 1) for k in (1, 2, 3))
        amounts = jnp.round(gates * step)
        upper = jnp.floor(amounts * (1.0 / PART))
        lower = amounts - upper * PART
        ids = jnp.where(lanes < top_count, values, -1.0)
        high.append([])
        low.append([])
        for e in range(experts_all):
            chosen = ids == e
            high[-1].append(jnp.sum(jnp.where(chosen, upper, 0.0), 0, keepdims=True))
            low[-1].append(jnp.sum(jnp.where(chosen, lower, 0.0), 0, keepdims=True))
    sums = []
    for part in (high, low):
        rows = [sum(block[e] for block in part) for e in range(experts_all)]
        sums.append(jnp.sum(jnp.concatenate(rows, 0), 1, keepdims=True))
    totals = (sums[0] * PART + sums[1]) * (1.0 / step)
    expert = lax.broadcasted_iota(jnp.int32, (experts_all, LANES), 0)
    owner = lax.broadcasted_iota(jnp.int32, (experts_all, LANES), 1)
    home = expert // per_device
    slot = jnp.zeros_like(home)
    for h in range(owners):
        slot = jnp.where(home == h, swap_slot[h], slot)
    partner = (home + owners // 2) % owners
    holder = jnp.where(expert % per_device == slot, partner, home)
    load_ref[...] = jnp.sum(jnp.where(holder == owner, totals, 0.0), 0, keepdims=True) * scale


def planned_load(metas, swap_slot, owners, per_device, top_count, after):
    count = sum(meta.shape[0] for meta in metas)
    step = 2.0 ** (31 - (count * GATE_MOST).bit_length())
    layout = (owners, per_device, top_count, step, owners / count)
    in_vmem = pl.BlockSpec(memory_space=pltpu.VMEM)
    load = pl.pallas_call(
        lambda *refs: load_kernel(layout, *refs),
        in_specs=[pl.BlockSpec(memory_space=pltpu.SMEM)]
        + [in_vmem] * len(metas)
        + [pl.BlockSpec(memory_space=pl.ANY)],
        out_specs=in_vmem,
        out_shape=jax.ShapeDtypeStruct((1, LANES), jnp.float32),
        compiler_params=pltpu.CompilerParams(vmem_limit_bytes=VMEM_LIMIT),
        cost_estimate=pl.CostEstimate(
            flops=0, bytes_accessed=sum(meta.nbytes for meta in metas), transcendentals=0
        ),
    )(swap_slot, *metas, after)
    return load


def on_device(tokens, expert_ids, gate_probs, in_weight, out_weight, swap_slot):
    groups, chips = lax.axis_size("dp"), lax.axis_size("chip")
    owners = 2 * chips
    per_device = in_weight.shape[0]
    rows, width = tokens.shape
    part = width // 2
    top_count = expert_ids.shape[1]
    half_width = out_weight.shape[1]
    core = lax.axis_index("core")
    first = core == 0
    first_expert = (lax.axis_index("chip") * 2 + core) * per_device
    place = jnp.stack([core, first_expert]).astype(jnp.int32)

    keep, give = first_halves(place, tokens, expert_ids, gate_probs)
    taken = swap(give, "core", 1)
    chip_rows = row_major(
        jnp.concatenate([jnp.where(first, keep, taken), jnp.where(first, taken, keep)], 0)
    )

    def sums_of(own, weights, *mark):
        other = swap(own[:, :part], "core", 1)
        return gated_sums(place, top_count, own, other, *weights, *mark)

    def chip_sums(keep, give):
        return (wide(keep) + wide(swap(give, "core", 1))).astype(jnp.bfloat16)

    chip_blocks = [swap(chip_rows, "chip", j) for j in range(chips - 1, 0, -1)]
    chip_blocks = [chip_rows, *chip_blocks[::-1]]
    direct = [swap(chip_rows, "dp", k) for k in range(1, groups)]
    up, mark = loaded(in_weight, direct[0])
    chip_blocks[1:], mark = lax.optimization_barrier((chip_blocks[1:], mark))
    far = row_major(jnp.concatenate(chip_blocks[1:], 0))
    held = row_major(jnp.concatenate([*chip_blocks, *direct], 0))
    near = spread_near(far)
    if groups == 4:
        fourth_rows = [swap(direct[2], "chip", j) for j in range(chips - 1, 0, -1)]
        fourth_rows = jnp.concatenate(fourth_rows[::-1], 0)
    weights = [up, out_weight.reshape(per_device * half_width, width)]
    pieces = [held]
    if held.shape[0] > MOST_ROWS:
        pieces = [row_major(jnp.concatenate(chip_blocks, 0)), *direct]
    keep, give, weights[1] = sums_of(pieces[0], weights, mark)
    later = [sums_of(piece, weights) for piece in pieces[1:]]
    if later:
        keep, give = (jnp.concatenate(x, 0) for x in zip((keep, give), *later))
    first_sum = chip_sums(keep, give)
    near = behind(near, give)
    border = chips * 2 * rows
    near_sums = [first_sum[: 2 * rows]]
    near_sums += [
        first_sum[low : low + 2 * rows] for low in range(border, first_sum.shape[0], 2 * rows)
    ]
    far_sums = [first_sum[2 * rows : border]]

    def parts(block):
        return [block[low : low + 2 * rows] for low in range(0, block.shape[0], 2 * rows)]

    def along_chips(blocks):
        return [swap(blocks[j - 1], "chip", j) for j in range(chips - 1, 0, -1)]

    if groups == 4:
        rest = row_major(jnp.concatenate([*near, fourth_rows], 0))
        other = swap(rest[:, :part], "core", 1)
        keep, give = gated_sums_in_steps(place, top_count, rest, other, *weights)
        pair = added(keep, swap(give, "core", 1))
        far_sums += [*jnp.split(pair, 3)]
        whole = [jnp.concatenate(blocks, 0) for blocks in zip(near_sums, far_sums[:3])]
        fourth = parts(far_sums[3])
        fourth = along_chips(fourth)
        metas = [held, rest]
    else:
        far_sums += [chip_sums(*sums_of(block, weights)) for block in near]
        whole = [jnp.concatenate(pair, 0) for pair in zip(near_sums, far_sums)]
        fourth = []
        metas = [held, *near]
    metas = [block[:, block.shape[1] - LANES :] for block in metas]
    total = parts(collected(whole[0], received(whole)))
    came = along_chips(total[1:])
    if fourth:
        fourth = collected(near_sums[3], behind(fourth, came[-1]))
        came.append(swap(fourth, "dp", 3))
    load = planned_load(metas, swap_slot, owners, per_device, top_count, total[0])
    total = collected(total[0], came)
    upper, lower = total[:rows], total[rows:]
    arrived = swap(jnp.where(first, lower, upper), "core", 1)
    kept = jnp.where(first, upper, lower)
    mixed_out = row_major(
        jnp.concatenate([jnp.where(first, kept, arrived), jnp.where(first, arrived, kept)], 1)
    )

    return (mixed_out, load[0, :owners])


def solution(mesh):
    groups, owners = mesh.devices.shape
    fine = Mesh(mesh.devices.reshape(groups, owners // 2, 2), ("dp", "chip", "core"))
    rows = P(("dp", "chip", "core"), None)
    return jax.shard_map(
        on_device,
        mesh=fine,
        in_specs=(
            rows,
            rows,
            rows,
            P(("chip", "core"), None, "dp"),
            P(("chip", "core"), "dp", None),
            P(),
        ),
        out_specs=(rows, P()),
        check_vma=False,
    )
```
